128 devices in a mesh: enc: 4 (over x), seq: 32 (over y, z, core).
Axes of the slice: x: 4, y: 4, z: 4, core: 2. Of those that a mesh axis runs over, the one named last changes fastest.
Arguments:
- queries: bfloat16 [28672, 4096], P('seq', 'enc'), may hold values from -180 to 180
- d_attended: bfloat16 [28672, 4096], P('seq', 'enc'), may hold values from -5 to 5
- encodings: bfloat16 [64, 128, 4096], P('seq'), may hold values from -6 to 6
- w_key: bfloat16 [4096, 4096], P(None, 'enc'), may hold values from -0.09375 to 0.09375
- w_value: bfloat16 [4096, 4096], P(None, 'enc'), may hold values from -0.09375 to 0.09375
- neighbour_owner: int32 [448, 2], P('seq'), may hold values from 0 to 31, all different within a row; in each aligned block of 14 rows (0 to 13, 14 to 27, ...) at most 2 rows name the same one
- neighbour_slot: int32 [448, 2], P('seq'), may hold values from 0 to 1
Outputs:
- attended: bfloat16 [28672, 4096], P('seq', 'enc')
- d_queries: bfloat16 [28672, 4096], P('seq', 'enc')
- d_encodings: bfloat16 [64, 128, 4096], P('seq', None, 'enc')
The draws below stay inside these ranges and needn't reach their ends.
Inputs may be any that keep to these rules, and one draw needn't show every extreme that they name: `neighbour_owner`: the two owners of a span differ. Among the 14 spans of one device (aligned blocks of rows), no owner is named more than 2 times, and in some block one owner is named exactly 2 times.
All inputs are finite; a program needn't handle non-finite values.
Results may differ from the reference program's by a relative error of at most 0.013.
The reference program's roundings to bfloat16 on the way count: a program that leaves them out, or rounds other values in their place, can miss the bound.
Values may be sent and summed in bfloat16 or wider, within the bound.
A program may use at most 256 MiB of HBM per device.

```python
import math
import jax
import jax.numpy as jnp
import numpy as np
from jax import lax

D = 4096
H = 32
HD = 128
SPAN = 64
NBR_LEN = 128
CH_DEV = 14
NEIGH_DEV = 2
CAP = 2
SPANS = 448
TOKENS = 28672
NEIGHBOURS = 64
N_SEQ = 32


def draw_queries(key, part):
    key = jax.random.fold_in(key, 17)
    drawn = jax.random.normal(jax.random.fold_in(key, 1), (TOKENS, D), jnp.float32)
    return jnp.clip(drawn, -180.0, 180.0).astype(jnp.bfloat16)


def plant(array, stream_key, low, largest):
    spot = [jax.random.randint(jax.random.fold_in(stream_key, axis), (), 0, length) for axis, length in enumerate(array.shape)]
    longest = array.shape.index(max(array.shape))
    neighbour = spot[:longest] + [(spot[longest] + 1) % array.shape[longest]] + spot[longest + 1:]
    return array.at[tuple(spot)].set(low).at[tuple(neighbour)].set(largest)


def steps_of(key, extent, cuts, least, largest):
    factor_of, own = 1.0, jax.random.fold_in(key, 6)
    for axis_at, blocks in cuts:
        draws = jnp.exp(jax.random.uniform(jax.random.fold_in(own, axis_at), (blocks,), jnp.float32, least / len(cuts), largest / len(cuts)))
        factor_of = factor_of * jnp.repeat(draws, extent[axis_at] // blocks).reshape([-1 if axis == axis_at else 1 for axis in range(len(extent))])
    return factor_of


def assign_block(key, own, number, rows, count, top, reach, lean):
    ranking = jax.random.permutation(key, count)
    packed, ordinary = shares(count, rows * top, reach, lean, True), shares(count, rows * top, reach, lean, False)
    places = jnp.arange(count)

    def named(lengths, rotation):
        used = int((lengths > 0).sum())
        fixed = max(1, used // 4)
        shifted = fixed + (places - fixed + rotation * (used - fixed)) % max(1, count - fixed)
        return jnp.zeros((count,), jnp.int32).at[ranking[jnp.where(places < fixed, places, shifted)]].set(jnp.asarray(lengths, jnp.int32))

    lengths = jnp.where(number % 4 == 0, named(packed, number // 4), named(ordinary, number - number // 4 - 1))
    mixed = jax.random.permutation(jax.random.fold_in(own, 3), count)
    source_of, sink = mixed[0:count // 2 * 2:2], mixed[1:count // 2 * 2:2]
    room = jnp.minimum(lengths[source_of] - 1, reach - lengths[sink]) // 2
    room = jnp.where((source_of == ranking[0]) | (sink == ranking[0]) | (lengths[sink] == 0), 0, jnp.maximum(room, 0))
    shifted = jax.random.randint(jax.random.fold_in(own, 4), (count // 2,), 0, 1 << 20) % (room + 1)
    lengths = lengths.at[source_of].add(-shifted).at[sink].add(shifted)
    members = jnp.searchsorted(jnp.cumsum(lengths), jnp.arange(rows * top), side="right").astype(jnp.int32)
    listing = members.reshape(top, rows).T
    listing = listing[jax.random.permutation(jax.random.fold_in(own, 1), rows)]
    rotation = jax.random.randint(jax.random.fold_in(own, 2), (rows, 1), 0, top)
    return jnp.take_along_axis(listing, (jnp.arange(top)[None, :] + rotation) % top, axis=1)


def shares(amount, total, reach, slope, full):
    portions = [(1 << 20) // math.isqrt(standing ** slope) + 1 for standing in range(1, amount + 1)]
    largest = reach if full else min(reach, max(-(-total // amount), total * portions[0] // sum(portions)))
    least = 1 if total - largest >= amount - 1 else 0
    holding, rest = [largest] + [least] * (amount - 1), total - largest - least * (amount - 1)
    while rest > 0:
        free = [i for i in range(1, amount) if holding[i] < largest] or [i for i in range(1, amount) if holding[i] < reach]
        whole, budget = sum([portions[i] for i in free]), rest
        for i in free:
            extra = min(reach - holding[i], max(1, budget * portions[i] // whole), rest)
            holding[i] = holding[i] + extra
            rest = rest - extra
    return np.array(holding)


def gaussian(own_key, shape, spread, reach, pieces=(), held_as=jnp.bfloat16):
    loudness = steps_of(own_key, shape, pieces, -0.22, 0.18) if pieces else 1.0
    result = jax.random.normal(own_key, shape, jnp.float32) * spread * loudness
    return jnp.minimum(jnp.maximum(result, -reach), reach).astype(held_as)


def setup_inputs(seed: int = 0) -> dict:
    seeds = jax.random.split(jax.random.key(seed), 8)
    queries = draw_queries(jax.random.fold_in(seeds[7], 71), 0)
    d_attended = gaussian(seeds[1], (TOKENS, D), 1.0, 5.0, ((0, 32), (1, 4)))
    encodings = gaussian(seeds[2], (NEIGHBOURS, NBR_LEN, D), 1.0, 6.0, ((0, 32),))
    w_key = gaussian(seeds[3], (D, D), D ** -0.5, 0.09375, ((1, 4),))
    w_value = gaussian(seeds[4], (D, D), D ** -0.5, 0.09375, ((1, 4),))
    neighbour_owner_keys = jax.random.split(jax.random.fold_in(seeds[5], 1), SPANS // CH_DEV)
    neighbour_owner_turns = jax.random.permutation(jax.random.fold_in(seeds[5], 3), SPANS // CH_DEV)
    neighbour_owner = jax.vmap(lambda own, number: assign_block(jax.random.fold_in(seeds[5], 2), own, number, CH_DEV, N_SEQ, 2, CAP, 2))(neighbour_owner_keys, neighbour_owner_turns).reshape((SPANS, 2))
    neighbour_slot = plant(jax.random.randint(seeds[6], (SPANS, 2), 0, NEIGH_DEV), jax.random.fold_in(seeds[6], 1), 0, NEIGH_DEV - 1).astype(jnp.int32)
    return dict(queries=queries, d_attended=d_attended, encodings=encodings, w_key=w_key, w_value=w_value, neighbour_owner=neighbour_owner, neighbour_slot=neighbour_slot)


def reference(queries, d_attended, encodings, w_key, w_value, neighbour_owner, neighbour_slot):
    score_scale = 1.0 / math.sqrt(HD)
    margin = SPAN - 1
    enc_flat = encodings.reshape(NEIGHBOURS * NBR_LEN, D)
    key_table = jnp.dot(enc_flat, w_key, preferred_element_type=jnp.float32).astype(jnp.bfloat16).reshape(NEIGHBOURS, NBR_LEN, H, HD)
    value_table = jnp.dot(enc_flat, w_value, preferred_element_type=jnp.float32).astype(jnp.bfloat16).reshape(NEIGHBOURS, NBR_LEN, H, HD)
    neighbour_ids = (neighbour_owner * NEIGH_DEV + neighbour_slot).astype(jnp.int32)
    filler = jnp.zeros((margin, D), jnp.bfloat16)
    query_rows = jnp.concatenate([queries[margin:], filler], axis=0).reshape(SPANS, SPAN, H, HD)
    grad_rows = jnp.concatenate([d_attended[margin:], filler], axis=0).reshape(SPANS, SPAN, H, HD)

    def span_step(grad_accum, inputs):
        query_span, grad_span, span_ids = inputs
        key_pair = key_table[span_ids].astype(jnp.float32)
        value_pair = value_table[span_ids].astype(jnp.float32)
        query_wide = query_span.astype(jnp.float32)
        grad_wide = grad_span.astype(jnp.float32)
        scores = jnp.einsum('thd,jrhd->jhtr', query_wide, key_pair) * score_scale
        part_lse = jax.nn.logsumexp(scores, axis=-1)
        prob_round = jnp.exp(scores - part_lse[..., None]).astype(jnp.bfloat16)
        part_out = jnp.einsum('jhtr,jrhd->jthd', prob_round.astype(jnp.float32), value_pair).astype(jnp.bfloat16)
        lse_total = jnp.logaddexp(part_lse[0], part_lse[1])
        share_rows = jnp.exp(part_lse - lse_total[None])
        merged = jnp.einsum('jht,jthd->thd', share_rows, part_out.astype(jnp.float32))
        delta_rows = lax.optimization_barrier(jnp.sum(grad_wide * merged, axis=-1)).T
        full_prob = jnp.exp(scores - lse_total[None, :, :, None])
        full_round = full_prob.astype(jnp.bfloat16)
        prob_grad = jnp.einsum('thd,jrhd->jhtr', grad_wide, value_pair)
        score_grad = (full_prob * (prob_grad - delta_rows[None, :, :, None]) * score_scale).astype(jnp.bfloat16)
        query_part = jnp.einsum('jhtr,jrhd->jthd', score_grad.astype(jnp.float32), key_pair).astype(jnp.bfloat16)
        query_grad = (query_part[0].astype(jnp.float32) + query_part[1].astype(jnp.float32)).astype(jnp.bfloat16)
        key_step = jnp.einsum('jhtr,thd->jrhd', score_grad.astype(jnp.float32), query_wide)
        value_step = jnp.einsum('jhtr,thd->jrhd', full_round.astype(jnp.float32), grad_wide)
        key_accum, value_accum = grad_accum
        key_accum = key_accum.at[span_ids].add(key_step)
        value_accum = value_accum.at[span_ids].add(value_step)
        return ((key_accum, value_accum), (merged.astype(jnp.bfloat16), query_grad))
    empty_grad = jnp.zeros((NEIGHBOURS, NBR_LEN, H, HD), jnp.float32)
    sums, outputs = lax.scan(span_step, (empty_grad, empty_grad), (query_rows, grad_rows, neighbour_ids))
    key_accum, value_accum = sums
    merged_all, query_all = outputs
    attended = jnp.concatenate([filler, merged_all.reshape(TOKENS, D)[:TOKENS - margin]], axis=0)
    d_queries = jnp.concatenate([filler, query_all.reshape(TOKENS, D)[:TOKENS - margin]], axis=0)
    key_grad = key_accum.astype(jnp.bfloat16).reshape(NEIGHBOURS * NBR_LEN, D)
    value_grad = value_accum.astype(jnp.bfloat16).reshape(NEIGHBOURS * NBR_LEN, D)
    enc_grad = jnp.dot(key_grad, w_key.T, preferred_element_type=jnp.float32) + jnp.dot(value_grad, w_value.T, preferred_element_type=jnp.float32)
    d_encodings = enc_grad.astype(jnp.bfloat16).reshape(NEIGHBOURS, NBR_LEN, D)
    return (attended, d_queries, d_encodings)
```

```python
import math

import jax
import jax.numpy as jnp
from jax import lax
from jax.experimental import pallas as pl
from jax.experimental.pallas import tpu as pltpu
from jax.sharding import PartitionSpec as P

HD = 128
SPAN = 64
NBR_LEN = 128
MESH = pl.DeviceIdType.MESH
SCALE = 1.0 / math.sqrt(HD)
RING = 4
MIB = 1024 * 1024


def place():
    s = lax.axis_index("seq")
    return lax.div(s, 8), lax.rem(lax.div(s, 2), RING), lax.rem(s, 2)


def up(i):
    return lax.rem(i + 1, RING)


def down(i):
    return lax.rem(i + RING - 1, RING)


def across(i):
    return lax.rem(i + 2, RING)


def index_of(y, z, c):
    return y * 8 + z * 2 + c


def greet(y, z, c):
    barrier = pltpu.get_barrier_semaphore()
    for other in (
        index_of(up(y), z, c),
        index_of(down(y), z, c),
        index_of(y, up(z), c),
        index_of(y, down(z), c),
        index_of(y, z, 1 - c),
    ):
        pl.semaphore_signal(barrier, inc=1, device_id={"seq": other}, device_id_type=MESH)
    pl.semaphore_wait(barrier, 5)


def gather_kernel(own, tab, send_sem, recv_sem, own_sem):
    y, z, c = place()
    greet(y, z, c)
    pairs = own.shape[0] // 2

    def head_ops(h, parity):
        f, g = (y, z) if parity == 0 else (z, y)

        def dev(a, b):
            return index_of(a, b, c) if parity == 0 else index_of(b, a, c)

        def block(a, *half):
            return tab.at[(h, a, g, c) + half] if parity == 0 else tab.at[(h, g, a, c) + half]

        def band(b, *half):
            if parity == 0:
                return tab.at[(h, slice(None), b, c) + half]
            return tab.at[(h, b, slice(None), c) + half]

        def remote(kind, src, dst, to):
            return pltpu.make_async_remote_copy(
                src_ref=src,
                dst_ref=dst,
                send_sem=send_sem.at[h, kind],
                recv_sem=recv_sem.at[h, kind],
                device_id={"seq": to},
                device_id_type=MESH,
            )

        sibling = index_of(y, z, 1 - c)
        mine = pltpu.make_async_copy(own.at[h], block(f), own_sem.at[h])
        moves = [
            remote(0, own.at[h], block(f), dev(up(f), g)),
            remote(1, own.at[h], block(f), dev(down(f), g)),
            remote(2, block(down(f), 0), block(down(f), 0), dev(up(f), g)),
            remote(3, block(up(f), 1), block(up(f), 1), dev(down(f), g)),
            remote(4, band(g), band(g), dev(f, up(g))),
            remote(5, band(g), band(g), dev(f, down(g))),
            remote(6, band(down(g), slice(0, 1)), band(down(g), slice(0, 1)), dev(f, up(g))),
            remote(7, band(up(g), slice(1, 2)), band(up(g), slice(1, 2)), dev(f, down(g))),
            remote(8, band(g), band(g), sibling),
            remote(9, band(down(g)), band(down(g)), sibling),
            remote(10, band(up(g)), band(up(g)), sibling),
            remote(11, band(across(g)), band(across(g)), sibling),
        ]
        return mine, moves

    def stage0(mine, moves):
        mine.start()
        moves[0].start()
        moves[1].start()

    def stage1(mine, moves):
        moves[0].wait_recv()
        moves[2].start()
        moves[1].wait_recv()
        moves[3].start()

    def stage2(mine, moves):
        mine.wait()
        moves[2].wait_recv()
        moves[3].wait_recv()
        moves[4].start()
        moves[5].start()
        moves[8].start()

    def stage3(mine, moves):
        moves[4].wait_recv()
        moves[6].start()
        moves[9].start()
        moves[5].wait_recv()
        moves[7].start()
        moves[10].start()

    def stage4(mine, moves):
        moves[6].wait_recv()
        moves[7].wait_recv()
        moves[11].start()

    def stage5(mine, moves):
        for kind in (8, 9, 10, 11):
            moves[kind].wait_recv()
        for move in moves:
            move.wait_send()

    stages = (stage0, stage1, stage2, stage3, stage4, stage5)

    def step(i, carry):
        for lag, stage in enumerate(stages):

            @pl.when((i >= lag) & (i < pairs + lag))
            def _(lag=lag, stage=stage):
                for parity in (0, 1):
                    stage(*head_ops(2 * (i - lag) + parity, parity))

        return carry

    lax.fori_loop(0, pairs + len(stages) - 1, step, 0)


def gather_tables(own):
    heads = own.shape[0]
    return pl.pallas_call(
        gather_kernel,
        out_shape=jax.ShapeDtypeStruct((heads, RING, RING, 2) + own.shape[1:], own.dtype),
        in_specs=[pl.BlockSpec(memory_space=pl.ANY)],
        out_specs=pl.BlockSpec(memory_space=pl.ANY),
        scratch_shapes=[
            pltpu.SemaphoreType.DMA((heads, 12)),
            pltpu.SemaphoreType.DMA((heads, 12)),
            pltpu.SemaphoreType.DMA((heads,)),
        ],
        compiler_params=pltpu.CompilerParams(collective_id=0, has_side_effects=True),
        name="gather_tables",
    )(own)


def dot_t(a, b):
    return lax.dot_general(a, b, (((1,), (1,)), ((), ())), preferred_element_type=jnp.float32)


def t_dot(a, b):
    return lax.dot_general(a, b, (((0,), (0,)), ((), ())), preferred_element_type=jnp.float32)


def span_math(q, g, keys, values):
    exps, tops, sums, outs = [], [], [], []
    for k, v in zip(keys, values):
        s = dot_t(q, k) * SCALE
        top = jnp.max(s, axis=1, keepdims=True)
        e = jnp.exp(s - top)
        total = jnp.sum(e, axis=1, keepdims=True)
        p = (e * (1.0 / total)).astype(jnp.bfloat16)
        out = jnp.dot(p, v, preferred_element_type=jnp.float32)
        exps.append(e)
        tops.append(top)
        sums.append(total)
        outs.append(out.astype(jnp.bfloat16).astype(jnp.float32))
    top = jnp.maximum(tops[0], tops[1])
    lifts = [jnp.exp(t - top) for t in tops]
    inverse = 1.0 / (sums[0] * lifts[0] + sums[1] * lifts[1])
    shares = [sums[j] * lifts[j] * inverse for j in (0, 1)]
    merged = shares[0] * outs[0] + shares[1] * outs[1]
    delta = jnp.sum(g.astype(jnp.float32) * merged, axis=1, keepdims=True)
    d_query, d_keys, d_values = 0.0, [], []
    for j in (0, 1):
        full = exps[j] * (lifts[j] * inverse)
        grad = dot_t(g, values[j])
        ds = (full * (grad - delta) * SCALE).astype(jnp.bfloat16)
        part = jnp.dot(ds, keys[j], preferred_element_type=jnp.float32)
        d_query = d_query + part.astype(jnp.bfloat16).astype(jnp.float32)
        d_keys.append(t_dot(ds, q))
        d_values.append(t_dot(full.astype(jnp.bfloat16), g))
    return merged, d_query, d_keys, d_values


def attend_kernel(ids, first, second, q_ref, g_ref, tab, att_ref, dq_ref, con, ck, cv):
    spans = q_ref.shape[0] // SPAN
    reads = 2 * spans
    ck[reads] = jnp.zeros(ck.shape[1:], jnp.float32)
    cv[reads] = jnp.zeros(cv.shape[1:], jnp.float32)

    def one(c, carry):
        rows = pl.ds(pl.multiple_of(c * SPAN, SPAN), SPAN)
        q, g = q_ref[rows, :], g_ref[rows, :]
        picks = [ids[2 * c + j] for j in (0, 1)]
        spots = [(lax.div(n, 2), lax.rem(n, 2)) for n in picks]
        keys = [tab[0, o, 0, s] for o, s in spots]
        values = [tab[0, o, 1, s] for o, s in spots]
        merged, d_query, d_keys, d_values = span_math(q, g, keys, values)
        att_ref[rows, :] = merged.astype(jnp.bfloat16)
        dq_ref[rows, :] = d_query.astype(jnp.bfloat16)
        for j in (0, 1):
            ck[2 * c + j] = d_keys[j]
            cv[2 * c + j] = d_values[j]
        return carry

    lax.fori_loop(0, spans, one, 0, unroll=2)

    def fold(o, carry):
        for s in (0, 1):
            a, b = first[2 * o + s], second[2 * o + s]
            con[0, o, 0, s] = (ck[a] + ck[b]).astype(jnp.bfloat16)
            con[0, o, 1, s] = (cv[a] + cv[b]).astype(jnp.bfloat16)
        return carry

    lax.fori_loop(0, tab.shape[1], fold, 0)


def attend(ids, first, second, query_shift, grad_shift, tables):
    rows, width = query_shift.shape
    heads, owners = tables.shape[0], tables.shape[1]
    reads = ids.shape[0]
    row_spec = pl.BlockSpec((rows, HD), lambda h, *_: (0, h))
    tab_spec = pl.BlockSpec((1,) + tables.shape[1:], lambda h, *_: (h, 0, 0, 0, 0, 0))
    return pl.pallas_call(
        attend_kernel,
        grid_spec=pltpu.PrefetchScalarGridSpec(
            num_scalar_prefetch=3,
            grid=(heads,),
            in_specs=[row_spec, row_spec, tab_spec],
            out_specs=[row_spec, row_spec, tab_spec],
            scratch_shapes=[
                pltpu.VMEM((reads + 1, NBR_LEN, HD), jnp.float32),
                pltpu.VMEM((reads + 1, NBR_LEN, HD), jnp.float32),
            ],
        ),
        out_shape=[
            jax.ShapeDtypeStruct((rows, width), jnp.bfloat16),
            jax.ShapeDtypeStruct((rows, width), jnp.bfloat16),
            jax.ShapeDtypeStruct(tables.shape, jnp.bfloat16),
        ],
        compiler_params=pltpu.CompilerParams(vmem_limit_bytes=48 * MIB),
        name="attend",
    )(ids, first, second, query_shift, grad_shift, tables)


def wide(value):
    return value.astype(jnp.float32)


def scatter_kernel(con, out, acc, sib, r1, r2, r3, r4, send_sem, recv_sem, own_sem):
    y, z, c = place()
    greet(y, z, c)
    pairs = out.shape[0] // 2

    def head_ops(h, parity):
        f, g = (y, z) if parity == 0 else (z, y)

        def dev(a, b):
            return index_of(a, b, c) if parity == 0 else index_of(b, a, c)

        def spot(a, b):
            return (h, a, b) if parity == 0 else (h, b, a)

        def remote(kind, src, dst, to):
            return pltpu.make_async_remote_copy(
                src_ref=src,
                dst_ref=dst,
                send_sem=send_sem.at[h, kind],
                recv_sem=recv_sem.at[h, kind],
                device_id={"seq": to},
                device_id_type=MESH,
            )

        every = slice(None)
        mine = pltpu.make_async_copy(con.at[h, :, :, c], acc.at[h], own_sem.at[h])
        moves = [
            remote(0, con.at[h, :, :, 1 - c], sib.at[h], index_of(y, z, 1 - c)),
            remote(1, acc.at[spot(every, across(g)) + (0,)], r1.at[h, 0], dev(f, up(g))),
            remote(2, acc.at[spot(every, across(g)) + (1,)], r1.at[h, 1], dev(f, down(g))),
            remote(3, acc.at[spot(every, up(g))], r2.at[h, 0], dev(f, up(g))),
            remote(4, acc.at[spot(every, down(g))], r2.at[h, 1], dev(f, down(g))),
            remote(5, acc.at[spot(across(f), g) + (0,)], r3.at[h, 0], dev(up(f), g)),
            remote(6, acc.at[spot(across(f), g) + (1,)], r3.at[h, 1], dev(down(f), g)),
            remote(7, acc.at[spot(up(f), g)], r4.at[h, 0], dev(up(f), g)),
            remote(8, acc.at[spot(down(f), g)], r4.at[h, 1], dev(down(f), g)),
        ]
        return h, spot, f, g, mine, moves

    def stage0(h, spot, f, g, mine, moves):
        mine.start()
        moves[0].start()

    def stage1(h, spot, f, g, mine, moves):
        mine.wait()
        moves[0].wait_recv()

        def add(i, carry):
            a, b = lax.div(i, RING), lax.rem(i, RING)
            for kv in (0, 1):
                acc[h, a, b, kv] = acc[h, a, b, kv] + sib[h, a, b, kv]
            return carry

        lax.fori_loop(0, RING * RING, add, 0)
        moves[1].start()
        moves[2].start()

    def stage2(h, spot, f, g, mine, moves):
        for half, (move, toward) in enumerate(((1, up(g)), (2, down(g)))):
            moves[move].wait_recv()

            def add(a, carry):
                at = spot(a, toward) + (half,)
                acc[at] = acc[at] + r1[h, half, a]
                return carry

            lax.fori_loop(0, RING, add, 0)
            moves[3 + half].start()

    def stage3(h, spot, f, g, mine, moves):
        moves[3].wait_recv()
        moves[4].wait_recv()

        def add(a, carry):
            for kv in (0, 1):
                at = spot(a, g) + (kv,)
                total = wide(acc[at]) + wide(r2[h, 0, a, kv]) + wide(r2[h, 1, a, kv])
                acc[at] = total.astype(jnp.bfloat16)
            return carry

        lax.fori_loop(0, RING, add, 0)
        moves[5].start()
        moves[6].start()

    def stage4(h, spot, f, g, mine, moves):
        for half, (move, toward) in enumerate(((5, up(f)), (6, down(f)))):
            moves[move].wait_recv()
            at = spot(toward, g) + (half,)
            acc[at] = acc[at] + r3[h, half]
            moves[7 + half].start()

    def stage5(h, spot, f, g, mine, moves):
        moves[7].wait_recv()
        moves[8].wait_recv()
        for kv in (0, 1):
            total = wide(acc[spot(f, g) + (kv,)]) + wide(r4[h, 0, kv]) + wide(r4[h, 1, kv])
            out[h, kv] = total.astype(jnp.bfloat16)
        for move in moves:
            move.wait_send()

    stages = (stage0, stage1, stage2, stage3, stage4, stage5)

    def step(i, carry):
        for lag, stage in enumerate(stages):

            @pl.when((i >= lag) & (i < pairs + lag))
            def _(lag=lag, stage=stage):
                for parity in (0, 1):
                    stage(*head_ops(2 * (i - lag) + parity, parity))

        return carry

    lax.fori_loop(0, pairs + len(stages) - 1, step, 0)


def scatter_tables(con):
    heads = con.shape[0]
    tail = con.shape[5:]
    return pl.pallas_call(
        scatter_kernel,
        out_shape=jax.ShapeDtypeStruct((heads, 2) + tail, con.dtype),
        in_specs=[pl.BlockSpec(memory_space=pl.ANY)],
        out_specs=pl.BlockSpec(memory_space=pltpu.VMEM),
        scratch_shapes=[
            pltpu.VMEM((heads, RING, RING, 2) + tail, con.dtype),
            pltpu.VMEM((heads, RING, RING, 2) + tail, con.dtype),
            pltpu.VMEM((heads, 2, RING) + tail, con.dtype),
            pltpu.VMEM((heads, 2, RING, 2) + tail, con.dtype),
            pltpu.VMEM((heads, 2) + tail, con.dtype),
            pltpu.VMEM((heads, 2, 2) + tail, con.dtype),
            pltpu.SemaphoreType.DMA((heads, 9)),
            pltpu.SemaphoreType.DMA((heads, 9)),
            pltpu.SemaphoreType.DMA((heads,)),
        ],
        compiler_params=pltpu.CompilerParams(
            collective_id=1, has_side_effects=True, vmem_limit_bytes=56 * MIB
        ),
        name="scatter_tables",
    )(con)


def enc_kernel(part, out, s1, s2, r1, r2, send_sem, recv_sem):
    x = lax.axis_index("enc")
    right, left = up(x), down(x)
    barrier = pltpu.get_barrier_semaphore()
    for other in (right, left):
        pl.semaphore_signal(barrier, inc=1, device_id={"enc": other}, device_id_type=MESH)
    pl.semaphore_wait(barrier, 2)
    rows = part.shape[0]
    half = rows // 2
    width = out.shape[1]

    def cols(t):
        return pl.ds(pl.multiple_of(t * width, width), width)

    def remote(kind, src, dst, to):
        return pltpu.make_async_remote_copy(
            src_ref=src,
            dst_ref=dst,
            send_sem=send_sem.at[kind],
            recv_sem=recv_sem.at[kind],
            device_id={"enc": to},
            device_id_type=MESH,
        )

    moves = [
        remote(0, s1.at[0], r1.at[0], right),
        remote(1, s1.at[1], r1.at[1], left),
        remote(2, s2.at[0], r2.at[0], right),
        remote(3, s2.at[1], r2.at[1], left),
    ]
    far = cols(across(x))
    s1[0] = part[:half, far].astype(jnp.bfloat16)
    moves[0].start()
    s1[1] = part[half:, far].astype(jnp.bfloat16)
    moves[1].start()
    s2[0, half:] = part[half:, cols(right)].astype(jnp.bfloat16)
    s2[1, :half] = part[:half, cols(left)].astype(jnp.bfloat16)
    moves[0].wait_recv()
    s2[0, :half] = (part[:half, cols(right)] + wide(r1[0])).astype(jnp.bfloat16)
    moves[2].start()
    moves[1].wait_recv()
    s2[1, half:] = (part[half:, cols(left)] + wide(r1[1])).astype(jnp.bfloat16)
    moves[3].start()
    moves[2].wait_recv()
    moves[3].wait_recv()
    out[...] = (part[:, cols(x)] + wide(r2[0]) + wide(r2[1])).astype(jnp.bfloat16)
    for move in moves:
        move.wait_send()


def scatter_enc(part):
    rows, width = part.shape[0], part.shape[1] // RING
    half = rows // 2
    return pl.pallas_call(
        enc_kernel,
        out_shape=jax.ShapeDtypeStruct((rows, width), jnp.bfloat16),
        in_specs=[pl.BlockSpec(memory_space=pltpu.VMEM)],
        out_specs=pl.BlockSpec(memory_space=pltpu.VMEM),
        scratch_shapes=[
            pltpu.VMEM((2, half, width), jnp.bfloat16),
            pltpu.VMEM((2, rows, width), jnp.bfloat16),
            pltpu.VMEM((2, half, width), jnp.bfloat16),
            pltpu.VMEM((2, rows, width), jnp.bfloat16),
            pltpu.SemaphoreType.DMA((4,)),
            pltpu.SemaphoreType.DMA((4,)),
        ],
        compiler_params=pltpu.CompilerParams(
            collective_id=2, has_side_effects=True, vmem_limit_bytes=32 * MIB
        ),
        name="scatter_enc",
    )(part)


def shifted(value, axis, steps):
    count = lax.axis_size(axis)
    first, last = (max(0, -steps), min(count, count - steps))
    return lax.ppermute(value, axis, [(source, source + steps) for source in range(first, last)])


def per_device(queries, d_attended, encodings, w_key, w_value, neighbour_owner, neighbour_slot):
    tok_rows, feat_width = queries.shape
    heads = feat_width // HD
    margin = SPAN - 1
    owned = encodings.shape[0]
    owners = lax.axis_size("seq")
    reads = 2 * (tok_rows // SPAN)

    ids = (neighbour_owner * owned + neighbour_slot).reshape(reads).astype(jnp.int32)
    hit = ids[None, :] == jnp.arange(owners * owned, dtype=jnp.int32)[:, None]
    order = jnp.arange(reads, dtype=jnp.int32)[None, :]
    first = jnp.min(jnp.where(hit, order, reads), axis=1)
    last = jnp.max(jnp.where(hit, order, -1), axis=1)
    second = jnp.where(last > first, last, reads)

    rim_rows = shifted(jnp.stack([queries[:margin], d_attended[:margin]]), "seq", -1)
    query_shift = jnp.concatenate([queries[margin:], rim_rows[0]], axis=0)
    grad_shift = jnp.concatenate([d_attended[margin:], rim_rows[1]], axis=0)

    enc_flat = encodings.reshape(owned * NBR_LEN, encodings.shape[2])
    tables = [
        jnp.dot(enc_flat, w, preferred_element_type=jnp.float32)
        .astype(jnp.bfloat16)
        .reshape(owned * NBR_LEN, heads, HD)
        .transpose(1, 0, 2)
        for w in (w_key, w_value)
    ]
    table = gather_tables(jnp.stack(tables, axis=1))
    table = table.reshape(heads, owners, 2, owned, NBR_LEN, HD)
    attended_shift, dq_shift, con = attend(ids, first, second, query_shift, grad_shift, table)
    attended_tail = shifted(attended_shift[tok_rows - margin :], "seq", 1)
    query_tail = shifted(dq_shift[tok_rows - margin :], "seq", 1)
    con = con.reshape(heads, RING, RING, 2, 2, owned * NBR_LEN, HD)
    grads = scatter_tables(con)
    contract = (((1,), (1,)), ((), ()))
    part = 0.0
    for kv, w in enumerate((w_key, w_value)):
        rows = grads[:, kv].transpose(1, 0, 2).reshape(owned * NBR_LEN, feat_width)
        part = part + lax.dot_general(rows, w, contract, preferred_element_type=jnp.float32)
    d_encodings = scatter_enc(part).reshape(owned, NBR_LEN, feat_width)
    attended = jnp.concatenate([attended_tail, attended_shift[: tok_rows - margin]], axis=0)
    d_queries = jnp.concatenate([query_tail, dq_shift[: tok_rows - margin]], axis=0)
    return (attended, d_queries, d_encodings)


def solution(mesh):
    return jax.shard_map(
        per_device,
        mesh=mesh,
        in_specs=(
            P("seq", "enc"),
            P("seq", "enc"),
            P("seq", None, None),
            P(None, "enc"),
            P(None, "enc"),
            P("seq", None),
            P("seq", None),
        ),
        out_specs=(P("seq", "enc"), P("seq", "enc"), P("seq", None, "enc")),
        check_vma=False,
    )
```

```python
import math

import jax
import jax.numpy as jnp
from jax import lax
from jax.experimental import pallas as pl
from jax.experimental.pallas import tpu as pltpu
from jax.sharding import PartitionSpec as P

HD = 128
SPAN = 64
NBR_LEN = 128
MESH = pl.DeviceIdType.MESH
SCALE = 1.0 / math.sqrt(HD)
RING = 4
MIB = 1024 * 1024


def place():
    s = lax.axis_index("seq")
    return lax.div(s, 8), lax.rem(lax.div(s, 2), RING), lax.rem(s, 2)


def up(i):
    return lax.rem(i + 1, RING)


def down(i):
    return lax.rem(i + RING - 1, RING)


def across(i):
    return lax.rem(i + 2, RING)


def index_of(y, z, c):
    return y * 8 + z * 2 + c


def greet(y, z, c):
    barrier = pltpu.get_barrier_semaphore()
    for other in (
        index_of(up(y), z, c),
        index_of(down(y), z, c),
        index_of(y, up(z), c),
        index_of(y, down(z), c),
        index_of(y, z, 1 - c),
    ):
        pl.semaphore_signal(barrier, inc=1, device_id={"seq": other}, device_id_type=MESH)
    pl.semaphore_wait(barrier, 5)


def gather_kernel(own, tab, send_sem, recv_sem, own_sem):
    y, z, c = place()
    greet(y, z, c)
    pairs = own.shape[0] // 2

    def head_ops(h, parity):
        f, g = (y, z) if parity == 0 else (z, y)

        def dev(a, b):
            return index_of(a, b, c) if parity == 0 else index_of(b, a, c)

        def block(a, *half):
            return tab.at[(h, a, g, c) + half] if parity == 0 else tab.at[(h, g, a, c) + half]

        def band(b, *half):
            if parity == 0:
                return tab.at[(h, slice(None), b, c) + half]
            return tab.at[(h, b, slice(None), c) + half]

        def remote(kind, src, dst, to):
            return pltpu.make_async_remote_copy(
                src_ref=src,
                dst_ref=dst,
                send_sem=send_sem.at[h, kind],
                recv_sem=recv_sem.at[h, kind],
                device_id={"seq": to},
                device_id_type=MESH,
            )

        sibling = index_of(y, z, 1 - c)
        mine = pltpu.make_async_copy(own.at[h], block(f), own_sem.at[h])
        moves = [
            remote(0, own.at[h], block(f), dev(up(f), g)),
            remote(1, own.at[h], block(f), dev(down(f), g)),
            remote(2, block(down(f), 0), block(down(f), 0), dev(up(f), g)),
            remote(3, block(up(f), 1), block(up(f), 1), dev(down(f), g)),
            remote(4, band(g), band(g), dev(f, up(g))),
            remote(5, band(g), band(g), dev(f, down(g))),
            remote(6, band(down(g), slice(0, 1)), band(down(g), slice(0, 1)), dev(f, up(g))),
            remote(7, band(up(g), slice(1, 2)), band(up(g), slice(1, 2)), dev(f, down(g))),
            remote(8, band(g), band(g), sibling),
            remote(9, band(down(g)), band(down(g)), sibling),
            remote(10, band(up(g)), band(up(g)), sibling),
            remote(11, band(across(g)), band(across(g)), sibling),
        ]
        return mine, moves

    def stage0(mine, moves):
        mine.start()
        moves[0].start()
        moves[1].start()

    def stage1(mine, moves):
        moves[0].wait_recv()
        moves[2].start()
        moves[1].wait_recv()
        moves[3].start()

    def stage2(mine, moves):
        mine.wait()
        moves[2].wait_recv()
        moves[3].wait_recv()
        moves[4].start()
        moves[5].start()
        moves[8].start()

    def stage3(mine, moves):
        moves[4].wait_recv()
        moves[6].start()
        moves[9].start()
        moves[5].wait_recv()
        moves[7].start()
        moves[10].start()

    def stage4(mine, moves):
        moves[6].wait_recv()
        moves[7].wait_recv()
        moves[11].start()

    def stage5(mine, moves):
        for kind in (8, 9, 10, 11):
            moves[kind].wait_recv()
        for move in moves:
            move.wait_send()

    stages = (stage0, stage1, stage2, stage3, stage4, stage5)

    def step(i, carry):
        for lag, stage in enumerate(stages):

            @pl.when((i >= lag) & (i < pairs + lag))
            def _(lag=lag, stage=stage):
                for parity in (0, 1):
                    stage(*head_ops(2 * (i - lag) + parity, parity))

        return carry

    lax.fori_loop(0, pairs + len(stages) - 1, step, 0)


def gather_tables(own):
    heads = own.shape[0]
    return pl.pallas_call(
        gather_kernel,
        out_shape=jax.ShapeDtypeStruct((heads, RING, RING, 2) + own.shape[1:], own.dtype),
        in_specs=[pl.BlockSpec(memory_space=pl.ANY)],
        out_specs=pl.BlockSpec(memory_space=pl.ANY),
        scratch_shapes=[
            pltpu.SemaphoreType.DMA((heads, 12)),
            pltpu.SemaphoreType.DMA((heads, 12)),
            pltpu.SemaphoreType.DMA((heads,)),
        ],
        compiler_params=pltpu.CompilerParams(collective_id=0, has_side_effects=True),
        name="gather_tables",
    )(own)


def dot_t(a, b):
    return lax.dot_general(a, b, (((1,), (1,)), ((), ())), preferred_element_type=jnp.float32)


def t_dot(a, b):
    return lax.dot_general(a, b, (((0,), (0,)), ((), ())), preferred_element_type=jnp.float32)


def spans_math(qs, gs, keys, values):
    each, both = range(len(qs)), (0, 1)

    def pairs(rows, tables):
        joined = [dot_t(rows[u], jnp.concatenate(tables[u], axis=0)) for u in each]
        return [[x[:, :NBR_LEN], x[:, NBR_LEN:]] for x in joined]

    def narrow(x):
        return x.astype(jnp.bfloat16)

    s = pairs(qs, keys)
    grad = pairs(gs, values)
    top = [[jnp.max(s[u][j], axis=1, keepdims=True) for j in both] for u in each]
    e = [[jnp.exp((s[u][j] - top[u][j]) * SCALE) for j in both] for u in each]
    total = [[jnp.sum(e[u][j], axis=1, keepdims=True) for j in both] for u in each]
    p = [[narrow(e[u][j] * (1.0 / total[u][j])) for j in both] for u in each]
    out = [
        [wide(narrow(jnp.dot(p[u][j], values[u][j], preferred_element_type=jnp.float32))) for j in both]
        for u in each
    ]
    peak = [jnp.maximum(top[u][0], top[u][1]) for u in each]
    lift = [[jnp.exp((top[u][j] - peak[u]) * SCALE) for j in both] for u in each]
    inverse = [1.0 / (total[u][0] * lift[u][0] + total[u][1] * lift[u][1]) for u in each]
    weight = [[lift[u][j] * inverse[u] for j in both] for u in each]
    merged = [
        total[u][0] * weight[u][0] * out[u][0] + total[u][1] * weight[u][1] * out[u][1] for u in each
    ]
    delta = [jnp.sum(wide(gs[u]) * merged[u], axis=1, keepdims=True) for u in each]
    full = [[e[u][j] * weight[u][j] for j in both] for u in each]
    ds = [
        [narrow(full[u][j] * ((grad[u][j] - delta[u]) * SCALE)) for j in both] for u in each
    ]
    parts = [
        [wide(narrow(jnp.dot(ds[u][j], keys[u][j], preferred_element_type=jnp.float32))) for j in both]
        for u in each
    ]
    d_query = [parts[u][0] + parts[u][1] for u in each]
    d_keys = [t_dot(jnp.concatenate(ds[u], axis=1), qs[u]) for u in each]
    d_values = [
        t_dot(jnp.concatenate([narrow(full[u][j]) for j in both], axis=1), gs[u]) for u in each
    ]
    return merged, d_query, d_keys, d_values


def wide(value):
    return value.astype(jnp.float32)


def attend_kernel(ids, first, second, q_ref, g_ref, tab, att_ref, dq_ref, con, ck, cv):
    spans = q_ref.shape[0] // SPAN
    reads = 2 * spans
    group = max(n for n in range(1, 8) if spans % n == 0)
    ck[reads] = jnp.zeros(ck.shape[1:], jnp.float32)
    cv[reads] = jnp.zeros(cv.shape[1:], jnp.float32)

    def some(i, carry):
        spots = [i * group + u for u in range(group)]
        rows = [pl.ds(pl.multiple_of(c * SPAN, SPAN), SPAN) for c in spots]
        qs, gs = [q_ref[r, :] for r in rows], [g_ref[r, :] for r in rows]
        picks = [[ids[2 * c + j] for j in (0, 1)] for c in spots]
        keys = [[tab[0, lax.div(n, 2), 0, lax.rem(n, 2)] for n in two] for two in picks]
        values = [[tab[0, lax.div(n, 2), 1, lax.rem(n, 2)] for n in two] for two in picks]
        merged, d_query, d_keys, d_values = spans_math(qs, gs, keys, values)
        for u, c in enumerate(spots):
            att_ref[rows[u], :] = merged[u].astype(jnp.bfloat16)
            dq_ref[rows[u], :] = d_query[u].astype(jnp.bfloat16)
            for j in (0, 1):
                ck[2 * c + j] = d_keys[u][j * NBR_LEN : (j + 1) * NBR_LEN]
                cv[2 * c + j] = d_values[u][j * NBR_LEN : (j + 1) * NBR_LEN]
        return carry

    lax.fori_loop(0, spans // group, some, 0)

    def fold(o, carry):
        for s in (0, 1):
            a, b = first[2 * o + s], second[2 * o + s]
            con[0, o, 0, s] = (ck[a] + ck[b]).astype(jnp.bfloat16)
            con[0, o, 1, s] = (cv[a] + cv[b]).astype(jnp.bfloat16)
        return carry

    lax.fori_loop(0, tab.shape[1], fold, 0)


def attend(ids, first, second, query_shift, grad_shift, tables):
    rows, width = query_shift.shape
    heads, owners = tables.shape[0], tables.shape[1]
    reads = ids.shape[0]
    row_spec = pl.BlockSpec((rows, HD), lambda h, *_: (0, h))
    tab_spec = pl.BlockSpec((1,) + tables.shape[1:], lambda h, *_: (h, 0, 0, 0, 0, 0))
    return pl.pallas_call(
        attend_kernel,
        grid_spec=pltpu.PrefetchScalarGridSpec(
            num_scalar_prefetch=3,
            grid=(heads,),
            in_specs=[row_spec, row_spec, tab_spec],
            out_specs=[row_spec, row_spec, tab_spec],
            scratch_shapes=[
                pltpu.VMEM((reads + 1, NBR_LEN, HD), jnp.float32),
                pltpu.VMEM((reads + 1, NBR_LEN, HD), jnp.float32),
            ],
        ),
        out_shape=[
            jax.ShapeDtypeStruct((rows, width), jnp.bfloat16),
            jax.ShapeDtypeStruct((rows, width), jnp.bfloat16),
            jax.ShapeDtypeStruct(tables.shape, jnp.bfloat16),
        ],
        compiler_params=pltpu.CompilerParams(vmem_limit_bytes=48 * MIB),
        name="attend",
    )(ids, first, second, query_shift, grad_shift, tables)


def scatter_kernel(con, out, acc, sib, r1, r2, r3, r4, send_sem, recv_sem, own_sem):
    y, z, c = place()
    greet(y, z, c)
    pairs = out.shape[0] // 2

    def head_ops(h, parity):
        f, g = (y, z) if parity == 0 else (z, y)

        def dev(a, b):
            return index_of(a, b, c) if parity == 0 else index_of(b, a, c)

        def spot(a, b):
            return (h, a, b) if parity == 0 else (h, b, a)

        def remote(kind, src, dst, to):
            return pltpu.make_async_remote_copy(
                src_ref=src,
                dst_ref=dst,
                send_sem=send_sem.at[h, kind],
                recv_sem=recv_sem.at[h, kind],
                device_id={"seq": to},
                device_id_type=MESH,
            )

        every = slice(None)
        mine = pltpu.make_async_copy(con.at[h, :, :, c], acc.at[h], own_sem.at[h])
        moves = [
            remote(0, con.at[h, :, :, 1 - c], sib.at[h], index_of(y, z, 1 - c)),
            remote(1, acc.at[spot(every, across(g)) + (0,)], r1.at[h, 0], dev(f, up(g))),
            remote(2, acc.at[spot(every, across(g)) + (1,)], r1.at[h, 1], dev(f, down(g))),
            remote(3, acc.at[spot(every, up(g))], r2.at[h, 0], dev(f, up(g))),
            remote(4, acc.at[spot(every, down(g))], r2.at[h, 1], dev(f, down(g))),
            remote(5, acc.at[spot(across(f), g) + (0,)], r3.at[h, 0], dev(up(f), g)),
            remote(6, acc.at[spot(across(f), g) + (1,)], r3.at[h, 1], dev(down(f), g)),
            remote(7, acc.at[spot(up(f), g)], r4.at[h, 0], dev(up(f), g)),
            remote(8, acc.at[spot(down(f), g)], r4.at[h, 1], dev(down(f), g)),
        ]
        return h, spot, f, g, mine, moves

    def stage0(h, spot, f, g, mine, moves):
        mine.start()
        moves[0].start()

    def stage1(h, spot, f, g, mine, moves):
        mine.wait()
        moves[0].wait_recv()

        def add(i, carry):
            a, b = lax.div(i, RING), lax.rem(i, RING)
            for kv in (0, 1):
                acc[h, a, b, kv] = acc[h, a, b, kv] + sib[h, a, b, kv]
            return carry

        lax.fori_loop(0, RING * RING, add, 0)
        moves[1].start()
        moves[2].start()

    def stage2(h, spot, f, g, mine, moves):
        for half, (move, toward) in enumerate(((1, up(g)), (2, down(g)))):
            moves[move].wait_recv()

            def add(a, carry):
                at = spot(a, toward) + (half,)
                acc[at] = acc[at] + r1[h, half, a]
                return carry

            lax.fori_loop(0, RING, add, 0)
            moves[3 + half].start()

    def stage3(h, spot, f, g, mine, moves):
        moves[3].wait_recv()
        moves[4].wait_recv()

        def add(a, carry):
            for kv in (0, 1):
                at = spot(a, g) + (kv,)
                total = wide(acc[at]) + wide(r2[h, 0, a, kv]) + wide(r2[h, 1, a, kv])
                acc[at] = total.astype(jnp.bfloat16)
            return carry

        lax.fori_loop(0, RING, add, 0)
        moves[5].start()
        moves[6].start()

    def stage4(h, spot, f, g, mine, moves):
        for half, (move, toward) in enumerate(((5, up(f)), (6, down(f)))):
            moves[move].wait_recv()
            at = spot(toward, g) + (half,)
            acc[at] = acc[at] + r3[h, half]
            moves[7 + half].start()

    def stage5(h, spot, f, g, mine, moves):
        moves[7].wait_recv()
        moves[8].wait_recv()
        for kv in (0, 1):
            total = wide(acc[spot(f, g) + (kv,)]) + wide(r4[h, 0, kv]) + wide(r4[h, 1, kv])
            out[h, kv] = total.astype(jnp.bfloat16)
        for move in moves:
            move.wait_send()

    stages = (stage0, stage1, stage2, stage3, stage4, stage5)

    def step(i, carry):
        for lag, stage in enumerate(stages):

            @pl.when((i >= lag) & (i < pairs + lag))
            def _(lag=lag, stage=stage):
                for parity in (0, 1):
                    stage(*head_ops(2 * (i - lag) + parity, parity))

        return carry

    lax.fori_loop(0, pairs + len(stages) - 1, step, 0)


def scatter_tables(con):
    heads = con.shape[0]
    tail = con.shape[5:]
    return pl.pallas_call(
        scatter_kernel,
        out_shape=jax.ShapeDtypeStruct((heads, 2) + tail, con.dtype),
        in_specs=[pl.BlockSpec(memory_space=pl.ANY)],
        out_specs=pl.BlockSpec(memory_space=pltpu.VMEM),
        scratch_shapes=[
            pltpu.VMEM((heads, RING, RING, 2) + tail, con.dtype),
            pltpu.VMEM((heads, RING, RING, 2) + tail, con.dtype),
            pltpu.VMEM((heads, 2, RING) + tail, con.dtype),
            pltpu.VMEM((heads, 2, RING, 2) + tail, con.dtype),
            pltpu.VMEM((heads, 2) + tail, con.dtype),
            pltpu.VMEM((heads, 2, 2) + tail, con.dtype),
            pltpu.SemaphoreType.DMA((heads, 9)),
            pltpu.SemaphoreType.DMA((heads, 9)),
            pltpu.SemaphoreType.DMA((heads,)),
        ],
        compiler_params=pltpu.CompilerParams(
            collective_id=1, has_side_effects=True, vmem_limit_bytes=56 * MIB
        ),
        name="scatter_tables",
    )(con)


def enc_kernel(part, out, s1, s2, r1, r2, send_sem, recv_sem):
    x = lax.axis_index("enc")
    right, left = up(x), down(x)
    barrier = pltpu.get_barrier_semaphore()
    for other in (right, left):
        pl.semaphore_signal(barrier, inc=1, device_id={"enc": other}, device_id_type=MESH)
    pl.semaphore_wait(barrier, 2)
    rows = part.shape[0]
    half = rows // 2
    width = out.shape[1]

    def cols(t):
        return pl.ds(pl.multiple_of(t * width, width), width)

    def remote(kind, src, dst, to):
        return pltpu.make_async_remote_copy(
            src_ref=src,
            dst_ref=dst,
            send_sem=send_sem.at[kind],
            recv_sem=recv_sem.at[kind],
            device_id={"enc": to},
            device_id_type=MESH,
        )

    moves = [
        remote(0, s1.at[0], r1.at[0], right),
        remote(1, s1.at[1], r1.at[1], left),
        remote(2, s2.at[0], r2.at[0], right),
        remote(3, s2.at[1], r2.at[1], left),
    ]
    far = cols(across(x))
    s1[0] = part[:half, far].astype(jnp.bfloat16)
    moves[0].start()
    s1[1] = part[half:, far].astype(jnp.bfloat16)
    moves[1].start()
    s2[0, half:] = part[half:, cols(right)].astype(jnp.bfloat16)
    s2[1, :half] = part[:half, cols(left)].astype(jnp.bfloat16)
    moves[0].wait_recv()
    s2[0, :half] = (part[:half, cols(right)] + wide(r1[0])).astype(jnp.bfloat16)
    moves[2].start()
    moves[1].wait_recv()
    s2[1, half:] = (part[half:, cols(left)] + wide(r1[1])).astype(jnp.bfloat16)
    moves[3].start()
    moves[2].wait_recv()
    moves[3].wait_recv()
    out[...] = (part[:, cols(x)] + wide(r2[0]) + wide(r2[1])).astype(jnp.bfloat16)
    for move in moves:
        move.wait_send()


def scatter_enc(part):
    rows, width = part.shape[0], part.shape[1] // RING
    half = rows // 2
    return pl.pallas_call(
        enc_kernel,
        out_shape=jax.ShapeDtypeStruct((rows, width), jnp.bfloat16),
        in_specs=[pl.BlockSpec(memory_space=pltpu.VMEM)],
        out_specs=pl.BlockSpec(memory_space=pltpu.VMEM),
        scratch_shapes=[
            pltpu.VMEM((2, half, width), jnp.bfloat16),
            pltpu.VMEM((2, rows, width), jnp.bfloat16),
            pltpu.VMEM((2, half, width), jnp.bfloat16),
            pltpu.VMEM((2, rows, width), jnp.bfloat16),
            pltpu.SemaphoreType.DMA((4,)),
            pltpu.SemaphoreType.DMA((4,)),
        ],
        compiler_params=pltpu.CompilerParams(
            collective_id=2, has_side_effects=True, vmem_limit_bytes=32 * MIB
        ),
        name="scatter_enc",
    )(part)


def shifted(value, axis, steps):
    count = lax.axis_size(axis)
    first, last = (max(0, -steps), min(count, count - steps))
    return lax.ppermute(value, axis, [(source, source + steps) for source in range(first, last)])


def per_device(queries, d_attended, encodings, w_key, w_value, neighbour_owner, neighbour_slot):
    tok_rows, feat_width = queries.shape
    heads = feat_width // HD
    margin = SPAN - 1
    owned = encodings.shape[0]
    owners = lax.axis_size("seq")
    reads = 2 * (tok_rows // SPAN)

    ids = (neighbour_owner * owned + neighbour_slot).reshape(reads).astype(jnp.int32)
    hit = ids[None, :] == jnp.arange(owners * owned, dtype=jnp.int32)[:, None]
    order = jnp.arange(reads, dtype=jnp.int32)[None, :]
    first = jnp.min(jnp.where(hit, order, reads), axis=1)
    last = jnp.max(jnp.where(hit, order, -1), axis=1)
    second = jnp.where(last > first, last, reads)

    rim_rows = shifted(jnp.stack([queries[:margin], d_attended[:margin]]), "seq", -1)
    query_shift = jnp.concatenate([queries[margin:], rim_rows[0]], axis=0)
    grad_shift = jnp.concatenate([d_attended[margin:], rim_rows[1]], axis=0)

    enc_flat = encodings.reshape(owned * NBR_LEN, encodings.shape[2])
    tables = [
        jnp.dot(enc_flat, w, preferred_element_type=jnp.float32)
        .astype(jnp.bfloat16)
        .reshape(owned * NBR_LEN, heads, HD)
        .transpose(1, 0, 2)
        for w in (w_key, w_value)
    ]
    table = gather_tables(jnp.stack(tables, axis=1))
    table = table.reshape(heads, owners, 2, owned, NBR_LEN, HD)
    attended_shift, dq_shift, con = attend(ids, first, second, query_shift, grad_shift, table)
    attended_tail = shifted(attended_shift[tok_rows - margin :], "seq", 1)
    query_tail = shifted(dq_shift[tok_rows - margin :], "seq", 1)
    con = con.reshape(heads, RING, RING, 2, 2, owned * NBR_LEN, HD)
    grads = scatter_tables(con)
    contract = (((1,), (1,)), ((), ()))
    part = 0.0
    for kv, w in enumerate((w_key, w_value)):
        rows = grads[:, kv].transpose(1, 0, 2).reshape(owned * NBR_LEN, feat_width)
        part = part + lax.dot_general(rows, w, contract, preferred_element_type=jnp.float32)
    d_encodings = scatter_enc(part).reshape(owned, NBR_LEN, feat_width)
    attended = jnp.concatenate([attended_tail, attended_shift[: tok_rows - margin]], axis=0)
    d_queries = jnp.concatenate([query_tail, dq_shift[: tok_rows - margin]], axis=0)
    return (attended, d_queries, d_encodings)


def solution(mesh):
    return jax.shard_map(
        per_device,
        mesh=mesh,
        in_specs=(
            P("seq", "enc"),
            P("seq", "enc"),
            P("seq", None, None),
            P(None, "enc"),
            P(None, "enc"),
            P("seq", None),
            P("seq", None),
        ),
        out_specs=(P("seq", "enc"), P("seq", "enc"), P("seq", None, "enc")),
        check_vma=False,
    )
```

```python
import math

import jax
import jax.numpy as jnp
from jax import lax
from jax.experimental import pallas as pl
from jax.experimental.pallas import tpu as pltpu
from jax.sharding import PartitionSpec as P

HD = 128
SPAN = 64
NBR_LEN = 128
MESH = pl.DeviceIdType.MESH
SCALE = 1.0 / math.sqrt(HD)
RING = 4
MIB = 1024 * 1024


def place():
    s = lax.axis_index("seq")
    return lax.div(s, 8), lax.rem(lax.div(s, 2), RING), lax.rem(s, 2)


def up(i):
    return lax.rem(i + 1, RING)


def down(i):
    return lax.rem(i + RING - 1, RING)


def across(i):
    return lax.rem(i + 2, RING)


def index_of(y, z, c):
    return y * 8 + z * 2 + c


def greet(y, z, c):
    barrier = pltpu.get_barrier_semaphore()
    for other in (
        index_of(up(y), z, c),
        index_of(down(y), z, c),
        index_of(y, up(z), c),
        index_of(y, down(z), c),
        index_of(y, z, 1 - c),
    ):
        pl.semaphore_signal(barrier, inc=1, device_id={"seq": other}, device_id_type=MESH)
    pl.semaphore_wait(barrier, 5)


def dot_t(a, b):
    return lax.dot_general(a, b, (((1,), (1,)), ((), ())), preferred_element_type=jnp.float32)


def t_dot(a, b):
    return lax.dot_general(a, b, (((0,), (0,)), ((), ())), preferred_element_type=jnp.float32)


def spans_math(qs, gs, keys, values):
    each, both = range(len(qs)), (0, 1)

    def pairs(rows, tables):
        joined = [dot_t(rows[u], jnp.concatenate(tables[u], axis=0)) for u in each]
        return [[x[:, :NBR_LEN], x[:, NBR_LEN:]] for x in joined]

    def narrow(x):
        return x.astype(jnp.bfloat16)

    s = pairs(qs, keys)
    grad = pairs(gs, values)
    top = [[jnp.max(s[u][j], axis=1, keepdims=True) for j in both] for u in each]
    e = [[jnp.exp((s[u][j] - top[u][j]) * SCALE) for j in both] for u in each]
    total = [[jnp.sum(e[u][j], axis=1, keepdims=True) for j in both] for u in each]
    p = [[narrow(e[u][j] * (1.0 / total[u][j])) for j in both] for u in each]
    out = [
        [wide(narrow(jnp.dot(p[u][j], values[u][j], preferred_element_type=jnp.float32))) for j in both]
        for u in each
    ]
    peak = [jnp.maximum(top[u][0], top[u][1]) for u in each]
    lift = [[jnp.exp((top[u][j] - peak[u]) * SCALE) for j in both] for u in each]
    inverse = [1.0 / (total[u][0] * lift[u][0] + total[u][1] * lift[u][1]) for u in each]
    weight = [[lift[u][j] * inverse[u] for j in both] for u in each]
    merged = [
        total[u][0] * weight[u][0] * out[u][0] + total[u][1] * weight[u][1] * out[u][1] for u in each
    ]
    delta = [jnp.sum(wide(gs[u]) * merged[u], axis=1, keepdims=True) for u in each]
    full = [[e[u][j] * weight[u][j] for j in both] for u in each]
    ds = [
        [narrow(full[u][j] * ((grad[u][j] - delta[u]) * SCALE)) for j in both] for u in each
    ]
    parts = [
        [wide(narrow(jnp.dot(ds[u][j], keys[u][j], preferred_element_type=jnp.float32))) for j in both]
        for u in each
    ]
    d_query = [parts[u][0] + parts[u][1] for u in each]
    d_keys = [t_dot(jnp.concatenate(ds[u], axis=1), qs[u]) for u in each]
    d_values = [
        t_dot(jnp.concatenate([narrow(full[u][j]) for j in both], axis=1), gs[u]) for u in each
    ]
    return merged, d_query, d_keys, d_values


def wide(value):
    return value.astype(jnp.float32)


def core_kernel(
    ids, first, second, own, q_ref, g_ref,
    att_ref, dq_ref, out, tab, landed,
    table_even, table_odd, ck, cv, acc, give_even, give_odd, got_even, got_odd,
    r1, r2, r3, r4, send_sem, recv_sem, back_send, back_recv, own_sem, load_sem,
):
    y, z, c = place()
    greet(y, z, c)
    pairs = own.shape[0] // 2
    spans = q_ref.shape[0] // SPAN
    reads = 2 * spans
    group = max(n for n in range(1, 8) if spans % n == 0)
    sibling = index_of(y, z, 1 - c)
    every = slice(None)
    held = (table_even, table_odd)
    give = (give_even, give_odd)
    got = (got_even, got_odd)
    ck[reads] = jnp.zeros(ck.shape[1:], jnp.float32)
    cv[reads] = jnp.zeros(cv.shape[1:], jnp.float32)

    class Head:
        def __init__(self, h, parity):
            self.h, self.parity = h, parity
            self.f, self.g = (y, z) if parity == 0 else (z, y)

        def dev(self, a, b):
            return index_of(a, b, c) if self.parity == 0 else index_of(b, a, c)

        def spot(self, a, b):
            return (self.h, a, b) if self.parity == 0 else (self.h, b, a)

        def block(self, a, *half):
            return tab.at[self.spot(a, self.g) + (c,) + half]

        def band(self, b, *half):
            return tab.at[self.spot(every, b) + (c,) + half]

        def mine(self):
            return pltpu.make_async_copy(own.at[self.h], self.block(self.f), own_sem.at[self.h])

        def load(self):
            return pltpu.make_async_copy(
                tab.at[self.h], held[self.parity], load_sem.at[self.h, 0]
            )

        def fetch(self):
            return pltpu.make_async_copy(
                landed.at[self.h], got[self.parity], load_sem.at[self.h, 1]
            )

        def out_move(self, kind):
            f, g, dev = self.f, self.g, self.dev
            if kind < 4:
                src = (own.at[self.h], own.at[self.h], None, None)[kind]
                dst = (
                    lambda: self.block(f),
                    lambda: self.block(f),
                    lambda: self.block(down(f), 0),
                    lambda: self.block(up(f), 1),
                )[kind]()
                to = dev(up(f), g) if kind % 2 == 0 else dev(down(f), g)
            elif kind < 8:
                dst = (
                    lambda: self.band(g),
                    lambda: self.band(g),
                    lambda: self.band(down(g), slice(0, 1)),
                    lambda: self.band(up(g), slice(1, 2)),
                )[kind - 4]()
                src, to = None, dev(f, up(g)) if kind % 2 == 0 else dev(f, down(g))
            else:
                dst = self.band((g, down(g), up(g), across(g))[kind - 8])
                src, to = None, sibling
            return pltpu.make_async_remote_copy(
                src_ref=dst if src is None else src,
                dst_ref=dst,
                send_sem=send_sem.at[self.h, kind],
                recv_sem=recv_sem.at[self.h, kind],
                device_id={"seq": to},
                device_id_type=MESH,
            )

        def back_move(self, kind):
            f, g, dev, h = self.f, self.g, self.dev, self.h
            src, dst, to = (
                lambda: (give[self.parity], landed.at[h], sibling),
                lambda: (acc.at[self.spot(every, across(g)) + (0,)], r1.at[h, 0], dev(f, up(g))),
                lambda: (acc.at[self.spot(every, across(g)) + (1,)], r1.at[h, 1], dev(f, down(g))),
                lambda: (acc.at[self.spot(every, up(g))], r2.at[h, 0], dev(f, up(g))),
                lambda: (acc.at[self.spot(every, down(g))], r2.at[h, 1], dev(f, down(g))),
                lambda: (acc.at[self.spot(across(f), g) + (0,)], r3.at[h, 0], dev(up(f), g)),
                lambda: (acc.at[self.spot(across(f), g) + (1,)], r3.at[h, 1], dev(down(f), g)),
                lambda: (acc.at[self.spot(up(f), g)], r4.at[h, 0], dev(up(f), g)),
                lambda: (acc.at[self.spot(down(f), g)], r4.at[h, 1], dev(down(f), g)),
            )[kind]()
            return pltpu.make_async_remote_copy(
                src_ref=src,
                dst_ref=dst,
                send_sem=back_send.at[h, kind],
                recv_sem=back_recv.at[h, kind],
                device_id={"seq": to},
                device_id_type=MESH,
            )

    def own_out(t):
        t.mine().start()
        t.out_move(0).start()
        t.out_move(1).start()

    def block_on(t):
        t.out_move(0).wait_recv()
        t.out_move(2).start()
        t.out_move(1).wait_recv()
        t.out_move(3).start()

    def band_out(t):
        t.mine().wait()
        t.out_move(2).wait_recv()
        t.out_move(3).wait_recv()
        t.out_move(4).start()
        t.out_move(5).start()
        t.out_move(8).start()

    def band_on(t):
        t.out_move(4).wait_recv()
        t.out_move(6).start()
        t.out_move(9).start()
        t.out_move(5).wait_recv()
        t.out_move(7).start()
        t.out_move(10).start()

    def band_last(t):
        t.out_move(6).wait_recv()
        t.out_move(7).wait_recv()
        t.out_move(11).start()

    def table_in(t):
        for kind in (8, 9, 10, 11):
            t.out_move(kind).wait_recv()
        t.load().start()
        for kind in range(12):
            t.out_move(kind).wait_send()

    def sibling_in(t):
        t.back_move(0).wait_recv()
        t.fetch().start()
        t.back_move(0).wait_send()

    def attend(t):
        table, cols = held[t.parity], pl.ds(pl.multiple_of(t.h * HD, HD), HD)
        t.load().wait()

        def pick(n, kv):
            return table[lax.div(n, 16), lax.rem(lax.div(n, 4), RING), lax.rem(lax.div(n, 2), 2), kv, lax.rem(n, 2)]

        def some(i, carry):
            spots = [i * group + u for u in range(group)]
            rows = [pl.ds(pl.multiple_of(s * SPAN, SPAN), SPAN) for s in spots]
            qs, gs = [q_ref[r, cols] for r in rows], [g_ref[r, cols] for r in rows]
            picks = [[ids[2 * s + j] for j in (0, 1)] for s in spots]
            keys = [[pick(n, 0) for n in two] for two in picks]
            values = [[pick(n, 1) for n in two] for two in picks]
            merged, d_query, d_keys, d_values = spans_math(qs, gs, keys, values)
            for u, s in enumerate(spots):
                att_ref[rows[u], cols] = merged[u].astype(jnp.bfloat16)
                dq_ref[rows[u], cols] = d_query[u].astype(jnp.bfloat16)
                for j in (0, 1):
                    ck[2 * s + j] = d_keys[u][j * NBR_LEN : (j + 1) * NBR_LEN]
                    cv[2 * s + j] = d_values[u][j * NBR_LEN : (j + 1) * NBR_LEN]
            return carry

        lax.fori_loop(0, spans // group, some, 0)

        def fold(chip, carry):
            a, b = lax.div(chip, RING), lax.rem(chip, RING)
            for s in (0, 1):
                for core, keep in ((c, True), (1 - c, False)):
                    n = (2 * chip + core) * 2 + s
                    one, two = first[n], second[n]
                    for kv, part in ((0, ck), (1, cv)):
                        total = (part[one] + part[two]).astype(jnp.bfloat16)
                        lines = pl.ds(s * NBR_LEN, NBR_LEN)
                        if keep:
                            acc[t.h, a, b, kv, lines] = total
                        else:
                            give[t.parity][a, b, kv, lines] = total
            return carry

        lax.fori_loop(0, RING * RING, fold, 0)
        t.back_move(0).start()

    def sum_sibling(t):
        t.fetch().wait()

        def add(i, carry):
            a, b = lax.div(i, RING), lax.rem(i, RING)
            for kv in (0, 1):
                acc[t.h, a, b, kv] = acc[t.h, a, b, kv] + got[t.parity][a, b, kv]
            return carry

        lax.fori_loop(0, RING * RING, add, 0)
        t.back_move(1).start()
        t.back_move(2).start()

    def sum_band_half(t):
        for half, (kind, toward) in enumerate(((1, up(t.g)), (2, down(t.g)))):
            t.back_move(kind).wait_recv()

            def add(a, carry):
                at = t.spot(a, toward) + (half,)
                acc[at] = acc[at] + r1[t.h, half, a]
                return carry

            lax.fori_loop(0, RING, add, 0)
            t.back_move(3 + half).start()

    def sum_band(t):
        t.back_move(3).wait_recv()
        t.back_move(4).wait_recv()

        def add(a, carry):
            for kv in (0, 1):
                at = t.spot(a, t.g) + (kv,)
                total = wide(acc[at]) + wide(r2[t.h, 0, a, kv]) + wide(r2[t.h, 1, a, kv])
                acc[at] = total.astype(jnp.bfloat16)
            return carry

        lax.fori_loop(0, RING, add, 0)
        t.back_move(5).start()
        t.back_move(6).start()

    def sum_block_half(t):
        for half, (kind, toward) in enumerate(((5, up(t.f)), (6, down(t.f)))):
            t.back_move(kind).wait_recv()
            at = t.spot(toward, t.g) + (half,)
            acc[at] = acc[at] + r3[t.h, half]
            t.back_move(7 + half).start()

    def sum_block(t):
        t.back_move(7).wait_recv()
        t.back_move(8).wait_recv()
        for kv in (0, 1):
            total = wide(acc[t.spot(t.f, t.g) + (kv,)])
            total = total + wide(r4[t.h, 0, kv]) + wide(r4[t.h, 1, kv])
            out[t.h, kv] = total.astype(jnp.bfloat16)
        for kind in range(1, 9):
            t.back_move(kind).wait_send()

    stages = (
        (0, own_out),
        (1, block_on),
        (2, band_out),
        (3, band_on),
        (4, band_last),
        (5, table_in),
        (6, sibling_in),
        (10, sum_block),
        (9, sum_block_half),
        (8, sum_band),
        (7, sum_band_half),
        (5, attend),
        (6, sum_sibling),
    )

    def step(i, carry):
        for lag, stage in stages:

            @pl.when((i >= lag) & (i < pairs + lag))
            def _(lag=lag, stage=stage):
                for parity in (0, 1):
                    stage(Head(2 * (i - lag) + parity, parity))

        return carry

    lax.fori_loop(0, pairs + max(lag for lag, _ in stages), step, 0)


def core(ids, first, second, own, query_shift, grad_shift):
    rows, width = query_shift.shape
    heads, reads = own.shape[0], ids.shape[0]
    rest = own.shape[1:]
    tail = (2, 2 * NBR_LEN, HD)
    bf16, f32 = jnp.bfloat16, jnp.float32
    in_vmem = pl.BlockSpec(memory_space=pltpu.VMEM)
    in_smem = pl.BlockSpec(memory_space=pltpu.SMEM)
    anywhere = pl.BlockSpec(memory_space=pl.ANY)
    band = (RING, RING) + tail
    dma = pltpu.SemaphoreType.DMA
    return pl.pallas_call(
        core_kernel,
        in_specs=[in_smem, in_smem, in_smem, anywhere, in_vmem, in_vmem],
        out_specs=[in_vmem, in_vmem, in_vmem, anywhere, anywhere],
        out_shape=[
            jax.ShapeDtypeStruct((rows, width), bf16),
            jax.ShapeDtypeStruct((rows, width), bf16),
            jax.ShapeDtypeStruct((heads,) + tail, bf16),
            jax.ShapeDtypeStruct((heads, RING, RING, 2) + rest, bf16),
            jax.ShapeDtypeStruct((heads,) + band, bf16),
        ],
        scratch_shapes=[
            pltpu.VMEM((RING, RING, 2) + rest, bf16),
            pltpu.VMEM((RING, RING, 2) + rest, bf16),
            pltpu.VMEM((reads + 1, NBR_LEN, HD), f32),
            pltpu.VMEM((reads + 1, NBR_LEN, HD), f32),
            pltpu.VMEM((heads,) + band, bf16),
            pltpu.VMEM(band, bf16),
            pltpu.VMEM(band, bf16),
            pltpu.VMEM(band, bf16),
            pltpu.VMEM(band, bf16),
            pltpu.VMEM((heads, 2, RING) + tail[1:], bf16),
            pltpu.VMEM((heads, 2, RING) + tail, bf16),
            pltpu.VMEM((heads, 2) + tail[1:], bf16),
            pltpu.VMEM((heads, 2) + tail, bf16),
            dma((heads, 12)),
            dma((heads, 12)),
            dma((heads, 9)),
            dma((heads, 9)),
            dma((heads,)),
            dma((heads, 2)),
        ],
        compiler_params=pltpu.CompilerParams(
            collective_id=0, has_side_effects=True, vmem_limit_bytes=63 * MIB
        ),
        name="core",
    )(ids, first, second, own, query_shift, grad_shift)


def enc_kernel(part, out, s1, s2, r1, r2, send_sem, recv_sem):
    x = lax.axis_index("enc")
    right, left = up(x), down(x)
    barrier = pltpu.get_barrier_semaphore()
    for other in (right, left):
        pl.semaphore_signal(barrier, inc=1, device_id={"enc": other}, device_id_type=MESH)
    pl.semaphore_wait(barrier, 2)
    rows = part.shape[0]
    half = rows // 2
    width = out.shape[1]

    def cols(t):
        return pl.ds(pl.multiple_of(t * width, width), width)

    def remote(kind, src, dst, to):
        return pltpu.make_async_remote_copy(
            src_ref=src,
            dst_ref=dst,
            send_sem=send_sem.at[kind],
            recv_sem=recv_sem.at[kind],
            device_id={"enc": to},
            device_id_type=MESH,
        )

    moves = [
        remote(0, s1.at[0], r1.at[0], right),
        remote(1, s1.at[1], r1.at[1], left),
        remote(2, s2.at[0], r2.at[0], right),
        remote(3, s2.at[1], r2.at[1], left),
    ]
    far = cols(across(x))
    s1[0] = part[:half, far].astype(jnp.bfloat16)
    moves[0].start()
    s1[1] = part[half:, far].astype(jnp.bfloat16)
    moves[1].start()
    s2[0, half:] = part[half:, cols(right)].astype(jnp.bfloat16)
    s2[1, :half] = part[:half, cols(left)].astype(jnp.bfloat16)
    moves[0].wait_recv()
    s2[0, :half] = (part[:half, cols(right)] + wide(r1[0])).astype(jnp.bfloat16)
    moves[2].start()
    moves[1].wait_recv()
    s2[1, half:] = (part[half:, cols(left)] + wide(r1[1])).astype(jnp.bfloat16)
    moves[3].start()
    moves[2].wait_recv()
    moves[3].wait_recv()
    out[...] = (part[:, cols(x)] + wide(r2[0]) + wide(r2[1])).astype(jnp.bfloat16)
    for move in moves:
        move.wait_send()


def scatter_enc(part):
    rows, width = part.shape[0], part.shape[1] // RING
    half = rows // 2
    return pl.pallas_call(
        enc_kernel,
        out_shape=jax.ShapeDtypeStruct((rows, width), jnp.bfloat16),
        in_specs=[pl.BlockSpec(memory_space=pltpu.VMEM)],
        out_specs=pl.BlockSpec(memory_space=pltpu.VMEM),
        scratch_shapes=[
            pltpu.VMEM((2, half, width), jnp.bfloat16),
            pltpu.VMEM((2, rows, width), jnp.bfloat16),
            pltpu.VMEM((2, half, width), jnp.bfloat16),
            pltpu.VMEM((2, rows, width), jnp.bfloat16),
            pltpu.SemaphoreType.DMA((4,)),
            pltpu.SemaphoreType.DMA((4,)),
        ],
        compiler_params=pltpu.CompilerParams(
            collective_id=2, has_side_effects=True, vmem_limit_bytes=32 * MIB
        ),
        name="scatter_enc",
    )(part)


def shifted(value, axis, steps):
    count = lax.axis_size(axis)
    first, last = (max(0, -steps), min(count, count - steps))
    return lax.ppermute(value, axis, [(source, source + steps) for source in range(first, last)])


def per_device(queries, d_attended, encodings, w_key, w_value, neighbour_owner, neighbour_slot):
    tok_rows, feat_width = queries.shape
    heads = feat_width // HD
    margin = SPAN - 1
    owned = encodings.shape[0]
    owners = lax.axis_size("seq")
    reads = 2 * (tok_rows // SPAN)

    ids = (neighbour_owner * owned + neighbour_slot).reshape(reads).astype(jnp.int32)
    hit = ids[None, :] == jnp.arange(owners * owned, dtype=jnp.int32)[:, None]
    order = jnp.arange(reads, dtype=jnp.int32)[None, :]
    first = jnp.min(jnp.where(hit, order, reads), axis=1)
    last = jnp.max(jnp.where(hit, order, -1), axis=1)
    second = jnp.where(last > first, last, reads)

    rim_rows = shifted(jnp.stack([queries[:margin], d_attended[:margin]]), "seq", -1)
    query_shift = jnp.concatenate([queries[margin:], rim_rows[0]], axis=0)
    grad_shift = jnp.concatenate([d_attended[margin:], rim_rows[1]], axis=0)

    enc_flat = encodings.reshape(owned * NBR_LEN, encodings.shape[2])
    tables = [
        jnp.dot(enc_flat, w, preferred_element_type=jnp.float32)
        .astype(jnp.bfloat16)
        .reshape(owned, NBR_LEN, heads, HD)
        .transpose(2, 0, 1, 3)
        for w in (w_key, w_value)
    ]
    attended_shift, dq_shift, grads, _, _ = core(
        ids, first, second, jnp.stack(tables, axis=1), query_shift, grad_shift
    )
    attended_tail = shifted(attended_shift[tok_rows - margin :], "seq", 1)
    query_tail = shifted(dq_shift[tok_rows - margin :], "seq", 1)
    contract = (((1,), (1,)), ((), ()))
    part = 0.0
    for kv, w in enumerate((w_key, w_value)):
        rows = grads[:, kv].transpose(1, 0, 2).reshape(owned * NBR_LEN, feat_width)
        part = part + lax.dot_general(rows, w, contract, preferred_element_type=jnp.float32)
    d_encodings = scatter_enc(part).reshape(owned, NBR_LEN, feat_width)
    attended = jnp.concatenate([attended_tail, attended_shift[: tok_rows - margin]], axis=0)
    d_queries = jnp.concatenate([query_tail, dq_shift[: tok_rows - margin]], axis=0)
    return (attended, d_queries, d_encodings)


def solution(mesh):
    return jax.shard_map(
        per_device,
        mesh=mesh,
        in_specs=(
            P("seq", "enc"),
            P("seq", "enc"),
            P("seq", None, None),
            P(None, "enc"),
            P(None, "enc"),
            P("seq", None),
            P("seq", None),
        ),
        out_specs=(P("seq", "enc"), P("seq", "enc"), P("seq", None, "enc")),
        check_vma=False,
    )
```

```python
import math

import jax
import jax.numpy as jnp
from jax import lax
from jax.experimental import pallas as pl
from jax.experimental.pallas import tpu as pltpu
from jax.sharding import PartitionSpec as P

HD = 128
SPAN = 64
NBR_LEN = 128
MESH = pl.DeviceIdType.MESH
SCALE = 1.0 / math.sqrt(HD)
RING = 4
MIB = 1024 * 1024


def place():
    s = lax.axis_index("seq")
    return lax.div(s, 8), lax.rem(lax.div(s, 2), RING), lax.rem(s, 2)


def up(i):
    return lax.rem(i + 1, RING)


def down(i):
    return lax.rem(i + RING - 1, RING)


def across(i):
    return lax.rem(i + 2, RING)


def index_of(y, z, c):
    return y * 8 + z * 2 + c


def greet(y, z, c, *more):
    barrier = pltpu.get_barrier_semaphore()
    for other in (
        index_of(up(y), z, c),
        index_of(down(y), z, c),
        index_of(y, up(z), c),
        index_of(y, down(z), c),
        index_of(y, z, 1 - c),
    ) + more:
        pl.semaphore_signal(barrier, inc=1, device_id={"seq": other}, device_id_type=MESH)
    pl.semaphore_wait(barrier, 5 + len(more))


def dot_t(a, b):
    return lax.dot_general(a, b, (((1,), (1,)), ((), ())), preferred_element_type=jnp.float32)


def t_dot(a, b):
    return lax.dot_general(a, b, (((0,), (0,)), ((), ())), preferred_element_type=jnp.float32)


def spans_math(qs, gs, keys, values):
    each, both = range(len(qs)), (0, 1)

    def pairs(rows, tables):
        joined = [dot_t(rows[u], jnp.concatenate(tables[u], axis=0)) for u in each]
        return [[x[:, :NBR_LEN], x[:, NBR_LEN:]] for x in joined]

    def narrow(x):
        return x.astype(jnp.bfloat16)

    s = pairs(qs, keys)
    grad = pairs(gs, values)
    top = [[jnp.max(s[u][j], axis=1, keepdims=True) for j in both] for u in each]
    e = [[jnp.exp((s[u][j] - top[u][j]) * SCALE) for j in both] for u in each]
    total = [[jnp.sum(e[u][j], axis=1, keepdims=True) for j in both] for u in each]
    p = [[narrow(e[u][j] * (1.0 / total[u][j])) for j in both] for u in each]
    out = [
        [wide(narrow(jnp.dot(p[u][j], values[u][j], preferred_element_type=jnp.float32))) for j in both]
        for u in each
    ]
    peak = [jnp.maximum(top[u][0], top[u][1]) for u in each]
    lift = [[jnp.exp((top[u][j] - peak[u]) * SCALE) for j in both] for u in each]
    inverse = [1.0 / (total[u][0] * lift[u][0] + total[u][1] * lift[u][1]) for u in each]
    weight = [[lift[u][j] * inverse[u] for j in both] for u in each]
    merged = [
        total[u][0] * weight[u][0] * out[u][0] + total[u][1] * weight[u][1] * out[u][1] for u in each
    ]
    delta = [jnp.sum(wide(gs[u]) * merged[u], axis=1, keepdims=True) for u in each]
    full = [[e[u][j] * weight[u][j] for j in both] for u in each]
    ds = [
        [narrow(full[u][j] * ((grad[u][j] - delta[u]) * SCALE)) for j in both] for u in each
    ]
    parts = [
        [wide(narrow(jnp.dot(ds[u][j], keys[u][j], preferred_element_type=jnp.float32))) for j in both]
        for u in each
    ]
    d_query = [parts[u][0] + parts[u][1] for u in each]
    d_keys = [t_dot(jnp.concatenate(ds[u], axis=1), qs[u]) for u in each]
    d_values = [
        t_dot(jnp.concatenate([narrow(full[u][j]) for j in both], axis=1), gs[u]) for u in each
    ]
    return merged, d_query, d_keys, d_values


def wide(value):
    return value.astype(jnp.float32)


def core_kernel(
    ids, first, second, enc, w_key, w_value, queries, cotangents,
    att_out, dq_out, out, tab, landed,
    table_even, table_odd, ck, cv, acc, give_even, give_odd, got_even, got_odd,
    own, q_buf, g_buf, att_buf, dq_buf, r1, r2, r3, r4,
    send_sem, recv_sem, back_send, back_recv, own_sem, load_sem,
    enc_sem, w_sem, row_sem, rim_send, rim_recv,
):
    y, z, c = place()
    me = index_of(y, z, c)
    count = 2 * RING * RING
    ahead, behind = lax.rem(me + 1, count), lax.rem(me + count - 1, count)
    pairs = own.shape[0] // 2
    tokens = queries.shape[0]
    spans = tokens // SPAN
    reads = 2 * spans
    group = max(n for n in range(1, 8) if spans % n == 0)
    sibling = index_of(y, z, 1 - c)
    every = slice(None)
    held = (table_even, table_odd)
    give = (give_even, give_odd)
    got = (got_even, got_odd)
    weights = (w_key, w_value)
    body, head_rows, tail_rows = pl.ds(0, tokens), pl.ds(0, SPAN), pl.ds(tokens, SPAN)

    def enc_copy(piece):
        at = (lax.div(piece, 8), lax.rem(lax.div(piece, 2), RING), lax.rem(piece, 2))
        return pltpu.make_async_copy(
            enc.at[:, pl.ds(pl.multiple_of(piece * HD, HD), HD)], got_even.at[at], enc_sem.at[piece]
        )

    def weight_copy(h, kv):
        cols = pl.ds(pl.multiple_of(h * HD, HD), HD)
        return pltpu.make_async_copy(
            weights[kv].at[:, :, :, cols], acc.at[h, :, :, kv], w_sem.at[h, kv]
        )

    def for_pieces(action):
        def one(piece, carry):
            action(enc_copy(piece))
            return carry

        lax.fori_loop(0, enc_sem.shape[0], one, 0)

    for_pieces(lambda copy: copy.start())
    for h in (0, 1):
        for kv in (0, 1):
            weight_copy(h, kv).start()
    greet(y, z, c, ahead, behind)
    ck[reads] = jnp.zeros(ck.shape[1:], jnp.float32)
    cv[reads] = jnp.zeros(cv.shape[1:], jnp.float32)
    for_pieces(lambda copy: copy.wait())

    def row_copies():
        return (
            pltpu.make_async_copy(queries, q_buf.at[body], row_sem.at[0]),
            pltpu.make_async_copy(cotangents, g_buf.at[body], row_sem.at[1]),
        )

    def result_copies():
        return (
            pltpu.make_async_copy(att_buf.at[body], att_out, row_sem.at[2]),
            pltpu.make_async_copy(dq_buf.at[body], dq_out, row_sem.at[3]),
        )

    def rim_move(kind):
        src, dst, to = (
            (queries.at[head_rows], q_buf.at[tail_rows], behind),
            (cotangents.at[head_rows], g_buf.at[tail_rows], behind),
            (att_buf.at[tail_rows], att_buf.at[head_rows], ahead),
            (dq_buf.at[tail_rows], dq_buf.at[head_rows], ahead),
        )[kind]
        return pltpu.make_async_remote_copy(
            src_ref=src,
            dst_ref=dst,
            send_sem=rim_send.at[kind],
            recv_sem=rim_recv.at[kind],
            device_id={"seq": to},
            device_id_type=MESH,
        )

    def by_blocks(refs, blend):
        strip = 256
        line = lax.broadcasted_iota(jnp.int32, (SPAN, strip), 0)

        def one(block, carry):
            for ref in refs:
                for start in range(0, ref.shape[1], strip):
                    blend(ref, block, pl.ds(start, strip), line)
            return carry

        lax.fori_loop(0, spans, one, 0)

    def rows_start():
        for copy in row_copies():
            copy.start()
        rim_move(0).start()
        rim_move(1).start()

    def rows_in():
        for kind, copy in enumerate(row_copies()):
            copy.wait()
            rim_move(kind).wait()

        @pl.when(me == count - 1)
        def _():
            for ref in (q_buf, g_buf):
                ref[tail_rows] = jnp.zeros((SPAN, ref.shape[1]), jnp.bfloat16)

        def blend(ref, block, cols, line):
            at = pl.multiple_of(block * SPAN, SPAN)
            before = wide(ref[pl.ds(at + SPAN - 16, 16), cols])[15:16]
            after = pltpu.roll(wide(ref[pl.ds(at + SPAN, SPAN), cols]), 1, 0)
            ref[pl.ds(at, SPAN), cols] = jnp.where(line == 0, before, after).astype(jnp.bfloat16)

        by_blocks((q_buf, g_buf), blend)

    def tail_out():
        rim_move(2).start()
        rim_move(3).start()

    def rows_out():
        rim_move(2).wait()
        rim_move(3).wait()

        @pl.when(me == 0)
        def _():
            for ref in (att_buf, dq_buf):
                ref[head_rows] = jnp.zeros((SPAN, ref.shape[1]), jnp.bfloat16)

        def blend(ref, block, cols, line):
            at = pl.multiple_of(block * SPAN, SPAN)
            here = pltpu.roll(wide(ref[pl.ds(at, SPAN), cols]), SPAN - 1, 0)
            after = wide(ref[pl.ds(at + SPAN, 16), cols])[0:1]
            ref[pl.ds(at, SPAN), cols] = jnp.where(line == SPAN - 1, after, here).astype(jnp.bfloat16)

        by_blocks((att_buf, dq_buf), blend)
        for copy in result_copies():
            copy.start()

    class Head:
        def __init__(self, h, parity):
            self.h, self.parity = h, parity
            self.f, self.g = (y, z) if parity == 0 else (z, y)

        def dev(self, a, b):
            return index_of(a, b, c) if self.parity == 0 else index_of(b, a, c)

        def spot(self, a, b):
            return (self.h, a, b) if self.parity == 0 else (self.h, b, a)

        def block(self, a, *half):
            return tab.at[self.spot(a, self.g) + (c,) + half]

        def band(self, b, *half):
            return tab.at[self.spot(every, b) + (c,) + half]

        def mine(self):
            return pltpu.make_async_copy(own.at[self.h], self.block(self.f), own_sem.at[self.h])

        def load(self):
            return pltpu.make_async_copy(
                tab.at[self.h], held[self.parity], load_sem.at[self.h, 0]
            )

        def fetch(self):
            return pltpu.make_async_copy(
                landed.at[self.h], got[self.parity], load_sem.at[self.h, 1]
            )

        def out_move(self, kind):
            f, g, dev = self.f, self.g, self.dev
            if kind < 4:
                src = (own.at[self.h], own.at[self.h], None, None)[kind]
                dst = (
                    lambda: self.block(f),
                    lambda: self.block(f),
                    lambda: self.block(down(f), 0),
                    lambda: self.block(up(f), 1),
                )[kind]()
                to = dev(up(f), g) if kind % 2 == 0 else dev(down(f), g)
            elif kind < 8:
                dst = (
                    lambda: self.band(g),
                    lambda: self.band(g),
                    lambda: self.band(down(g), slice(0, 1)),
                    lambda: self.band(up(g), slice(1, 2)),
                )[kind - 4]()
                src, to = None, dev(f, up(g)) if kind % 2 == 0 else dev(f, down(g))
            else:
                dst = self.band((g, down(g), up(g), across(g))[kind - 8])
                src, to = None, sibling
            return pltpu.make_async_remote_copy(
                src_ref=dst if src is None else src,
                dst_ref=dst,
                send_sem=send_sem.at[self.h, kind],
                recv_sem=recv_sem.at[self.h, kind],
                device_id={"seq": to},
                device_id_type=MESH,
            )

        def back_move(self, kind):
            f, g, dev, h = self.f, self.g, self.dev, self.h
            src, dst, to = (
                lambda: (give[self.parity], landed.at[h], sibling),
                lambda: (acc.at[self.spot(every, across(g)) + (0,)], r1.at[h, 0], dev(f, up(g))),
                lambda: (acc.at[self.spot(every, across(g)) + (1,)], r1.at[h, 1], dev(f, down(g))),
                lambda: (acc.at[self.spot(every, up(g))], r2.at[h, 0], dev(f, up(g))),
                lambda: (acc.at[self.spot(every, down(g))], r2.at[h, 1], dev(f, down(g))),
                lambda: (acc.at[self.spot(across(f), g) + (0,)], r3.at[h, 0], dev(up(f), g)),
                lambda: (acc.at[self.spot(across(f), g) + (1,)], r3.at[h, 1], dev(down(f), g)),
                lambda: (acc.at[self.spot(up(f), g)], r4.at[h, 0], dev(up(f), g)),
                lambda: (acc.at[self.spot(down(f), g)], r4.at[h, 1], dev(down(f), g)),
            )[kind]()
            return pltpu.make_async_remote_copy(
                src_ref=src,
                dst_ref=dst,
                send_sem=back_send.at[h, kind],
                recv_sem=back_recv.at[h, kind],
                device_id={"seq": to},
                device_id_type=MESH,
            )

    def project(t):
        for kv in (0, 1):
            weight_copy(t.h, kv).wait()

        @pl.when(t.h + 2 < 2 * pairs)
        def _():
            for kv in (0, 1):
                weight_copy(t.h + 2, kv).start()

        deep = [(a, b) for a in range(RING) for b in range(RING)]

        def one(s, carry):
            lines = pl.ds(pl.multiple_of(s * NBR_LEN, NBR_LEN), NBR_LEN)
            left = jnp.concatenate([got_even[a, b, k, lines] for a, b in deep for k in (0, 1)], axis=1)
            right = jnp.concatenate(
                [jnp.concatenate([acc[t.h, a, b, kv] for kv in (0, 1)], axis=1) for a, b in deep], axis=0
            )
            rows = jnp.dot(left, right, preferred_element_type=jnp.float32).astype(jnp.bfloat16)
            for kv in (0, 1):
                own[t.h, kv, s] = rows[:, kv * HD : (kv + 1) * HD]
            return carry

        lax.fori_loop(0, 2, one, 0)

    def own_out(t):
        t.mine().start()
        t.out_move(0).start()
        t.out_move(1).start()

    def block_on(t):
        t.out_move(0).wait_recv()
        t.out_move(2).start()
        t.out_move(1).wait_recv()
        t.out_move(3).start()

    def band_out(t):
        t.mine().wait()
        t.out_move(2).wait_recv()
        t.out_move(3).wait_recv()
        t.out_move(4).start()
        t.out_move(5).start()
        t.out_move(8).start()

    def band_on(t):
        t.out_move(4).wait_recv()
        t.out_move(6).start()
        t.out_move(9).start()
        t.out_move(5).wait_recv()
        t.out_move(7).start()
        t.out_move(10).start()

    def band_last(t):
        t.out_move(6).wait_recv()
        t.out_move(7).wait_recv()
        t.out_move(11).start()

    def table_in(t):
        for kind in (8, 9, 10, 11):
            t.out_move(kind).wait_recv()
        t.load().start()
        for kind in range(12):
            t.out_move(kind).wait_send()

    def sibling_in(t):
        t.back_move(0).wait_recv()
        t.fetch().start()
        t.back_move(0).wait_send()

    def attend(t):
        table, cols = held[t.parity], pl.ds(pl.multiple_of(t.h * HD, HD), HD)
        t.load().wait()

        def pick(n, kv):
            return table[lax.div(n, 16), lax.rem(lax.div(n, 4), RING), lax.rem(lax.div(n, 2), 2), kv, lax.rem(n, 2)]

        def some(i, carry):
            spots = [i * group + u for u in range(group)]
            rows = [pl.ds(pl.multiple_of(s * SPAN, SPAN), SPAN) for s in spots]
            qs, gs = [q_buf[r, cols] for r in rows], [g_buf[r, cols] for r in rows]
            picks = [[ids[2 * s + j] for j in (0, 1)] for s in spots]
            keys = [[pick(n, 0) for n in two] for two in picks]
            values = [[pick(n, 1) for n in two] for two in picks]
            merged, d_query, d_keys, d_values = spans_math(qs, gs, keys, values)
            for u, s in enumerate(spots):
                put = pl.ds(pl.multiple_of((s + 1) * SPAN, SPAN), SPAN)
                att_buf[put, cols] = merged[u].astype(jnp.bfloat16)
                dq_buf[put, cols] = d_query[u].astype(jnp.bfloat16)
                for j in (0, 1):
                    ck[2 * s + j] = d_keys[u][j * NBR_LEN : (j + 1) * NBR_LEN]
                    cv[2 * s + j] = d_values[u][j * NBR_LEN : (j + 1) * NBR_LEN]
            return carry

        lax.fori_loop(0, spans // group, some, 0)

        def fold(chip, carry):
            a, b = lax.div(chip, RING), lax.rem(chip, RING)
            for s in (0, 1):
                for core, keep in ((c, True), (1 - c, False)):
                    n = (2 * chip + core) * 2 + s
                    one, two = first[n], second[n]
                    for kv, part in ((0, ck), (1, cv)):
                        total = (part[one] + part[two]).astype(jnp.bfloat16)
                        lines = pl.ds(s * NBR_LEN, NBR_LEN)
                        if keep:
                            acc[t.h, a, b, kv, lines] = total
                        else:
                            give[t.parity][a, b, kv, lines] = total
            return carry

        lax.fori_loop(0, RING * RING, fold, 0)
        t.back_move(0).start()

    def sum_sibling(t):
        t.fetch().wait()

        def add(i, carry):
            a, b = lax.div(i, RING), lax.rem(i, RING)
            for kv in (0, 1):
                acc[t.h, a, b, kv] = acc[t.h, a, b, kv] + got[t.parity][a, b, kv]
            return carry

        lax.fori_loop(0, RING * RING, add, 0)
        t.back_move(1).start()
        t.back_move(2).start()

    def sum_band_half(t):
        for half, (kind, toward) in enumerate(((1, up(t.g)), (2, down(t.g)))):
            t.back_move(kind).wait_recv()

            def add(a, carry):
                at = t.spot(a, toward) + (half,)
                acc[at] = acc[at] + r1[t.h, half, a]
                return carry

            lax.fori_loop(0, RING, add, 0)
            t.back_move(3 + half).start()

    def sum_band(t):
        t.back_move(3).wait_recv()
        t.back_move(4).wait_recv()

        def add(a, carry):
            for kv in (0, 1):
                at = t.spot(a, t.g) + (kv,)
                total = wide(acc[at]) + wide(r2[t.h, 0, a, kv]) + wide(r2[t.h, 1, a, kv])
                acc[at] = total.astype(jnp.bfloat16)
            return carry

        lax.fori_loop(0, RING, add, 0)
        t.back_move(5).start()
        t.back_move(6).start()

    def sum_block_half(t):
        for half, (kind, toward) in enumerate(((5, up(t.f)), (6, down(t.f)))):
            t.back_move(kind).wait_recv()
            at = t.spot(toward, t.g) + (half,)
            acc[at] = acc[at] + r3[t.h, half]
            t.back_move(7 + half).start()

    def sum_block(t):
        t.back_move(7).wait_recv()
        t.back_move(8).wait_recv()
        for kv in (0, 1):
            total = wide(acc[t.spot(t.f, t.g) + (kv,)])
            total = total + wide(r4[t.h, 0, kv]) + wide(r4[t.h, 1, kv])
            out[t.h, kv] = total.astype(jnp.bfloat16)
        for kind in range(1, 9):
            t.back_move(kind).wait_send()

    stages = (
        (0, project),
        (0, own_out),
        (1, block_on),
        (2, band_out),
        (3, band_on),
        (4, band_last),
        (5, table_in),
        (6, sibling_in),
        (10, sum_block),
        (9, sum_block_half),
        (8, sum_band),
        (7, sum_band_half),
        (5, attend),
        (6, sum_sibling),
    )

    once = {0: rows_start, 3: rows_in, pairs + 4: tail_out, pairs + 5: rows_out}

    def step(i, carry):
        for lag, stage in stages:

            @pl.when((i >= lag) & (i < pairs + lag))
            def _(lag=lag, stage=stage):
                for parity in (0, 1):
                    stage(Head(2 * (i - lag) + parity, parity))

        for when, act in once.items():
            pl.when(i == when)(act)
        return carry

    lax.fori_loop(0, pairs + max(lag for lag, _ in stages), step, 0)
    for copy in result_copies():
        copy.wait()


def core(ids, first, second, enc, w_key, w_value, queries, cotangents):
    rows, width = queries.shape
    depth = enc.shape[1]
    heads, reads = width // HD, ids.shape[0]
    rest = (2, 2, NBR_LEN, HD)
    tail = (2, 2 * NBR_LEN, HD)
    bf16, f32 = jnp.bfloat16, jnp.float32
    in_vmem = pl.BlockSpec(memory_space=pltpu.VMEM)
    in_smem = pl.BlockSpec(memory_space=pltpu.SMEM)
    anywhere = pl.BlockSpec(memory_space=pl.ANY)
    band = (RING, RING) + tail
    dma = pltpu.SemaphoreType.DMA
    folded = (RING, RING, depth // (RING * RING), width)
    return pl.pallas_call(
        core_kernel,
        in_specs=[in_smem] * 3 + [anywhere] * 5,
        out_specs=[anywhere, anywhere, in_vmem, anywhere, anywhere],
        out_shape=[
            jax.ShapeDtypeStruct((rows, width), bf16),
            jax.ShapeDtypeStruct((rows, width), bf16),
            jax.ShapeDtypeStruct((heads,) + tail, bf16),
            jax.ShapeDtypeStruct((heads, RING, RING, 2) + rest, bf16),
            jax.ShapeDtypeStruct((heads,) + band, bf16),
        ],
        scratch_shapes=[
            pltpu.VMEM((RING, RING, 2) + rest, bf16),
            pltpu.VMEM((RING, RING, 2) + rest, bf16),
            pltpu.VMEM((reads + 1, NBR_LEN, HD), f32),
            pltpu.VMEM((reads + 1, NBR_LEN, HD), f32),
            pltpu.VMEM((heads,) + band, bf16),
            pltpu.VMEM(band, bf16),
            pltpu.VMEM(band, bf16),
            pltpu.VMEM(band, bf16),
            pltpu.VMEM(band, bf16),
            pltpu.VMEM((heads,) + rest, bf16),
            pltpu.VMEM((rows + SPAN, width), bf16),
            pltpu.VMEM((rows + SPAN, width), bf16),
            pltpu.VMEM((rows + SPAN, width), bf16),
            pltpu.VMEM((rows + SPAN, width), bf16),
            pltpu.VMEM((heads, 2, RING) + tail[1:], bf16),
            pltpu.VMEM((heads, 2, RING) + tail, bf16),
            pltpu.VMEM((heads, 2) + tail[1:], bf16),
            pltpu.VMEM((heads, 2) + tail, bf16),
            dma((heads, 12)),
            dma((heads, 12)),
            dma((heads, 9)),
            dma((heads, 9)),
            dma((heads,)),
            dma((heads, 2)),
            dma((depth // HD,)),
            dma((heads, 2)),
            dma((4,)),
            dma((4,)),
            dma((4,)),
        ],
        compiler_params=pltpu.CompilerParams(
            collective_id=0, has_side_effects=True, vmem_limit_bytes=63 * MIB
        ),
        name="core",
    )(ids, first, second, enc, w_key.reshape(folded), w_value.reshape(folded), queries, cotangents)


def final_kernel(
    grads, w_key, w_value, out, held, wide_right, wide_left, s1, s2, r1, r2, send_sem, recv_sem, w_sem
):
    x = lax.axis_index("enc")
    right, left = up(x), down(x)
    order = (across(x), right, left, x)
    weights = (w_key, w_value)
    heads = grads.shape[0]

    def weight_copy(k, kv):
        return pltpu.make_async_copy(weights[kv].at[order[k]], held.at[k, kv], w_sem.at[k, kv])

    for k in range(RING):
        for kv in (0, 1):
            weight_copy(k, kv).start()
    barrier = pltpu.get_barrier_semaphore()
    for other in (right, left):
        pl.semaphore_signal(barrier, inc=1, device_id={"enc": other}, device_id_type=MESH)
    pl.semaphore_wait(barrier, 2)
    rows, width = out.shape
    half = rows // 2
    strip = 256
    lhs = [jnp.concatenate([grads[h, kv] for h in range(heads)], axis=1) for kv in (0, 1)]

    def product(k, put):
        for kv in (0, 1):
            weight_copy(k, kv).wait()

        def one(n, carry):
            lines = pl.ds(pl.multiple_of(n * strip, strip), strip)
            put(lines, sum(dot_t(lhs[kv], held[k, kv, lines, :]) for kv in (0, 1)))
            return carry

        lax.fori_loop(0, width // strip, one, 0)

    def remote(kind, src, dst, to):
        return pltpu.make_async_remote_copy(
            src_ref=src,
            dst_ref=dst,
            send_sem=send_sem.at[kind],
            recv_sem=recv_sem.at[kind],
            device_id={"enc": to},
            device_id_type=MESH,
        )

    moves = [
        remote(0, s1.at[0], r1.at[0], right),
        remote(1, s1.at[1], r1.at[1], left),
        remote(2, s2.at[0], r2.at[0], right),
        remote(3, s2.at[1], r2.at[1], left),
    ]

    def put_far(cols, part):
        s1[0, :, cols] = part[:half].astype(jnp.bfloat16)
        s1[1, :, cols] = part[half:].astype(jnp.bfloat16)

    def put_right(cols, part):
        wide_right[:, cols] = part[:half]
        s2[0, pl.ds(half, half), cols] = part[half:].astype(jnp.bfloat16)

    def put_left(cols, part):
        s2[1, pl.ds(0, half), cols] = part[:half].astype(jnp.bfloat16)
        wide_left[:, cols] = part[half:]

    product(0, put_far)
    moves[0].start()
    moves[1].start()
    product(1, put_right)
    product(2, put_left)
    moves[0].wait_recv()
    s2[0, :half] = (wide_right[...] + wide(r1[0])).astype(jnp.bfloat16)
    moves[2].start()
    moves[1].wait_recv()
    s2[1, half:] = (wide_left[...] + wide(r1[1])).astype(jnp.bfloat16)
    moves[3].start()

    def put_mine(cols, part):
        wide_right[:, cols] = part[:half]
        wide_left[:, cols] = part[half:]

    product(3, put_mine)
    moves[2].wait_recv()
    moves[3].wait_recv()
    for part, lines in ((wide_right, pl.ds(0, half)), (wide_left, pl.ds(half, half))):
        total = part[...] + wide(r2[0, lines]) + wide(r2[1, lines])
        out[lines] = total.astype(jnp.bfloat16)
    for move in moves:
        move.wait_send()


def final(grads, w_key, w_value):
    rows, width = grads.shape[2], w_key.shape[1]
    half = rows // 2
    bf16 = jnp.bfloat16
    blocks = (RING, w_key.shape[0] // RING, width)
    in_vmem = pl.BlockSpec(memory_space=pltpu.VMEM)
    anywhere = pl.BlockSpec(memory_space=pl.ANY)
    return pl.pallas_call(
        final_kernel,
        out_shape=jax.ShapeDtypeStruct((rows, blocks[1]), bf16),
        in_specs=[in_vmem, anywhere, anywhere],
        out_specs=in_vmem,
        scratch_shapes=[
            pltpu.VMEM((RING, 2) + blocks[1:], bf16),
            pltpu.VMEM((half, blocks[1]), jnp.float32),
            pltpu.VMEM((half, blocks[1]), jnp.float32),
            pltpu.VMEM((2, half, blocks[1]), bf16),
            pltpu.VMEM((2, rows, blocks[1]), bf16),
            pltpu.VMEM((2, half, blocks[1]), bf16),
            pltpu.VMEM((2, rows, blocks[1]), bf16),
            pltpu.SemaphoreType.DMA((4,)),
            pltpu.SemaphoreType.DMA((4,)),
            pltpu.SemaphoreType.DMA((RING, 2)),
        ],
        compiler_params=pltpu.CompilerParams(
            collective_id=1, has_side_effects=True, vmem_limit_bytes=48 * MIB
        ),
        name="final",
    )(grads, w_key.reshape(blocks), w_value.reshape(blocks))


def per_device(queries, d_attended, encodings, w_key, w_value, neighbour_owner, neighbour_slot):
    tok_rows, feat_width = queries.shape
    heads = feat_width // HD
    owned = encodings.shape[0]
    owners = lax.axis_size("seq")
    reads = 2 * (tok_rows // SPAN)

    ids = (neighbour_owner * owned + neighbour_slot).reshape(reads).astype(jnp.int32)
    hit = ids[None, :] == jnp.arange(owners * owned, dtype=jnp.int32)[:, None]
    order = jnp.arange(reads, dtype=jnp.int32)[None, :]
    first = jnp.min(jnp.where(hit, order, reads), axis=1)
    last = jnp.max(jnp.where(hit, order, -1), axis=1)
    second = jnp.where(last > first, last, reads)

    enc_flat = encodings.reshape(owned * NBR_LEN, encodings.shape[2])
    attended, d_queries, grads, _, _ = core(
        ids, first, second, enc_flat, w_key, w_value, queries, d_attended
    )
    d_encodings = final(grads, w_key, w_value).reshape(owned, NBR_LEN, feat_width)
    return (attended, d_queries, d_encodings)


def solution(mesh):
    return jax.shard_map(
        per_device,
        mesh=mesh,
        in_specs=(
            P("seq", "enc"),
            P("seq", "enc"),
            P("seq", None, None),
            P(None, "enc"),
            P(None, "enc"),
            P("seq", None),
            P("seq", None),
        ),
        out_specs=(P("seq", "enc"), P("seq", "enc"), P("seq", None, "enc")),
        check_vma=False,
    )
```

```python
import math

import jax
import jax.numpy as jnp
from jax import lax
from jax.experimental import pallas as pl
from jax.experimental.pallas import tpu as pltpu
from jax.sharding import PartitionSpec as P

HD = 128
SPAN = 64
NBR_LEN = 128
MESH = pl.DeviceIdType.MESH
SCALE = 1.0 / math.sqrt(HD)
RING = 4
MIB = 1024 * 1024


def place():
    s = lax.axis_index("seq")
    return lax.div(s, 8), lax.rem(lax.div(s, 2), RING), lax.rem(s, 2)


def up(i):
    return lax.rem(i + 1, RING)


def down(i):
    return lax.rem(i + RING - 1, RING)


def across(i):
    return lax.rem(i + 2, RING)


def index_of(y, z, c):
    return y * 8 + z * 2 + c


def greet(y, z, c, seq_more, enc_more):
    barrier = pltpu.get_barrier_semaphore()
    near = (
        index_of(up(y), z, c),
        index_of(down(y), z, c),
        index_of(y, up(z), c),
        index_of(y, down(z), c),
        index_of(y, z, 1 - c),
    )
    partners = [{"seq": other} for other in near + seq_more] + [{"enc": other} for other in enc_more]
    for partner in partners:
        pl.semaphore_signal(barrier, inc=1, device_id=partner, device_id_type=MESH)
    pl.semaphore_wait(barrier, len(partners))


def dot_t(a, b):
    return lax.dot_general(a, b, (((1,), (1,)), ((), ())), preferred_element_type=jnp.float32)


def t_dot(a, b):
    return lax.dot_general(a, b, (((0,), (0,)), ((), ())), preferred_element_type=jnp.float32)


def spans_math(qs, gs, keys, values):
    each, both = range(len(qs)), (0, 1)

    def pairs(rows, tables):
        joined = [dot_t(rows[u], jnp.concatenate(tables[u], axis=0)) for u in each]
        return [[x[:, :NBR_LEN], x[:, NBR_LEN:]] for x in joined]

    def narrow(x):
        return x.astype(jnp.bfloat16)

    s = pairs(qs, keys)
    grad = pairs(gs, values)
    top = [[jnp.max(s[u][j], axis=1, keepdims=True) for j in both] for u in each]
    e = [[jnp.exp((s[u][j] - top[u][j]) * SCALE) for j in both] for u in each]
    total = [[jnp.sum(e[u][j], axis=1, keepdims=True) for j in both] for u in each]
    p = [[narrow(e[u][j] * (1.0 / total[u][j])) for j in both] for u in each]
    out = [
        [wide(narrow(jnp.dot(p[u][j], values[u][j], preferred_element_type=jnp.float32))) for j in both]
        for u in each
    ]
    peak = [jnp.maximum(top[u][0], top[u][1]) for u in each]
    lift = [[jnp.exp((top[u][j] - peak[u]) * SCALE) for j in both] for u in each]
    inverse = [1.0 / (total[u][0] * lift[u][0] + total[u][1] * lift[u][1]) for u in each]
    weight = [[lift[u][j] * inverse[u] for j in both] for u in each]
    merged = [
        total[u][0] * weight[u][0] * out[u][0] + total[u][1] * weight[u][1] * out[u][1] for u in each
    ]
    delta = [jnp.sum(wide(gs[u]) * merged[u], axis=1, keepdims=True) for u in each]
    full = [[e[u][j] * weight[u][j] for j in both] for u in each]
    ds = [
        [narrow(full[u][j] * ((grad[u][j] - delta[u]) * SCALE)) for j in both] for u in each
    ]
    parts = [
        [wide(narrow(jnp.dot(ds[u][j], keys[u][j], preferred_element_type=jnp.float32))) for j in both]
        for u in each
    ]
    d_query = [parts[u][0] + parts[u][1] for u in each]
    d_keys = [t_dot(jnp.concatenate(ds[u], axis=1), qs[u]) for u in each]
    d_values = [
        t_dot(jnp.concatenate([narrow(full[u][j]) for j in both], axis=1), gs[u]) for u in each
    ]
    return merged, d_query, d_keys, d_values


def wide(value):
    return value.astype(jnp.float32)


def core_kernel(
    ids, first, second, enc, w_key, w_value, queries, cotangents,
    att_out, dq_out, enc_out, tab, landed,
    table_even, table_odd, ck, cv, acc, give_even, give_odd, got_even, got_odd,
    own, q_buf, g_buf, att_buf, dq_buf, r1, r2, r3, r4, e1, e2,
    send_sem, recv_sem, back_send, back_recv, own_sem, load_sem,
    enc_sem, w_sem, row_sem, rim_send, rim_recv, block_sem, enc_send, enc_recv,
):
    x = lax.axis_index("enc")
    right, left = up(x), down(x)
    y, z, c = place()
    me = index_of(y, z, c)
    count = 2 * RING * RING
    ahead, behind = lax.rem(me + 1, count), lax.rem(me + count - 1, count)
    heads = own.shape[0]
    tokens = queries.shape[0]
    spans = tokens // SPAN
    reads = 2 * spans
    group = max(n for n in range(1, 8) if spans % n == 0)
    sibling = index_of(y, z, 1 - c)
    every = slice(None)
    held = (table_even, table_odd)
    give = (give_even, give_odd)
    got = (got_even, got_odd)
    weights = (w_key, w_value)
    body, head_rows, tail_rows = pl.ds(0, tokens), pl.ds(0, SPAN), pl.ds(tokens, SPAN)

    def enc_copy(piece):
        at = (lax.div(piece, 8), lax.rem(lax.div(piece, 2), RING), lax.rem(piece, 2))
        return pltpu.make_async_copy(
            enc.at[:, pl.ds(pl.multiple_of(piece * HD, HD), HD)], got_even.at[at], enc_sem.at[piece]
        )

    def weight_copy(h, kv):
        cols = pl.ds(pl.multiple_of(h * HD, HD), HD)
        return pltpu.make_async_copy(
            weights[kv].at[:, :, :, cols], acc.at[h, :, :, kv], w_sem.at[h, kv]
        )

    def for_pieces(action):
        def one(piece, carry):
            action(enc_copy(piece))
            return carry

        lax.fori_loop(0, enc_sem.shape[0], one, 0)

    for_pieces(lambda copy: copy.start())
    for h in (0, 1):
        for kv in (0, 1):
            weight_copy(h, kv).start()
    greet(y, z, c, (ahead, behind), (right, left))
    ck[reads] = jnp.zeros(ck.shape[1:], jnp.float32)
    cv[reads] = jnp.zeros(cv.shape[1:], jnp.float32)
    for_pieces(lambda copy: copy.wait())

    def row_copies():
        return (
            pltpu.make_async_copy(queries, q_buf.at[body], row_sem.at[0]),
            pltpu.make_async_copy(cotangents, g_buf.at[body], row_sem.at[1]),
        )

    def result_copies():
        return (
            pltpu.make_async_copy(att_buf.at[body], att_out, row_sem.at[2]),
            pltpu.make_async_copy(dq_buf.at[body], dq_out, row_sem.at[3]),
        )

    def rim_move(kind):
        src, dst, to = (
            (queries.at[head_rows], q_buf.at[tail_rows], behind),
            (cotangents.at[head_rows], g_buf.at[tail_rows], behind),
            (att_buf.at[tail_rows], att_buf.at[head_rows], ahead),
            (dq_buf.at[tail_rows], dq_buf.at[head_rows], ahead),
        )[kind]
        return pltpu.make_async_remote_copy(
            src_ref=src,
            dst_ref=dst,
            send_sem=rim_send.at[kind],
            recv_sem=rim_recv.at[kind],
            device_id={"seq": to},
            device_id_type=MESH,
        )

    def by_blocks(refs, blend):
        strip = 256
        line = lax.broadcasted_iota(jnp.int32, (SPAN, strip), 0)

        def one(block, carry):
            for ref in refs:
                for start in range(0, ref.shape[1], strip):
                    blend(ref, block, pl.ds(start, strip), line)
            return carry

        lax.fori_loop(0, spans, one, 0)

    def rows_start():
        for copy in row_copies():
            copy.start()
        rim_move(0).start()
        rim_move(1).start()

    def rows_in():
        for kind, copy in enumerate(row_copies()):
            copy.wait()
            rim_move(kind).wait()

        @pl.when(me == count - 1)
        def _():
            for ref in (q_buf, g_buf):
                ref[tail_rows] = jnp.zeros((SPAN, ref.shape[1]), jnp.bfloat16)

        def blend(ref, block, cols, line):
            at = pl.multiple_of(block * SPAN, SPAN)
            before = wide(ref[pl.ds(at + SPAN - 16, 16), cols])[15:16]
            after = pltpu.roll(wide(ref[pl.ds(at + SPAN, SPAN), cols]), 1, 0)
            ref[pl.ds(at, SPAN), cols] = jnp.where(line == 0, before, after).astype(jnp.bfloat16)

        by_blocks((q_buf, g_buf), blend)

    def tail_out():
        rim_move(2).start()
        rim_move(3).start()

    def rows_out():
        rim_move(2).wait()
        rim_move(3).wait()

        @pl.when(me == 0)
        def _():
            for ref in (att_buf, dq_buf):
                ref[head_rows] = jnp.zeros((SPAN, ref.shape[1]), jnp.bfloat16)

        def blend(ref, block, cols, line):
            at = pl.multiple_of(block * SPAN, SPAN)
            here = pltpu.roll(wide(ref[pl.ds(at, SPAN), cols]), SPAN - 1, 0)
            after = wide(ref[pl.ds(at + SPAN, 16), cols])[0:1]
            ref[pl.ds(at, SPAN), cols] = jnp.where(line == SPAN - 1, after, here).astype(jnp.bfloat16)

        by_blocks((att_buf, dq_buf), blend)
        for copy in result_copies():
            copy.start()

    class Head:
        def __init__(self, h, parity, slots=(0, 1)):
            self.h, self.parity, self.slots = h, parity, slots
            self.lines = pl.ds(slots[0] * NBR_LEN, len(slots) * NBR_LEN)
            self.f, self.g = (y, z) if parity == 0 else (z, y)

        def dev(self, a, b):
            return index_of(a, b, c) if self.parity == 0 else index_of(b, a, c)

        def spot(self, a, b):
            return (self.h, a, b) if self.parity == 0 else (self.h, b, a)

        def block(self, a, *half):
            return tab.at[self.spot(a, self.g) + (c,) + half]

        def band(self, b, *half):
            return tab.at[self.spot(every, b) + (c,) + half]

        def mine(self):
            return pltpu.make_async_copy(own.at[self.h], self.block(self.f), own_sem.at[self.h])

        def load(self):
            return pltpu.make_async_copy(
                tab.at[self.h], held[self.parity], load_sem.at[self.h, 0]
            )

        def fetch(self):
            return pltpu.make_async_copy(
                landed.at[self.h], got[self.parity], load_sem.at[self.h, 1]
            )

        def out_move(self, kind):
            f, g, dev = self.f, self.g, self.dev
            if kind < 4:
                src = (own.at[self.h], own.at[self.h], None, None)[kind]
                dst = (
                    lambda: self.block(f),
                    lambda: self.block(f),
                    lambda: self.block(down(f), 0),
                    lambda: self.block(up(f), 1),
                )[kind]()
                to = dev(up(f), g) if kind % 2 == 0 else dev(down(f), g)
            elif kind < 8:
                dst = (
                    lambda: self.band(g),
                    lambda: self.band(g),
                    lambda: self.band(down(g), slice(0, 1)),
                    lambda: self.band(up(g), slice(1, 2)),
                )[kind - 4]()
                src, to = None, dev(f, up(g)) if kind % 2 == 0 else dev(f, down(g))
            else:
                dst = self.band((g, down(g), up(g), across(g))[kind - 8])
                src, to = None, sibling
            return pltpu.make_async_remote_copy(
                src_ref=dst if src is None else src,
                dst_ref=dst,
                send_sem=send_sem.at[self.h, kind],
                recv_sem=recv_sem.at[self.h, kind],
                device_id={"seq": to},
                device_id_type=MESH,
            )

        def back_move(self, kind):
            f, g, dev, h, spot = self.f, self.g, self.dev, self.h, self.spot
            here = self.lines
            src, dst, to = (
                lambda: (give[self.parity], landed.at[h], sibling),
                lambda: (acc.at[spot(every, across(g)) + (0, here)], r1.at[h, 0, :, here], dev(f, up(g))),
                lambda: (acc.at[spot(every, across(g)) + (1, here)], r1.at[h, 1, :, here], dev(f, down(g))),
                lambda: (acc.at[spot(every, up(g)) + (every, here)], r2.at[h, 0, :, :, here], dev(f, up(g))),
                lambda: (acc.at[spot(every, down(g)) + (every, here)], r2.at[h, 1, :, :, here], dev(f, down(g))),
                lambda: (acc.at[spot(across(f), g) + (0, here)], r3.at[h, 0, here], dev(up(f), g)),
                lambda: (acc.at[spot(across(f), g) + (1, here)], r3.at[h, 1, here], dev(down(f), g)),
                lambda: (acc.at[spot(up(f), g) + (every, here)], r4.at[h, 0, :, here], dev(up(f), g)),
                lambda: (acc.at[spot(down(f), g) + (every, here)], r4.at[h, 1, :, here], dev(down(f), g)),
            )[kind]()
            place_of = 0 if kind == 0 else self.slots[0] * 8 + kind
            return pltpu.make_async_remote_copy(
                src_ref=src,
                dst_ref=dst,
                send_sem=back_send.at[h, place_of],
                recv_sem=back_recv.at[h, place_of],
                device_id={"seq": to},
                device_id_type=MESH,
            )

    def project(t):
        for kv in (0, 1):
            weight_copy(t.h, kv).wait()

        @pl.when(t.h + 2 < heads)
        def _():
            for kv in (0, 1):
                weight_copy(t.h + 2, kv).start()

        deep = [(a, b) for a in range(RING) for b in range(RING)]

        def one(s, carry):
            lines = pl.ds(pl.multiple_of(s * NBR_LEN, NBR_LEN), NBR_LEN)
            left = jnp.concatenate([got_even[a, b, k, lines] for a, b in deep for k in (0, 1)], axis=1)
            right = jnp.concatenate(
                [jnp.concatenate([acc[t.h, a, b, kv] for kv in (0, 1)], axis=1) for a, b in deep], axis=0
            )
            rows = jnp.dot(left, right, preferred_element_type=jnp.float32).astype(jnp.bfloat16)
            for kv in (0, 1):
                own[t.h, kv, s] = rows[:, kv * HD : (kv + 1) * HD]
            return carry

        lax.fori_loop(0, 2, one, 0)

    def own_out(t):
        project(t)
        t.mine().start()
        t.out_move(0).start()
        t.out_move(1).start()

    def block_on(t):
        t.out_move(0).wait_recv()
        t.out_move(2).start()
        t.out_move(1).wait_recv()
        t.out_move(3).start()

    def band_out(t):
        t.mine().wait()
        t.out_move(2).wait_recv()
        t.out_move(3).wait_recv()
        t.out_move(4).start()
        t.out_move(5).start()
        t.out_move(8).start()

    def band_on(t):
        t.out_move(4).wait_recv()
        t.out_move(6).start()
        t.out_move(9).start()
        t.out_move(5).wait_recv()
        t.out_move(7).start()
        t.out_move(10).start()

    def band_last(t):
        t.out_move(6).wait_recv()
        t.out_move(7).wait_recv()
        t.out_move(11).start()

    def table_in(t):
        for kind in (8, 9, 10, 11):
            t.out_move(kind).wait_recv()
        t.load().start()
        for kind in range(12):
            t.out_move(kind).wait_send()

    def sibling_in(t):
        t.back_move(0).wait_recv()
        t.fetch().start()
        t.back_move(0).wait_send()

    def attend(t):
        table, cols = held[t.parity], pl.ds(pl.multiple_of(t.h * HD, HD), HD)
        t.load().wait()

        def pick(n, kv):
            return table[lax.div(n, 16), lax.rem(lax.div(n, 4), RING), lax.rem(lax.div(n, 2), 2), kv, lax.rem(n, 2)]

        def some(i, carry):
            spots = [i * group + u for u in range(group)]
            rows = [pl.ds(pl.multiple_of(s * SPAN, SPAN), SPAN) for s in spots]
            qs, gs = [q_buf[r, cols] for r in rows], [g_buf[r, cols] for r in rows]
            picks = [[ids[2 * s + j] for j in (0, 1)] for s in spots]
            keys = [[pick(n, 0) for n in two] for two in picks]
            values = [[pick(n, 1) for n in two] for two in picks]
            merged, d_query, d_keys, d_values = spans_math(qs, gs, keys, values)
            for u, s in enumerate(spots):
                put = pl.ds(pl.multiple_of((s + 1) * SPAN, SPAN), SPAN)
                att_buf[put, cols] = merged[u].astype(jnp.bfloat16)
                dq_buf[put, cols] = d_query[u].astype(jnp.bfloat16)
                for j in (0, 1):
                    ck[2 * s + j] = d_keys[u][j * NBR_LEN : (j + 1) * NBR_LEN]
                    cv[2 * s + j] = d_values[u][j * NBR_LEN : (j + 1) * NBR_LEN]
            return carry

        lax.fori_loop(0, spans // group, some, 0)

        def fold(chip, carry):
            a, b = lax.div(chip, RING), lax.rem(chip, RING)
            for s in (0, 1):
                for core, keep in ((c, True), (1 - c, False)):
                    n = (2 * chip + core) * 2 + s
                    one, two = first[n], second[n]
                    for kv, part in ((0, ck), (1, cv)):
                        total = (part[one] + part[two]).astype(jnp.bfloat16)
                        lines = pl.ds(s * NBR_LEN, NBR_LEN)
                        if keep:
                            acc[t.h, a, b, kv, lines] = total
                        else:
                            give[t.parity][a, b, kv, lines] = total
            return carry

        lax.fori_loop(0, RING * RING, fold, 0)
        t.back_move(0).start()

    def sum_sibling(t):
        t.fetch().wait()

        def add(i, carry):
            a, b = lax.div(i, RING), lax.rem(i, RING)
            for kv in (0, 1):
                acc[t.h, a, b, kv] = acc[t.h, a, b, kv] + got[t.parity][a, b, kv]
            return carry

        lax.fori_loop(0, RING * RING, add, 0)

    def halves_out(t):
        t.back_move(1).start()
        t.back_move(2).start()

    def sum_band_half(t):
        for half, (kind, toward) in enumerate(((1, up(t.g)), (2, down(t.g)))):
            t.back_move(kind).wait_recv()

            def add(a, carry):
                at = t.spot(a, toward) + (half, t.lines)
                acc[at] = acc[at] + r1[t.h, half, a, t.lines]
                return carry

            lax.fori_loop(0, RING, add, 0)
            t.back_move(3 + half).start()

    def sum_band(t):
        t.back_move(3).wait_recv()
        t.back_move(4).wait_recv()

        def add(a, carry):
            for kv in (0, 1):
                at = t.spot(a, t.g) + (kv, t.lines)
                total = wide(acc[at]) + wide(r2[t.h, 0, a, kv, t.lines]) + wide(r2[t.h, 1, a, kv, t.lines])
                acc[at] = total.astype(jnp.bfloat16)
            return carry

        lax.fori_loop(0, RING, add, 0)
        t.back_move(5).start()
        t.back_move(6).start()

    def sum_block_half(t):
        for half, (kind, toward) in enumerate(((5, up(t.f)), (6, down(t.f)))):
            t.back_move(kind).wait_recv()
            at = t.spot(toward, t.g) + (half, t.lines)
            acc[at] = acc[at] + r3[t.h, half, t.lines]
            t.back_move(7 + half).start()

    def sum_block(t):
        t.back_move(7).wait_recv()
        t.back_move(8).wait_recv()
        for kv in (0, 1):
            for slot in t.slots:
                lines = pl.ds(slot * NBR_LEN, NBR_LEN)
                total = wide(acc[t.spot(t.f, t.g) + (kv, lines)])
                total = total + wide(r4[t.h, 0, kv, lines]) + wide(r4[t.h, 1, kv, lines])
                own[t.h, kv, slot] = total.astype(jnp.bfloat16)
        for kind in range(1, 9):
            t.back_move(kind).wait_send()

    pairs = heads // 2
    split = (pairs - 2, pairs - 1)
    sums = (ck, cv)

    def pair_copies(pair, action):
        for n in (0, 1):
            cols = pl.ds((2 * pair + n) * HD, HD)
            for core in (0, 1):
                for kv in (0, 1):
                    action(
                        pltpu.make_async_copy(
                            weights[kv].at[:, :, pl.ds(core * HD, HD), cols],
                            held[pair % 2].at[:, :, core, kv, n],
                            block_sem.at[pair, 4 * n + 2 * core + kv],
                        )
                    )

    def pair_start(*which):
        for pair in which:
            pair_copies(pair, lambda copy: copy.start())

    deep = [(kv, n) for kv in (0, 1) for n in (0, 1)]

    def rows_of(pair, slot):
        return jnp.concatenate([own[2 * pair + n, kv, slot] for kv, n in deep], axis=1)

    def weights_of(pair, t, a):
        table = held[pair % 2]
        return jnp.concatenate(
            [jnp.concatenate([table[t, a, core, kv, n] for kv, n in deep], axis=1) for core in (0, 1)],
            axis=0,
        )

    def gather_pair(pair):
        pair_copies(pair, lambda copy: copy.wait())
        lhs = jnp.concatenate([rows_of(pair, slot) for slot in (0, 1)], axis=0)

        def one(m, carry):
            t, a = lax.div(m, RING), lax.rem(m, RING)
            part = dot_t(lhs, weights_of(pair, t, a))
            for slot in (0, 1):
                for core in (0, 1):
                    at = 8 * t + 2 * a + core
                    piece = part[slot * NBR_LEN : (slot + 1) * NBR_LEN, core * HD : (core + 1) * HD]
                    sums[slot][at] = piece if pair == 0 else sums[slot][at] + piece
            return carry

        lax.fori_loop(0, RING * RING, one, 0)

    def product(slot, t, put):
        lhs = [rows_of(pair, slot) for pair in split]

        def one(a, carry):
            part = sum(dot_t(rows, weights_of(pair, t, a)) for rows, pair in zip(lhs, split))
            for core in (0, 1):
                at = 8 * t + 2 * a + core
                put(a, core, at, sums[slot][at] + part[:, core * HD : (core + 1) * HD])
            return carry

        lax.fori_loop(0, RING, one, 0)

    half = NBR_LEN // 2
    low, high, whole = pl.ds(0, half), pl.ds(half, half), pl.ds(0, NBR_LEN)

    def enc_move(slot, kind):
        src, dst, to = (
            lambda: (give[slot].at[0, :, :, low], e1.at[slot, 0], right),
            lambda: (give[slot].at[1, :, :, low], e1.at[slot, 1], left),
            lambda: (give[slot].at[2, :, :, whole], e2.at[slot, 0], right),
            lambda: (give[slot].at[3, :, :, whole], e2.at[slot, 1], left),
        )[kind]()
        return pltpu.make_async_remote_copy(
            src_ref=src,
            dst_ref=dst,
            send_sem=enc_send.at[slot, kind],
            recv_sem=enc_recv.at[slot, kind],
            device_id={"enc": to},
            device_id_type=MESH,
        )

    def by_columns(action):
        def one(a, carry):
            for core in (0, 1):
                action(a, core)
            return carry

        lax.fori_loop(0, RING, one, 0)

    def enc_far(slot):
        send, sum_of = give[slot], sums[slot]

        def put_far(a, core, at, total):
            send[0, a, core, low] = total[:half].astype(jnp.bfloat16)
            send[1, a, core, low] = total[half:].astype(jnp.bfloat16)

        def put_right(a, core, at, total):
            sum_of[at] = total
            send[2, a, core, high] = total[half:].astype(jnp.bfloat16)

        def put_left(a, core, at, total):
            sum_of[at] = total
            send[3, a, core, low] = total[:half].astype(jnp.bfloat16)

        def put_mine(a, core, at, total):
            sum_of[at] = total

        if slot == 0:
            for pair in split:
                pair_copies(pair, lambda copy: copy.wait())
        product(slot, across(x), put_far)
        enc_move(slot, 0).start()
        enc_move(slot, 1).start()
        product(slot, right, put_right)
        product(slot, left, put_left)
        product(slot, x, put_mine)

    def enc_near(slot):
        send, sum_of = give[slot], sums[slot]

        def add_right(a, core):
            total = sum_of[8 * right + 2 * a + core, low] + wide(e1[slot, 0, a, core])
            send[2, a, core, low] = total.astype(jnp.bfloat16)

        def add_left(a, core):
            total = sum_of[8 * left + 2 * a + core, high] + wide(e1[slot, 1, a, core])
            send[3, a, core, high] = total.astype(jnp.bfloat16)

        enc_move(slot, 0).wait_recv()
        by_columns(add_right)
        enc_move(slot, 2).start()
        enc_move(slot, 1).wait_recv()
        by_columns(add_left)
        enc_move(slot, 3).start()

    def enc_done(slot):
        enc_move(slot, 2).wait_recv()
        enc_move(slot, 3).wait_recv()

        for a in range(RING):
            for core in (0, 1):
                total = sums[slot][8 * x + 2 * a + core] + wide(e2[slot, 0, a, core]) + wide(e2[slot, 1, a, core])
                n = 2 * a + core
                enc_out[slot * NBR_LEN : (slot + 1) * NBR_LEN, n * HD : (n + 1) * HD] = total.astype(
                    jnp.bfloat16
                )
        for kind in range(4):
            enc_move(slot, kind).wait_send()

    there = (
        (0, own_out),
        (1, block_on),
        (2, band_out),
        (3, band_on),
        (4, band_last),
        (4, table_in),
    )
    back_small = ((9, sum_block), (8, sum_block_half))
    back_large = ((7, sum_band), (6, sum_band_half))
    turn = ((5, sibling_in), (4, attend), (5, sum_sibling))
    leave = ((5, halves_out),)
    between = {
        12: (lambda: enc_far(0),),
        13: (lambda: enc_near(0),),
        14: (lambda: enc_far(1),),
        15: (lambda: enc_near(1),),
    }
    after = {
        0: (rows_start,),
        3: (rows_in,),
        7: (tail_out,),
        8: (rows_out, lambda: pair_start(0, 1)),
        9: (lambda: gather_pair(0), lambda: pair_start(2)),
        10: (lambda: gather_pair(1), lambda: pair_start(3)),
        15: (lambda: enc_done(0),),
        16: (lambda: enc_done(1),),
    }

    def at_times(i, table):
        for when, acts in table.items():

            @pl.when(i == when)
            def _(acts=acts):
                for act in acts:
                    act()

    def run(i, stages, parts):
        for lag, stage in stages:
            for start, stop, skip, slots in parts:

                @pl.when((i >= start + lag) & (i < stop + lag))
                def _(lag=lag, stage=stage, skip=skip, slots=slots):
                    for parity in (0, 1):
                        stage(Head(2 * (i - lag - skip) + parity, parity, slots))

    both = ((0, pairs, 0, (0, 1)),)
    apart = (
        (0, pairs - 2, 0, (0, 1)),
        (pairs - 2, pairs, 0, (0,)),
        (pairs, pairs + 2, 2, (1,)),
    )

    def step(i, carry):
        run(i, there, both)
        run(i, back_small, apart)
        at_times(i, between)
        run(i, back_large, apart)
        run(i, turn, both)
        run(i, leave, apart)
        at_times(i, after)
        return carry

    lax.fori_loop(0, max(after) + 1, step, 0)
    for copy in result_copies():
        copy.wait()


def core(ids, first, second, enc, w_key, w_value, queries, cotangents):
    rows, width = queries.shape
    depth = enc.shape[1]
    heads, reads = width // HD, ids.shape[0]
    rest = (2, 2, NBR_LEN, HD)
    tail = (2, 2 * NBR_LEN, HD)
    bf16, f32 = jnp.bfloat16, jnp.float32
    in_vmem = pl.BlockSpec(memory_space=pltpu.VMEM)
    in_smem = pl.BlockSpec(memory_space=pltpu.SMEM)
    anywhere = pl.BlockSpec(memory_space=pl.ANY)
    band = (RING, RING) + tail
    dma = pltpu.SemaphoreType.DMA
    folded = (RING, RING, depth // (RING * RING), width)
    return pl.pallas_call(
        core_kernel,
        in_specs=[in_smem] * 3 + [anywhere] * 5,
        out_specs=[anywhere, anywhere, in_vmem, anywhere, anywhere],
        out_shape=[
            jax.ShapeDtypeStruct((rows, width), bf16),
            jax.ShapeDtypeStruct((rows, width), bf16),
            jax.ShapeDtypeStruct((tail[1], depth // RING), bf16),
            jax.ShapeDtypeStruct((heads, RING, RING, 2) + rest, bf16),
            jax.ShapeDtypeStruct((heads,) + band, bf16),
        ],
        scratch_shapes=[
            pltpu.VMEM((RING, RING, 2) + rest, bf16),
            pltpu.VMEM((RING, RING, 2) + rest, bf16),
            pltpu.VMEM((max(reads + 1, depth // HD), NBR_LEN, HD), f32),
            pltpu.VMEM((max(reads + 1, depth // HD), NBR_LEN, HD), f32),
            pltpu.VMEM((heads,) + band, bf16),
            pltpu.VMEM(band, bf16),
            pltpu.VMEM(band, bf16),
            pltpu.VMEM(band, bf16),
            pltpu.VMEM(band, bf16),
            pltpu.VMEM((heads,) + rest, bf16),
            pltpu.VMEM((rows + SPAN, width), bf16),
            pltpu.VMEM((rows + SPAN, width), bf16),
            pltpu.VMEM((rows + SPAN, width), bf16),
            pltpu.VMEM((rows + SPAN, width), bf16),
            pltpu.VMEM((heads, 2, RING) + tail[1:], bf16),
            pltpu.VMEM((heads, 2, RING) + tail, bf16),
            pltpu.VMEM((heads, 2) + tail[1:], bf16),
            pltpu.VMEM((heads, 2) + tail, bf16),
            pltpu.VMEM((2, 2, RING, 2, NBR_LEN // 2, HD), bf16),
            pltpu.VMEM((2, 2, RING, 2, NBR_LEN, HD), bf16),
            dma((heads, 12)),
            dma((heads, 12)),
            dma((heads, 17)),
            dma((heads, 17)),
            dma((heads,)),
            dma((heads, 2)),
            dma((depth // HD,)),
            dma((heads, 2)),
            dma((4,)),
            dma((4,)),
            dma((4,)),
            dma((heads // 2, 8)),
            dma((2, 4)),
            dma((2, 4)),
        ],
        compiler_params=pltpu.CompilerParams(
            collective_id=0, has_side_effects=True, vmem_limit_bytes=64 * MIB
        ),
        name="core",
    )(ids, first, second, enc, w_key.reshape(folded), w_value.reshape(folded), queries, cotangents)


def per_device(queries, d_attended, encodings, w_key, w_value, neighbour_owner, neighbour_slot):
    tok_rows, feat_width = queries.shape
    heads = feat_width // HD
    owned = encodings.shape[0]
    owners = lax.axis_size("seq")
    reads = 2 * (tok_rows // SPAN)

    ids = (neighbour_owner * owned + neighbour_slot).reshape(reads).astype(jnp.int32)
    hit = ids[None, :] == jnp.arange(owners * owned, dtype=jnp.int32)[:, None]
    order = jnp.arange(reads, dtype=jnp.int32)[None, :]
    first = jnp.min(jnp.where(hit, order, reads), axis=1)
    last = jnp.max(jnp.where(hit, order, -1), axis=1)
    second = jnp.where(last > first, last, reads)

    enc_flat = encodings.reshape(owned * NBR_LEN, encodings.shape[2])
    attended, d_queries, d_encodings, _, _ = core(
        ids, first, second, enc_flat, w_key, w_value, queries, d_attended
    )
    return (attended, d_queries, d_encodings.reshape(owned, NBR_LEN, feat_width))


def solution(mesh):
    return jax.shard_map(
        per_device,
        mesh=mesh,
        in_specs=(
            P("seq", "enc"),
            P("seq", "enc"),
            P("seq", None, None),
            P(None, "enc"),
            P(None, "enc"),
            P("seq", None),
            P("seq", None),
        ),
        out_specs=(P("seq", "enc"), P("seq", "enc"), P("seq", None, "enc")),
        check_vma=False,
    )
```

```python
import math

import jax
import jax.numpy as jnp
from jax import lax
from jax.experimental import pallas as pl
from jax.experimental.pallas import tpu as pltpu
from jax.sharding import PartitionSpec as P

HD = 128
SPAN = 64
NBR_LEN = 128
MESH = pl.DeviceIdType.MESH
SCALE = 1.0 / math.sqrt(HD)
RING = 4
MIB = 1024 * 1024


def place():
    s = lax.axis_index("seq")
    return lax.div(s, 8), lax.rem(lax.div(s, 2), RING), lax.rem(s, 2)


def up(i):
    return lax.rem(i + 1, RING)


def down(i):
    return lax.rem(i + RING - 1, RING)


def across(i):
    return lax.rem(i + 2, RING)


def index_of(y, z, c):
    return y * 8 + z * 2 + c


def greet(y, z, c, seq_more, enc_more):
    barrier = pltpu.get_barrier_semaphore()
    near = (
        index_of(up(y), z, c),
        index_of(down(y), z, c),
        index_of(y, up(z), c),
        index_of(y, down(z), c),
        index_of(y, z, 1 - c),
    )
    partners = [{"seq": other} for other in near + seq_more] + [{"enc": other} for other in enc_more]
    for partner in partners:
        pl.semaphore_signal(barrier, inc=1, device_id=partner, device_id_type=MESH)
    pl.semaphore_wait(barrier, len(partners))


def dot_t(a, b):
    return lax.dot_general(a, b, (((1,), (1,)), ((), ())), preferred_element_type=jnp.float32)


def t_dot(a, b):
    return lax.dot_general(a, b, (((0,), (0,)), ((), ())), preferred_element_type=jnp.float32)


def spans_math(qs, gs, keys, values):
    each, both = range(len(qs)), (0, 1)

    def pairs(rows, tables):
        joined = [dot_t(rows[u], jnp.concatenate(tables[u], axis=0)) for u in each]
        return [[x[:, :NBR_LEN], x[:, NBR_LEN:]] for x in joined]

    def narrow(x):
        return x.astype(jnp.bfloat16)

    s = pairs(qs, keys)
    grad = pairs(gs, values)
    top = [[jnp.max(s[u][j], axis=1, keepdims=True) for j in both] for u in each]
    e = [[jnp.exp((s[u][j] - top[u][j]) * SCALE) for j in both] for u in each]
    total = [[jnp.sum(e[u][j], axis=1, keepdims=True) for j in both] for u in each]
    p = [[narrow(e[u][j] * (1.0 / total[u][j])) for j in both] for u in each]
    out = [
        [wide(narrow(jnp.dot(p[u][j], values[u][j], preferred_element_type=jnp.float32))) for j in both]
        for u in each
    ]
    peak = [jnp.maximum(top[u][0], top[u][1]) for u in each]
    lift = [[jnp.exp((top[u][j] - peak[u]) * SCALE) for j in both] for u in each]
    inverse = [1.0 / (total[u][0] * lift[u][0] + total[u][1] * lift[u][1]) for u in each]
    weight = [[lift[u][j] * inverse[u] for j in both] for u in each]
    merged = [
        total[u][0] * weight[u][0] * out[u][0] + total[u][1] * weight[u][1] * out[u][1] for u in each
    ]
    delta = [jnp.sum(wide(gs[u]) * merged[u], axis=1, keepdims=True) for u in each]
    full = [[e[u][j] * weight[u][j] for j in both] for u in each]
    ds = [
        [narrow(full[u][j] * ((grad[u][j] - delta[u]) * SCALE)) for j in both] for u in each
    ]
    parts = [
        [wide(narrow(jnp.dot(ds[u][j], keys[u][j], preferred_element_type=jnp.float32))) for j in both]
        for u in each
    ]
    d_query = [parts[u][0] + parts[u][1] for u in each]
    d_keys = [t_dot(jnp.concatenate(ds[u], axis=1), qs[u]) for u in each]
    d_values = [
        t_dot(jnp.concatenate([narrow(full[u][j]) for j in both], axis=1), gs[u]) for u in each
    ]
    return merged, d_query, d_keys, d_values


def wide(value):
    return value.astype(jnp.float32)


def core_kernel(
    owner, slot_of, enc, w_key, w_value, queries, cotangents,
    att_out, dq_out, enc_out, tab, landed,
    table_even, table_odd, ck, cv, acc, give_even, give_odd, got_even, got_odd,
    own, q_buf, g_buf, att_buf, dq_buf, r1, r2, r3, r4, e1, e2,
    send_sem, recv_sem, back_send, back_recv, own_sem, load_sem,
    enc_sem, w_sem, row_sem, rim_send, rim_recv, block_sem, enc_send, enc_recv, ids, first, second,
):
    x = lax.axis_index("enc")
    right, left = up(x), down(x)
    y, z, c = place()
    me = index_of(y, z, c)
    count = 2 * RING * RING
    ahead, behind = lax.rem(me + 1, count), lax.rem(me + count - 1, count)
    heads = own.shape[0]
    tokens = queries.shape[0]
    spans = tokens // SPAN
    reads = 2 * spans
    group = max(n for n in range(1, 8) if spans % n == 0)
    sibling = index_of(y, z, 1 - c)
    every = slice(None)
    held = (table_even, table_odd)
    give = (give_even, give_odd)
    got = (got_even, got_odd)
    weights = (w_key, w_value)
    body, head_rows, tail_rows = pl.ds(0, tokens), pl.ds(0, SPAN), pl.ds(tokens, SPAN)

    def enc_copy(piece):
        at = (lax.div(piece, 8), lax.rem(lax.div(piece, 2), RING), lax.rem(piece, 2))
        return pltpu.make_async_copy(
            enc.at[:, pl.ds(pl.multiple_of(piece * HD, HD), HD)], got_even.at[at], enc_sem.at[piece]
        )

    def weight_copy(h, kv):
        cols = pl.ds(pl.multiple_of(h * HD, HD), HD)
        return pltpu.make_async_copy(
            weights[kv].at[:, :, :, cols], acc.at[h, :, :, kv], w_sem.at[h, kv]
        )

    def for_pieces(action):
        def one(piece, carry):
            action(enc_copy(piece))
            return carry

        lax.fori_loop(0, enc_sem.shape[0], one, 0)

    for_pieces(lambda copy: copy.start())
    for h in (0, 1):
        for kv in (0, 1):
            weight_copy(h, kv).start()
    greet(y, z, c, (ahead, behind), (right, left))
    ck[reads] = jnp.zeros(ck.shape[1:], jnp.float32)
    cv[reads] = jnp.zeros(cv.shape[1:], jnp.float32)
    for_pieces(lambda copy: copy.wait())

    def row_copies():
        return (
            pltpu.make_async_copy(queries, q_buf.at[body], row_sem.at[0]),
            pltpu.make_async_copy(cotangents, g_buf.at[body], row_sem.at[1]),
        )

    def result_copies():
        return (
            pltpu.make_async_copy(att_buf.at[body], att_out, row_sem.at[2]),
            pltpu.make_async_copy(dq_buf.at[body], dq_out, row_sem.at[3]),
        )

    def rim_move(kind):
        src, dst, to = (
            (queries.at[head_rows], q_buf.at[tail_rows], behind),
            (cotangents.at[head_rows], g_buf.at[tail_rows], behind),
            (att_buf.at[tail_rows], att_buf.at[head_rows], ahead),
            (dq_buf.at[tail_rows], dq_buf.at[head_rows], ahead),
        )[kind]
        return pltpu.make_async_remote_copy(
            src_ref=src,
            dst_ref=dst,
            send_sem=rim_send.at[kind],
            recv_sem=rim_recv.at[kind],
            device_id={"seq": to},
            device_id_type=MESH,
        )

    def by_blocks(refs, blend):
        strip = 256
        line = lax.broadcasted_iota(jnp.int32, (SPAN, strip), 0)

        def one(block, carry):
            for ref in refs:
                for start in range(0, ref.shape[1], strip):
                    blend(ref, block, pl.ds(start, strip), line)
            return carry

        lax.fori_loop(0, spans, one, 0)

    def reads_in():
        def one(s, carry):
            for j in (0, 1):
                ids[2 * s + j] = owner[j, s] * 2 + slot_of[j, s]
            return carry

        lax.fori_loop(0, spans, one, 0)

        def find(n, carry):
            hits = [ids[a] == n for a in range(reads)]
            low_read, high_read = reads, -1
            for a in range(reads):
                high_read = jnp.where(hits[a], a, high_read)
                low_read = jnp.where(hits[reads - 1 - a], reads - 1 - a, low_read)
            first[n] = low_read
            second[n] = jnp.where(high_read > low_read, high_read, reads)
            return carry

        lax.fori_loop(0, 2 * count, find, 0)

    def rows_start():
        for copy in row_copies():
            copy.start()
        rim_move(0).start()
        rim_move(1).start()

    def rows_in():
        for kind, copy in enumerate(row_copies()):
            copy.wait()
            rim_move(kind).wait()

        @pl.when(me == count - 1)
        def _():
            for ref in (q_buf, g_buf):
                ref[tail_rows] = jnp.zeros((SPAN, ref.shape[1]), jnp.bfloat16)

        def blend(ref, block, cols, line):
            at = pl.multiple_of(block * SPAN, SPAN)
            before = wide(ref[pl.ds(at + SPAN - 16, 16), cols])[15:16]
            after = pltpu.roll(wide(ref[pl.ds(at + SPAN, SPAN), cols]), 1, 0)
            ref[pl.ds(at, SPAN), cols] = jnp.where(line == 0, before, after).astype(jnp.bfloat16)

        by_blocks((q_buf, g_buf), blend)

    def tail_out():
        rim_move(2).start()
        rim_move(3).start()

    def rows_out():
        rim_move(2).wait()
        rim_move(3).wait()

        @pl.when(me == 0)
        def _():
            for ref in (att_buf, dq_buf):
                ref[head_rows] = jnp.zeros((SPAN, ref.shape[1]), jnp.bfloat16)

        def blend(ref, block, cols, line):
            at = pl.multiple_of(block * SPAN, SPAN)
            here = pltpu.roll(wide(ref[pl.ds(at, SPAN), cols]), SPAN - 1, 0)
            after = wide(ref[pl.ds(at + SPAN, 16), cols])[0:1]
            ref[pl.ds(at, SPAN), cols] = jnp.where(line == SPAN - 1, after, here).astype(jnp.bfloat16)

        by_blocks((att_buf, dq_buf), blend)
        for copy in result_copies():
            copy.start()

    class Head:
        def __init__(self, h, parity, slots=(0, 1)):
            self.h, self.parity, self.slots = h, parity, slots
            self.lines = pl.ds(slots[0] * NBR_LEN, len(slots) * NBR_LEN)
            self.f, self.g = (y, z) if parity == 0 else (z, y)

        def dev(self, a, b):
            return index_of(a, b, c) if self.parity == 0 else index_of(b, a, c)

        def spot(self, a, b):
            return (self.h, a, b) if self.parity == 0 else (self.h, b, a)

        def block(self, a, *half):
            return tab.at[self.spot(a, self.g) + (c,) + half]

        def band(self, b, *half):
            return tab.at[self.spot(every, b) + (c,) + half]

        def mine(self):
            return pltpu.make_async_copy(own.at[self.h], self.block(self.f), own_sem.at[self.h])

        def load(self):
            return pltpu.make_async_copy(
                tab.at[self.h], held[self.parity], load_sem.at[self.h, 0]
            )

        def fetch(self):
            return pltpu.make_async_copy(
                landed.at[self.h], got[self.parity], load_sem.at[self.h, 1]
            )

        def out_move(self, kind):
            f, g, dev = self.f, self.g, self.dev
            if kind < 4:
                src = (own.at[self.h], own.at[self.h], None, None)[kind]
                dst = (
                    lambda: self.block(f),
                    lambda: self.block(f),
                    lambda: self.block(down(f), 0),
                    lambda: self.block(up(f), 1),
                )[kind]()
                to = dev(up(f), g) if kind % 2 == 0 else dev(down(f), g)
            elif kind < 8:
                dst = (
                    lambda: self.band(g),
                    lambda: self.band(g),
                    lambda: self.band(down(g), slice(0, 1)),
                    lambda: self.band(up(g), slice(1, 2)),
                )[kind - 4]()
                src, to = None, dev(f, up(g)) if kind % 2 == 0 else dev(f, down(g))
            else:
                dst = self.band((g, down(g), up(g), across(g))[kind - 8])
                src, to = None, sibling
            return pltpu.make_async_remote_copy(
                src_ref=dst if src is None else src,
                dst_ref=dst,
                send_sem=send_sem.at[self.h, kind],
                recv_sem=recv_sem.at[self.h, kind],
                device_id={"seq": to},
                device_id_type=MESH,
            )

        def back_move(self, kind):
            f, g, dev, h, spot = self.f, self.g, self.dev, self.h, self.spot
            here = self.lines
            src, dst, to = (
                lambda: (give[self.parity], landed.at[h], sibling),
                lambda: (acc.at[spot(every, across(g)) + (0, here)], r1.at[h, 0, :, here], dev(f, up(g))),
                lambda: (acc.at[spot(every, across(g)) + (1, here)], r1.at[h, 1, :, here], dev(f, down(g))),
                lambda: (acc.at[spot(every, up(g)) + (every, here)], r2.at[h, 0, :, :, here], dev(f, up(g))),
                lambda: (acc.at[spot(every, down(g)) + (every, here)], r2.at[h, 1, :, :, here], dev(f, down(g))),
                lambda: (acc.at[spot(across(f), g) + (0, here)], r3.at[h, 0, here], dev(up(f), g)),
                lambda: (acc.at[spot(across(f), g) + (1, here)], r3.at[h, 1, here], dev(down(f), g)),
                lambda: (acc.at[spot(up(f), g) + (every, here)], r4.at[h, 0, :, here], dev(up(f), g)),
                lambda: (acc.at[spot(down(f), g) + (every, here)], r4.at[h, 1, :, here], dev(down(f), g)),
            )[kind]()
            place_of = 0 if kind == 0 else self.slots[0] * 8 + kind
            return pltpu.make_async_remote_copy(
                src_ref=src,
                dst_ref=dst,
                send_sem=back_send.at[h, place_of],
                recv_sem=back_recv.at[h, place_of],
                device_id={"seq": to},
                device_id_type=MESH,
            )

    def project(t):
        for kv in (0, 1):
            weight_copy(t.h, kv).wait()

        @pl.when(t.h + 2 < heads)
        def _():
            for kv in (0, 1):
                weight_copy(t.h + 2, kv).start()

        deep = [(a, b) for a in range(RING) for b in range(RING)]

        def one(s, carry):
            lines = pl.ds(pl.multiple_of(s * NBR_LEN, NBR_LEN), NBR_LEN)
            left = jnp.concatenate([got_even[a, b, k, lines] for a, b in deep for k in (0, 1)], axis=1)
            right = jnp.concatenate(
                [jnp.concatenate([acc[t.h, a, b, kv] for kv in (0, 1)], axis=1) for a, b in deep], axis=0
            )
            rows = jnp.dot(left, right, preferred_element_type=jnp.float32).astype(jnp.bfloat16)
            for kv in (0, 1):
                own[t.h, kv, s] = rows[:, kv * HD : (kv + 1) * HD]
            return carry

        lax.fori_loop(0, 2, one, 0)

    def own_out(t):
        project(t)
        t.mine().start()
        t.out_move(0).start()
        t.out_move(1).start()

    def block_on(t):
        t.out_move(0).wait_recv()
        t.out_move(2).start()
        t.out_move(1).wait_recv()
        t.out_move(3).start()

    def band_out(t):
        t.mine().wait()
        t.out_move(2).wait_recv()
        t.out_move(3).wait_recv()
        t.out_move(4).start()
        t.out_move(5).start()
        t.out_move(8).start()

    def band_on(t):
        t.out_move(4).wait_recv()
        t.out_move(6).start()
        t.out_move(9).start()
        t.out_move(5).wait_recv()
        t.out_move(7).start()
        t.out_move(10).start()

    def band_last(t):
        t.out_move(6).wait_recv()
        t.out_move(7).wait_recv()
        t.out_move(11).start()

    def table_in(t):
        for kind in (8, 9, 10, 11):
            t.out_move(kind).wait_recv()
        t.load().start()
        for kind in range(12):
            t.out_move(kind).wait_send()

    def sibling_in(t):
        t.back_move(0).wait_recv()
        t.fetch().start()
        t.back_move(0).wait_send()

    def attend(t):
        table, cols = held[t.parity], pl.ds(pl.multiple_of(t.h * HD, HD), HD)
        t.load().wait()

        def pick(n, kv):
            return table[lax.div(n, 16), lax.rem(lax.div(n, 4), RING), lax.rem(lax.div(n, 2), 2), kv, lax.rem(n, 2)]

        def some(i, carry):
            spots = [i * group + u for u in range(group)]
            rows = [pl.ds(pl.multiple_of(s * SPAN, SPAN), SPAN) for s in spots]
            qs, gs = [q_buf[r, cols] for r in rows], [g_buf[r, cols] for r in rows]
            picks = [[ids[2 * s + j] for j in (0, 1)] for s in spots]
            keys = [[pick(n, 0) for n in two] for two in picks]
            values = [[pick(n, 1) for n in two] for two in picks]
            merged, d_query, d_keys, d_values = spans_math(qs, gs, keys, values)
            for u, s in enumerate(spots):
                put = pl.ds(pl.multiple_of((s + 1) * SPAN, SPAN), SPAN)
                att_buf[put, cols] = merged[u].astype(jnp.bfloat16)
                dq_buf[put, cols] = d_query[u].astype(jnp.bfloat16)
                for j in (0, 1):
                    ck[2 * s + j] = d_keys[u][j * NBR_LEN : (j + 1) * NBR_LEN]
                    cv[2 * s + j] = d_values[u][j * NBR_LEN : (j + 1) * NBR_LEN]
            return carry

        lax.fori_loop(0, spans // group, some, 0)

        def fold(chip, carry):
            a, b = lax.div(chip, RING), lax.rem(chip, RING)
            for s in (0, 1):
                for core, keep in ((c, True), (1 - c, False)):
                    n = (2 * chip + core) * 2 + s
                    one, two = first[n], second[n]
                    for kv, part in ((0, ck), (1, cv)):
                        total = (part[one] + part[two]).astype(jnp.bfloat16)
                        lines = pl.ds(s * NBR_LEN, NBR_LEN)
                        if keep:
                            acc[t.h, a, b, kv, lines] = total
                        else:
                            give[t.parity][a, b, kv, lines] = total
            return carry

        lax.fori_loop(0, RING * RING, fold, 0)
        t.back_move(0).start()

    def sum_sibling(t):
        t.fetch().wait()

        def add(i, carry):
            a, b = lax.div(i, RING), lax.rem(i, RING)
            for kv in (0, 1):
                acc[t.h, a, b, kv] = acc[t.h, a, b, kv] + got[t.parity][a, b, kv]
            return carry

        lax.fori_loop(0, RING * RING, add, 0)

    def halves_out(t):
        t.back_move(1).start()
        t.back_move(2).start()

    def sum_band_half(t):
        for half, (kind, toward) in enumerate(((1, up(t.g)), (2, down(t.g)))):
            t.back_move(kind).wait_recv()

            def add(a, carry):
                at = t.spot(a, toward) + (half, t.lines)
                acc[at] = acc[at] + r1[t.h, half, a, t.lines]
                return carry

            lax.fori_loop(0, RING, add, 0)
            t.back_move(3 + half).start()

    def sum_band(t):
        t.back_move(3).wait_recv()
        t.back_move(4).wait_recv()

        def add(a, carry):
            for kv in (0, 1):
                at = t.spot(a, t.g) + (kv, t.lines)
                total = wide(acc[at]) + wide(r2[t.h, 0, a, kv, t.lines]) + wide(r2[t.h, 1, a, kv, t.lines])
                acc[at] = total.astype(jnp.bfloat16)
            return carry

        lax.fori_loop(0, RING, add, 0)
        t.back_move(5).start()
        t.back_move(6).start()

    def sum_block_half(t):
        for half, (kind, toward) in enumerate(((5, up(t.f)), (6, down(t.f)))):
            t.back_move(kind).wait_recv()
            at = t.spot(toward, t.g) + (half, t.lines)
            acc[at] = acc[at] + r3[t.h, half, t.lines]
            t.back_move(7 + half).start()

    def sum_block(t):
        t.back_move(7).wait_recv()
        t.back_move(8).wait_recv()
        for kv in (0, 1):
            for slot in t.slots:
                lines = pl.ds(slot * NBR_LEN, NBR_LEN)
                total = wide(acc[t.spot(t.f, t.g) + (kv, lines)])
                total = total + wide(r4[t.h, 0, kv, lines]) + wide(r4[t.h, 1, kv, lines])
                own[t.h, kv, slot] = total.astype(jnp.bfloat16)
        for kind in range(1, 9):
            t.back_move(kind).wait_send()

    pairs = heads // 2
    split = (pairs - 2, pairs - 1)
    sums = (ck, cv)

    def pair_copies(pair, action):
        for n in (0, 1):
            cols = pl.ds((2 * pair + n) * HD, HD)
            for core in (0, 1):
                for kv in (0, 1):
                    action(
                        pltpu.make_async_copy(
                            weights[kv].at[:, :, pl.ds(core * HD, HD), cols],
                            held[pair % 2].at[:, :, core, kv, n],
                            block_sem.at[pair, 4 * n + 2 * core + kv],
                        )
                    )

    def pair_start(*which):
        for pair in which:
            pair_copies(pair, lambda copy: copy.start())

    deep = [(kv, n) for kv in (0, 1) for n in (0, 1)]

    def rows_of(pair, slot):
        return jnp.concatenate([own[2 * pair + n, kv, slot] for kv, n in deep], axis=1)

    def weights_of(pair, t, a):
        table = held[pair % 2]
        return jnp.concatenate(
            [jnp.concatenate([table[t, a, core, kv, n] for kv, n in deep], axis=1) for core in (0, 1)],
            axis=0,
        )

    def gather_pair(pair):
        pair_copies(pair, lambda copy: copy.wait())
        lhs = jnp.concatenate([rows_of(pair, slot) for slot in (0, 1)], axis=0)

        def one(m, carry):
            t, a = lax.div(m, RING), lax.rem(m, RING)
            part = dot_t(lhs, weights_of(pair, t, a))
            for slot in (0, 1):
                for core in (0, 1):
                    at = 8 * t + 2 * a + core
                    piece = part[slot * NBR_LEN : (slot + 1) * NBR_LEN, core * HD : (core + 1) * HD]
                    sums[slot][at] = piece if pair == 0 else sums[slot][at] + piece
            return carry

        lax.fori_loop(0, RING * RING, one, 0)

    def product(slot, t, put):
        lhs = [rows_of(pair, slot) for pair in split]

        def one(a, carry):
            part = sum(dot_t(rows, weights_of(pair, t, a)) for rows, pair in zip(lhs, split))
            for core in (0, 1):
                at = 8 * t + 2 * a + core
                put(a, core, at, sums[slot][at] + part[:, core * HD : (core + 1) * HD])
            return carry

        lax.fori_loop(0, RING, one, 0)

    half = NBR_LEN // 2
    low, high = pl.ds(0, half), pl.ds(half, half)

    def enc_move(slot, kind):
        src, dst, to = (
            lambda: (give[slot].at[0, :, :, low], e1.at[slot, 0], right),
            lambda: (give[slot].at[1, :, :, low], e1.at[slot, 1], left),
            lambda: (give[slot].at[2, :, :, low], e2.at[slot, 0, :, :, low], right),
            lambda: (give[slot].at[3, :, :, high], e2.at[slot, 1, :, :, high], left),
            lambda: (give[slot].at[2, :, :, high], e2.at[slot, 0, :, :, high], right),
            lambda: (give[slot].at[3, :, :, low], e2.at[slot, 1, :, :, low], left),
        )[kind]()
        return pltpu.make_async_remote_copy(
            src_ref=src,
            dst_ref=dst,
            send_sem=enc_send.at[slot, kind],
            recv_sem=enc_recv.at[slot, kind],
            device_id={"enc": to},
            device_id_type=MESH,
        )

    def by_columns(action):
        def one(a, carry):
            for core in (0, 1):
                action(a, core)
            return carry

        lax.fori_loop(0, RING, one, 0)

    def enc_far(slot):
        send, sum_of = give[slot], sums[slot]

        def put_far(a, core, at, total):
            send[0, a, core, low] = total[:half].astype(jnp.bfloat16)
            send[1, a, core, low] = total[half:].astype(jnp.bfloat16)

        def put_right(a, core, at, total):
            sum_of[at] = total
            send[2, a, core, high] = total[half:].astype(jnp.bfloat16)

        def put_left(a, core, at, total):
            sum_of[at] = total
            send[3, a, core, low] = total[:half].astype(jnp.bfloat16)

        def put_mine(a, core, at, total):
            sum_of[at] = total

        if slot == 0:
            for pair in split:
                pair_copies(pair, lambda copy: copy.wait())
        product(slot, across(x), put_far)
        enc_move(slot, 0).start()
        enc_move(slot, 1).start()
        product(slot, right, put_right)
        enc_move(slot, 4).start()
        product(slot, left, put_left)
        enc_move(slot, 5).start()
        product(slot, x, put_mine)

    def enc_near(slot):
        send, sum_of = give[slot], sums[slot]

        def add_right(a, core):
            total = sum_of[8 * right + 2 * a + core, low] + wide(e1[slot, 0, a, core])
            send[2, a, core, low] = total.astype(jnp.bfloat16)

        def add_left(a, core):
            total = sum_of[8 * left + 2 * a + core, high] + wide(e1[slot, 1, a, core])
            send[3, a, core, high] = total.astype(jnp.bfloat16)

        enc_move(slot, 0).wait_recv()
        by_columns(add_right)
        enc_move(slot, 2).start()
        enc_move(slot, 1).wait_recv()
        by_columns(add_left)
        enc_move(slot, 3).start()

    def enc_done(slot):
        for kind in (4, 5, 2, 3):
            enc_move(slot, kind).wait_recv()

        for a in range(RING):
            for core in (0, 1):
                total = sums[slot][8 * x + 2 * a + core] + wide(e2[slot, 0, a, core]) + wide(e2[slot, 1, a, core])
                n = 2 * a + core
                enc_out[slot * NBR_LEN : (slot + 1) * NBR_LEN, n * HD : (n + 1) * HD] = total.astype(
                    jnp.bfloat16
                )
        for kind in range(6):
            enc_move(slot, kind).wait_send()

    there = (
        (0, own_out),
        (1, block_on),
        (2, band_out),
        (3, band_on),
        (4, band_last),
        (4, table_in),
    )
    back_small = ((9, sum_block), (8, sum_block_half))
    back_large = ((7, sum_band), (6, sum_band_half))
    turn = ((5, sibling_in), (4, attend), (5, sum_sibling))
    leave = ((5, halves_out),)
    between = {
        12: (lambda: enc_far(0),),
        13: (lambda: enc_near(0),),
        14: (lambda: enc_far(1),),
        15: (lambda: enc_near(1),),
    }
    after = {
        0: (rows_start,),
        2: (reads_in,),
        3: (rows_in,),
        7: (tail_out,),
        8: (rows_out, lambda: pair_start(0, 1)),
        9: (lambda: gather_pair(0), lambda: pair_start(2)),
        10: (lambda: gather_pair(1), lambda: pair_start(3)),
        15: (lambda: enc_done(0),),
        16: (lambda: enc_done(1),),
    }

    def at_times(i, table):
        for when, acts in table.items():

            @pl.when(i == when)
            def _(acts=acts):
                for act in acts:
                    act()

    def run(i, stages, parts):
        for lag, stage in stages:
            for start, stop, skip, slots in parts:

                @pl.when((i >= start + lag) & (i < stop + lag))
                def _(lag=lag, stage=stage, skip=skip, slots=slots):
                    for parity in (0, 1):
                        stage(Head(2 * (i - lag - skip) + parity, parity, slots))

    both = ((0, pairs, 0, (0, 1)),)
    apart = (
        (0, pairs - 2, 0, (0, 1)),
        (pairs - 2, pairs, 0, (0,)),
        (pairs, pairs + 2, 2, (1,)),
    )

    def step(i, carry):
        run(i, there, both)
        run(i, back_small, apart)
        at_times(i, between)
        run(i, back_large, apart)
        run(i, turn, both)
        run(i, leave, apart)
        at_times(i, after)
        return carry

    lax.fori_loop(0, max(after) + 1, step, 0)
    for copy in result_copies():
        copy.wait()


def core(owner, slot_of, enc, w_key, w_value, queries, cotangents):
    rows, width = queries.shape
    depth = enc.shape[1]
    heads, reads = width // HD, 2 * owner.shape[1]
    rest = (2, 2, NBR_LEN, HD)
    tail = (2, 2 * NBR_LEN, HD)
    bf16, f32 = jnp.bfloat16, jnp.float32
    in_vmem = pl.BlockSpec(memory_space=pltpu.VMEM)
    in_smem = pl.BlockSpec(memory_space=pltpu.SMEM)
    anywhere = pl.BlockSpec(memory_space=pl.ANY)
    band = (RING, RING) + tail
    dma = pltpu.SemaphoreType.DMA
    folded = (RING, RING, depth // (RING * RING), width)
    return pl.pallas_call(
        core_kernel,
        in_specs=[in_smem] * 2 + [anywhere] * 5,
        out_specs=[anywhere, anywhere, in_vmem, anywhere, anywhere],
        out_shape=[
            jax.ShapeDtypeStruct((rows, width), bf16),
            jax.ShapeDtypeStruct((rows, width), bf16),
            jax.ShapeDtypeStruct((tail[1], depth // RING), bf16),
            jax.ShapeDtypeStruct((heads, RING, RING, 2) + rest, bf16),
            jax.ShapeDtypeStruct((heads,) + band, bf16),
        ],
        scratch_shapes=[
            pltpu.VMEM((RING, RING, 2) + rest, bf16),
            pltpu.VMEM((RING, RING, 2) + rest, bf16),
            pltpu.VMEM((max(reads + 1, depth // HD), NBR_LEN, HD), f32),
            pltpu.VMEM((max(reads + 1, depth // HD), NBR_LEN, HD), f32),
            pltpu.VMEM((heads,) + band, bf16),
            pltpu.VMEM(band, bf16),
            pltpu.VMEM(band, bf16),
            pltpu.VMEM(band, bf16),
            pltpu.VMEM(band, bf16),
            pltpu.VMEM((heads,) + rest, bf16),
            pltpu.VMEM((rows + SPAN, width), bf16),
            pltpu.VMEM((rows + SPAN, width), bf16),
            pltpu.VMEM((rows + SPAN, width), bf16),
            pltpu.VMEM((rows + SPAN, width), bf16),
            pltpu.VMEM((heads, 2, RING) + tail[1:], bf16),
            pltpu.VMEM((heads, 2, RING) + tail, bf16),
            pltpu.VMEM((heads, 2) + tail[1:], bf16),
            pltpu.VMEM((heads, 2) + tail, bf16),
            pltpu.VMEM((2, 2, RING, 2, NBR_LEN // 2, HD), bf16),
            pltpu.VMEM((2, 2, RING, 2, NBR_LEN, HD), bf16),
            dma((heads, 12)),
            dma((heads, 12)),
            dma((heads, 17)),
            dma((heads, 17)),
            dma((heads,)),
            dma((heads, 2)),
            dma((depth // HD,)),
            dma((heads, 2)),
            dma((4,)),
            dma((4,)),
            dma((4,)),
            dma((heads // 2, 8)),
            dma((2, 6)),
            dma((2, 6)),
            pltpu.SMEM((reads,), jnp.int32),
            pltpu.SMEM((4 * RING * RING,), jnp.int32),
            pltpu.SMEM((4 * RING * RING,), jnp.int32),
        ],
        compiler_params=pltpu.CompilerParams(
            collective_id=0, has_side_effects=True, vmem_limit_bytes=64 * MIB
        ),
        name="core",
    )(owner, slot_of, enc, w_key.reshape(folded), w_value.reshape(folded), queries, cotangents)


def per_device(queries, d_attended, encodings, w_key, w_value, neighbour_owner, neighbour_slot):
    feat_width = queries.shape[1]
    owned = encodings.shape[0]
    enc_flat = encodings.reshape(owned * NBR_LEN, encodings.shape[2])
    attended, d_queries, d_encodings, _, _ = core(
        neighbour_owner.T, neighbour_slot.T, enc_flat, w_key, w_value, queries, d_attended
    )
    return (attended, d_queries, d_encodings.reshape(owned, NBR_LEN, feat_width))


def solution(mesh):
    return jax.shard_map(
        per_device,
        mesh=mesh,
        in_specs=(
            P("seq", "enc"),
            P("seq", "enc"),
            P("seq", None, None),
            P(None, "enc"),
            P(None, "enc"),
            P("seq", None),
            P("seq", None),
        ),
        out_specs=(P("seq", "enc"), P("seq", "enc"), P("seq", None, "enc")),
        check_vma=False,
    )
```

```python
import math

import jax
import jax.numpy as jnp
from jax import lax
from jax.experimental import pallas as pl
from jax.experimental.pallas import tpu as pltpu
from jax.sharding import PartitionSpec as P

HD = 128
SPAN = 64
NBR_LEN = 128
MESH = pl.DeviceIdType.MESH
SCALE = 1.0 / math.sqrt(HD)
RING = 4
MIB = 1024 * 1024


def place():
    s = lax.axis_index("seq")
    return lax.div(s, 8), lax.rem(lax.div(s, 2), RING), lax.rem(s, 2)


def up(i):
    return lax.rem(i + 1, RING)


def down(i):
    return lax.rem(i + RING - 1, RING)


def across(i):
    return lax.rem(i + 2, RING)


def index_of(y, z, c):
    return y * 8 + z * 2 + c


def greet(y, z, c, seq_more, enc_more):
    barrier = pltpu.get_barrier_semaphore()
    near = (
        index_of(up(y), z, c),
        index_of(down(y), z, c),
        index_of(y, up(z), c),
        index_of(y, down(z), c),
        index_of(y, z, 1 - c),
    )
    partners = [{"seq": other} for other in near + seq_more] + [{"enc": other} for other in enc_more]
    for partner in partners:
        pl.semaphore_signal(barrier, inc=1, device_id=partner, device_id_type=MESH)
    pl.semaphore_wait(barrier, len(partners))


def dot_t(a, b):
    return lax.dot_general(a, b, (((1,), (1,)), ((), ())), preferred_element_type=jnp.float32)


def t_dot(a, b):
    return lax.dot_general(a, b, (((0,), (0,)), ((), ())), preferred_element_type=jnp.float32)


def spans_math(qs, gs, keys, values):
    each, both = range(len(qs)), (0, 1)

    def pairs(rows, tables):
        joined = [dot_t(rows[u], jnp.concatenate(tables[u], axis=0)) for u in each]
        return [[x[:, :NBR_LEN], x[:, NBR_LEN:]] for x in joined]

    def narrow(x):
        return x.astype(jnp.bfloat16)

    s = pairs(qs, keys)
    grad = pairs(gs, values)
    top = [[jnp.max(s[u][j], axis=1, keepdims=True) for j in both] for u in each]
    e = [[jnp.exp((s[u][j] - top[u][j]) * SCALE) for j in both] for u in each]
    total = [[jnp.sum(e[u][j], axis=1, keepdims=True) for j in both] for u in each]
    p = [[narrow(e[u][j] * (1.0 / total[u][j])) for j in both] for u in each]
    out = [
        [wide(narrow(jnp.dot(p[u][j], values[u][j], preferred_element_type=jnp.float32))) for j in both]
        for u in each
    ]
    peak = [jnp.maximum(top[u][0], top[u][1]) for u in each]
    lift = [[jnp.exp((top[u][j] - peak[u]) * SCALE) for j in both] for u in each]
    inverse = [1.0 / (total[u][0] * lift[u][0] + total[u][1] * lift[u][1]) for u in each]
    weight = [[lift[u][j] * inverse[u] for j in both] for u in each]
    merged = [
        total[u][0] * weight[u][0] * out[u][0] + total[u][1] * weight[u][1] * out[u][1] for u in each
    ]
    delta = [jnp.sum(wide(gs[u]) * merged[u], axis=1, keepdims=True) for u in each]
    full = [[e[u][j] * weight[u][j] for j in both] for u in each]
    ds = [
        [narrow(full[u][j] * ((grad[u][j] - delta[u]) * SCALE)) for j in both] for u in each
    ]
    parts = [
        [wide(narrow(jnp.dot(ds[u][j], keys[u][j], preferred_element_type=jnp.float32))) for j in both]
        for u in each
    ]
    d_query = [parts[u][0] + parts[u][1] for u in each]
    d_keys = [t_dot(jnp.concatenate(ds[u], axis=1), qs[u]) for u in each]
    d_values = [
        t_dot(jnp.concatenate([narrow(full[u][j]) for j in both], axis=1), gs[u]) for u in each
    ]
    return merged, d_query, d_keys, d_values


def wide(value):
    return value.astype(jnp.float32)


def core_kernel(
    owner, slot_of, enc, w_key, w_value, queries, cotangents,
    att_out, dq_out, enc_out, tab, landed,
    table_even, table_odd, ck, cv, acc, give_even, give_odd, got_even, got_odd,
    own, q_buf, g_buf, att_buf, dq_buf, r1, r2, r3, r4, e1, e2,
    send_sem, recv_sem, back_send, back_recv, own_sem, load_sem,
    enc_sem, w_sem, row_sem, rim_send, rim_recv, block_sem, enc_send, enc_recv, ids, first, second,
):
    x = lax.axis_index("enc")
    right, left = up(x), down(x)
    y, z, c = place()
    me = index_of(y, z, c)
    count = 2 * RING * RING
    ahead, behind = lax.rem(me + 1, count), lax.rem(me + count - 1, count)
    heads = own.shape[0]
    tokens = queries.shape[0]
    spans = tokens // SPAN
    reads = 2 * spans
    group = max(n for n in range(1, 8) if spans % n == 0)
    sibling = index_of(y, z, 1 - c)
    every = slice(None)
    held = (table_even, table_odd)
    give = (give_even, give_odd)
    got = (got_even, got_odd)
    weights = (w_key, w_value)
    body, head_rows, tail_rows = pl.ds(0, tokens), pl.ds(0, SPAN), pl.ds(tokens, SPAN)

    def enc_copy(piece):
        at = (lax.div(piece, 8), lax.rem(lax.div(piece, 2), RING), lax.rem(piece, 2))
        return pltpu.make_async_copy(
            enc.at[:, pl.ds(pl.multiple_of(piece * HD, HD), HD)], got_even.at[at], enc_sem.at[piece]
        )

    def weight_copy(h, kv):
        cols = pl.ds(pl.multiple_of(h * HD, HD), HD)
        return pltpu.make_async_copy(
            weights[kv].at[:, :, :, cols], acc.at[h, :, :, kv], w_sem.at[h, kv]
        )

    def for_pieces(action):
        def one(piece, carry):
            action(enc_copy(piece))
            return carry

        lax.fori_loop(0, enc_sem.shape[0], one, 0)

    for_pieces(lambda copy: copy.start())
    for h in (0, 1):
        for kv in (0, 1):
            weight_copy(h, kv).start()
    greet(y, z, c, (ahead, behind), (right, left))
    ck[reads] = jnp.zeros(ck.shape[1:], jnp.float32)
    cv[reads] = jnp.zeros(cv.shape[1:], jnp.float32)
    for_pieces(lambda copy: copy.wait())

    def row_copies():
        return (
            pltpu.make_async_copy(queries, q_buf.at[body], row_sem.at[0]),
            pltpu.make_async_copy(cotangents, g_buf.at[body], row_sem.at[1]),
        )

    def result_copies():
        return (
            pltpu.make_async_copy(att_buf.at[body], att_out, row_sem.at[2]),
            pltpu.make_async_copy(dq_buf.at[body], dq_out, row_sem.at[3]),
        )

    def rim_move(kind):
        src, dst, to = (
            (queries.at[head_rows], q_buf.at[tail_rows], behind),
            (cotangents.at[head_rows], g_buf.at[tail_rows], behind),
            (att_buf.at[tail_rows], att_buf.at[head_rows], ahead),
            (dq_buf.at[tail_rows], dq_buf.at[head_rows], ahead),
        )[kind]
        return pltpu.make_async_remote_copy(
            src_ref=src,
            dst_ref=dst,
            send_sem=rim_send.at[kind],
            recv_sem=rim_recv.at[kind],
            device_id={"seq": to},
            device_id_type=MESH,
        )

    def by_blocks(refs, blend):
        strip = 256
        line = lax.broadcasted_iota(jnp.int32, (SPAN, strip), 0)

        def one(block, carry):
            for ref in refs:
                for start in range(0, ref.shape[1], strip):
                    blend(ref, block, pl.ds(start, strip), line)
            return carry

        lax.fori_loop(0, spans, one, 0)

    def reads_in():
        def one(s, carry):
            for j in (0, 1):
                ids[2 * s + j] = owner[j, s] * 2 + slot_of[j, s]
            return carry

        lax.fori_loop(0, spans, one, 0)

        def find(n, carry):
            hits = [ids[a] == n for a in range(reads)]
            low_read, high_read = reads, -1
            for a in range(reads):
                high_read = jnp.where(hits[a], a, high_read)
                low_read = jnp.where(hits[reads - 1 - a], reads - 1 - a, low_read)
            first[n] = low_read
            second[n] = jnp.where(high_read > low_read, high_read, reads)
            return carry

        lax.fori_loop(0, 2 * count, find, 0)

    def rows_start():
        for copy in row_copies():
            copy.start()
        rim_move(0).start()
        rim_move(1).start()

    def rows_in():
        for kind, copy in enumerate(row_copies()):
            copy.wait()
            rim_move(kind).wait()

        @pl.when(me == count - 1)
        def _():
            for ref in (q_buf, g_buf):
                ref[tail_rows] = jnp.zeros((SPAN, ref.shape[1]), jnp.bfloat16)

        def blend(ref, block, cols, line):
            at = pl.multiple_of(block * SPAN, SPAN)
            before = wide(ref[pl.ds(at + SPAN - 16, 16), cols])[15:16]
            after = pltpu.roll(wide(ref[pl.ds(at + SPAN, SPAN), cols]), 1, 0)
            ref[pl.ds(at, SPAN), cols] = jnp.where(line == 0, before, after).astype(jnp.bfloat16)

        by_blocks((q_buf, g_buf), blend)

    def tail_out():
        rim_move(2).start()
        rim_move(3).start()

    def rows_out():
        rim_move(2).wait()
        rim_move(3).wait()

        @pl.when(me == 0)
        def _():
            for ref in (att_buf, dq_buf):
                ref[head_rows] = jnp.zeros((SPAN, ref.shape[1]), jnp.bfloat16)

        def blend(ref, block, cols, line):
            at = pl.multiple_of(block * SPAN, SPAN)
            here = pltpu.roll(wide(ref[pl.ds(at, SPAN), cols]), SPAN - 1, 0)
            after = wide(ref[pl.ds(at + SPAN, 16), cols])[0:1]
            ref[pl.ds(at, SPAN), cols] = jnp.where(line == SPAN - 1, after, here).astype(jnp.bfloat16)

        by_blocks((att_buf, dq_buf), blend)
        for copy in result_copies():
            copy.start()

    class Head:
        def __init__(self, h, parity, slots=(0, 1)):
            self.h, self.parity, self.slots = h, parity, slots
            self.lines = pl.ds(slots[0] * NBR_LEN, len(slots) * NBR_LEN)
            self.f, self.g = (y, z) if parity == 0 else (z, y)

        def dev(self, a, b):
            return index_of(a, b, c) if self.parity == 0 else index_of(b, a, c)

        def spot(self, a, b):
            return (self.h, a, b) if self.parity == 0 else (self.h, b, a)

        def block(self, a, *half):
            return tab.at[self.spot(a, self.g) + (c,) + half]

        def band(self, b, *half):
            return tab.at[self.spot(every, b) + (c,) + half]

        def mine(self):
            return pltpu.make_async_copy(own.at[self.h], self.block(self.f), own_sem.at[self.h])

        def load(self):
            return pltpu.make_async_copy(
                tab.at[self.h], held[self.parity], load_sem.at[self.h, 0]
            )

        def fetch(self):
            return pltpu.make_async_copy(
                landed.at[self.h], got[self.parity], load_sem.at[self.h, 1]
            )

        def out_move(self, kind):
            f, g, dev = self.f, self.g, self.dev
            if kind < 4:
                src = (own.at[self.h], own.at[self.h], None, None)[kind]
                dst = (
                    lambda: self.block(f),
                    lambda: self.block(f),
                    lambda: self.block(down(f), 0),
                    lambda: self.block(up(f), 1),
                )[kind]()
                to = dev(up(f), g) if kind % 2 == 0 else dev(down(f), g)
            elif kind < 8:
                dst = (
                    lambda: self.band(g),
                    lambda: self.band(g),
                    lambda: self.band(down(g), slice(0, 1)),
                    lambda: self.band(up(g), slice(1, 2)),
                )[kind - 4]()
                src, to = None, dev(f, up(g)) if kind % 2 == 0 else dev(f, down(g))
            else:
                dst = self.band((g, down(g), up(g), across(g))[kind - 8])
                src, to = None, sibling
            return pltpu.make_async_remote_copy(
                src_ref=dst if src is None else src,
                dst_ref=dst,
                send_sem=send_sem.at[self.h, kind],
                recv_sem=recv_sem.at[self.h, kind],
                device_id={"seq": to},
                device_id_type=MESH,
            )

        def back_move(self, kind):
            f, g, dev, h, spot = self.f, self.g, self.dev, self.h, self.spot
            here = self.lines
            src, dst, to = (
                lambda: (give[self.parity], landed.at[h], sibling),
                lambda: (acc.at[spot(every, across(g)) + (0, here)], r1.at[h, 0, :, here], dev(f, up(g))),
                lambda: (acc.at[spot(every, across(g)) + (1, here)], r1.at[h, 1, :, here], dev(f, down(g))),
                lambda: (acc.at[spot(every, up(g)) + (every, here)], r2.at[h, 0, :, :, here], dev(f, up(g))),
                lambda: (acc.at[spot(every, down(g)) + (every, here)], r2.at[h, 1, :, :, here], dev(f, down(g))),
                lambda: (acc.at[spot(across(f), g) + (0, here)], r3.at[h, 0, here], dev(up(f), g)),
                lambda: (acc.at[spot(across(f), g) + (1, here)], r3.at[h, 1, here], dev(down(f), g)),
                lambda: (acc.at[spot(up(f), g) + (every, here)], r4.at[h, 0, :, here], dev(up(f), g)),
                lambda: (acc.at[spot(down(f), g) + (every, here)], r4.at[h, 1, :, here], dev(down(f), g)),
            )[kind]()
            place_of = 0 if kind == 0 else self.slots[0] * 8 + kind
            return pltpu.make_async_remote_copy(
                src_ref=src,
                dst_ref=dst,
                send_sem=back_send.at[h, place_of],
                recv_sem=back_recv.at[h, place_of],
                device_id={"seq": to},
                device_id_type=MESH,
            )

    def project(t):
        for kv in (0, 1):
            weight_copy(t.h, kv).wait()

        @pl.when(t.h + 2 < heads)
        def _():
            for kv in (0, 1):
                weight_copy(t.h + 2, kv).start()

        deep = [(a, b) for a in range(RING) for b in range(RING)]

        def one(s, carry):
            lines = pl.ds(pl.multiple_of(s * NBR_LEN, NBR_LEN), NBR_LEN)
            left = jnp.concatenate([got_even[a, b, k, lines] for a, b in deep for k in (0, 1)], axis=1)
            right = jnp.concatenate(
                [jnp.concatenate([acc[t.h, a, b, kv] for kv in (0, 1)], axis=1) for a, b in deep], axis=0
            )
            rows = jnp.dot(left, right, preferred_element_type=jnp.float32).astype(jnp.bfloat16)
            for kv in (0, 1):
                own[t.h, kv, s] = rows[:, kv * HD : (kv + 1) * HD]
            return carry

        lax.fori_loop(0, 2, one, 0)

    def own_out(t):
        project(t)
        t.mine().start()
        t.out_move(0).start()
        t.out_move(1).start()

    def block_on(t):
        t.out_move(0).wait_recv()
        t.out_move(2).start()
        t.out_move(1).wait_recv()
        t.out_move(3).start()

    def band_out(t):
        t.mine().wait()
        t.out_move(2).wait_recv()
        t.out_move(3).wait_recv()
        t.out_move(4).start()
        t.out_move(5).start()
        t.out_move(8).start()

    def band_on(t):
        t.out_move(4).wait_recv()
        t.out_move(6).start()
        t.out_move(9).start()
        t.out_move(5).wait_recv()
        t.out_move(7).start()
        t.out_move(10).start()

    def band_last(t):
        t.out_move(6).wait_recv()
        t.out_move(7).wait_recv()
        t.out_move(11).start()

    def table_in(t):
        for kind in (8, 9, 10, 11):
            t.out_move(kind).wait_recv()
        t.load().start()
        for kind in range(12):
            t.out_move(kind).wait_send()

    def sibling_in(t):
        t.back_move(0).wait_recv()
        t.fetch().start()
        t.back_move(0).wait_send()

    def attend(t):
        table, cols = held[t.parity], pl.ds(pl.multiple_of(t.h * HD, HD), HD)
        t.load().wait()

        def pick(n, kv):
            return table[lax.div(n, 16), lax.rem(lax.div(n, 4), RING), lax.rem(lax.div(n, 2), 2), kv, lax.rem(n, 2)]

        def some(i, carry):
            spots = [i * group + u for u in range(group)]
            rows = [pl.ds(pl.multiple_of(s * SPAN, SPAN), SPAN) for s in spots]
            qs, gs = [q_buf[r, cols] for r in rows], [g_buf[r, cols] for r in rows]
            picks = [[ids[2 * s + j] for j in (0, 1)] for s in spots]
            keys = [[pick(n, 0) for n in two] for two in picks]
            values = [[pick(n, 1) for n in two] for two in picks]
            merged, d_query, d_keys, d_values = spans_math(qs, gs, keys, values)
            for u, s in enumerate(spots):
                put = pl.ds(pl.multiple_of((s + 1) * SPAN, SPAN), SPAN)
                att_buf[put, cols] = merged[u].astype(jnp.bfloat16)
                dq_buf[put, cols] = d_query[u].astype(jnp.bfloat16)
                for j in (0, 1):
                    ck[2 * s + j] = d_keys[u][j * NBR_LEN : (j + 1) * NBR_LEN]
                    cv[2 * s + j] = d_values[u][j * NBR_LEN : (j + 1) * NBR_LEN]
            return carry

        lax.fori_loop(0, spans // group, some, 0)

        def fold(chip, carry):
            a, b = lax.div(chip, RING), lax.rem(chip, RING)
            for s in (0, 1):
                for core, keep in ((c, True), (1 - c, False)):
                    n = (2 * chip + core) * 2 + s
                    one, two = first[n], second[n]
                    for kv, part in ((0, ck), (1, cv)):
                        total = (part[one] + part[two]).astype(jnp.bfloat16)
                        lines = pl.ds(s * NBR_LEN, NBR_LEN)
                        if keep:
                            acc[t.h, a, b, kv, lines] = total
                        else:
                            give[t.parity][a, b, kv, lines] = total
            return carry

        lax.fori_loop(0, RING * RING, fold, 0)
        t.back_move(0).start()

    def sum_sibling(t):
        t.fetch().wait()

        def add(i, carry):
            a, b = lax.div(i, RING), lax.rem(i, RING)
            for kv in (0, 1):
                acc[t.h, a, b, kv] = acc[t.h, a, b, kv] + got[t.parity][a, b, kv]
            return carry

        lax.fori_loop(0, RING * RING, add, 0)

    def halves_out(t):
        t.back_move(1).start()
        t.back_move(2).start()

    def sum_band_half(t):
        for half, (kind, toward) in enumerate(((1, up(t.g)), (2, down(t.g)))):
            t.back_move(kind).wait_recv()

            def add(a, carry):
                at = t.spot(a, toward) + (half, t.lines)
                acc[at] = acc[at] + r1[t.h, half, a, t.lines]
                return carry

            lax.fori_loop(0, RING, add, 0)
            t.back_move(3 + half).start()

    def sum_band(t):
        t.back_move(3).wait_recv()
        t.back_move(4).wait_recv()

        def add(a, carry):
            for kv in (0, 1):
                at = t.spot(a, t.g) + (kv, t.lines)
                total = wide(acc[at]) + wide(r2[t.h, 0, a, kv, t.lines]) + wide(r2[t.h, 1, a, kv, t.lines])
                acc[at] = total.astype(jnp.bfloat16)
            return carry

        lax.fori_loop(0, RING, add, 0)
        t.back_move(5).start()
        t.back_move(6).start()

    def sum_block_half(t):
        for half, (kind, toward) in enumerate(((5, up(t.f)), (6, down(t.f)))):
            t.back_move(kind).wait_recv()
            at = t.spot(toward, t.g) + (half, t.lines)
            acc[at] = acc[at] + r3[t.h, half, t.lines]
            t.back_move(7 + half).start()

    def sum_block(t):
        t.back_move(7).wait_recv()
        t.back_move(8).wait_recv()
        for kv in (0, 1):
            for slot in t.slots:
                lines = pl.ds(slot * NBR_LEN, NBR_LEN)
                total = wide(acc[t.spot(t.f, t.g) + (kv, lines)])
                total = total + wide(r4[t.h, 0, kv, lines]) + wide(r4[t.h, 1, kv, lines])
                own[t.h, kv, slot] = total.astype(jnp.bfloat16)
        for kind in range(1, 9):
            t.back_move(kind).wait_send()

    pairs = heads // 2
    split = (pairs - 2, pairs - 1)
    sums = (ck, cv)

    def pair_copies(pair, action):
        for n in (0, 1):
            cols = pl.ds((2 * pair + n) * HD, HD)
            for core in (0, 1):
                for kv in (0, 1):
                    action(
                        pltpu.make_async_copy(
                            weights[kv].at[:, :, pl.ds(core * HD, HD), cols],
                            held[pair % 2].at[:, :, core, kv, n],
                            block_sem.at[pair, 4 * n + 2 * core + kv],
                        )
                    )

    def pair_start(*which):
        for pair in which:
            pair_copies(pair, lambda copy: copy.start())

    deep = [(kv, n) for kv in (0, 1) for n in (0, 1)]

    def rows_of(pair, slot):
        return jnp.concatenate([own[2 * pair + n, kv, slot] for kv, n in deep], axis=1)

    def weights_of(pair, t, a):
        table = held[pair % 2]
        return jnp.concatenate(
            [jnp.concatenate([table[t, a, core, kv, n] for kv, n in deep], axis=1) for core in (0, 1)],
            axis=0,
        )

    def gather_pair(pair):
        pair_copies(pair, lambda copy: copy.wait())
        lhs = jnp.concatenate([rows_of(pair, slot) for slot in (0, 1)], axis=0)

        def one(m, carry):
            t, a = lax.div(m, RING), lax.rem(m, RING)
            part = dot_t(lhs, weights_of(pair, t, a))
            for slot in (0, 1):
                for core in (0, 1):
                    at = 8 * t + 2 * a + core
                    piece = part[slot * NBR_LEN : (slot + 1) * NBR_LEN, core * HD : (core + 1) * HD]
                    sums[slot][at] = piece if pair == 0 else sums[slot][at] + piece
            return carry

        lax.fori_loop(0, RING * RING, one, 0)

    def product(slot, t, put):
        lhs = [rows_of(pair, slot) for pair in split]

        def one(a, carry):
            part = sum(dot_t(rows, weights_of(pair, t, a)) for rows, pair in zip(lhs, split))
            for core in (0, 1):
                at = 8 * t + 2 * a + core
                put(a, core, at, sums[slot][at] + part[:, core * HD : (core + 1) * HD])
            return carry

        lax.fori_loop(0, RING, one, 0)

    half = NBR_LEN // 2
    low, high = pl.ds(0, half), pl.ds(half, half)

    def enc_move(slot, kind):
        src, dst, to = (
            lambda: (give[slot].at[0, :, :, low], e1.at[slot, 0], right),
            lambda: (give[slot].at[1, :, :, low], e1.at[slot, 1], left),
            lambda: (give[slot].at[2, :, :, low], e2.at[slot, 0, :, :, low], right),
            lambda: (give[slot].at[3, :, :, high], e2.at[slot, 1, :, :, high], left),
            lambda: (give[slot].at[2, :, :, high], e2.at[slot, 0, :, :, high], right),
            lambda: (give[slot].at[3, :, :, low], e2.at[slot, 1, :, :, low], left),
        )[kind]()
        return pltpu.make_async_remote_copy(
            src_ref=src,
            dst_ref=dst,
            send_sem=enc_send.at[slot, kind],
            recv_sem=enc_recv.at[slot, kind],
            device_id={"enc": to},
            device_id_type=MESH,
        )

    def by_columns(action):
        def one(a, carry):
            for core in (0, 1):
                action(a, core)
            return carry

        lax.fori_loop(0, RING, one, 0)

    def enc_far(slot):
        send, sum_of = give[slot], sums[slot]

        def put_far(a, core, at, total):
            send[0, a, core, low] = total[:half].astype(jnp.bfloat16)
            send[1, a, core, low] = total[half:].astype(jnp.bfloat16)

        def put_right(a, core, at, total):
            sum_of[at] = total
            send[2, a, core, high] = total[half:].astype(jnp.bfloat16)

        def put_left(a, core, at, total):
            sum_of[at] = total
            send[3, a, core, low] = total[:half].astype(jnp.bfloat16)

        def put_mine(a, core, at, total):
            sum_of[at] = total

        if slot == 0:
            for pair in split:
                pair_copies(pair, lambda copy: copy.wait())
        product(slot, across(x), put_far)
        enc_move(slot, 0).start()
        enc_move(slot, 1).start()
        product(slot, right, put_right)
        enc_move(slot, 4).start()
        product(slot, left, put_left)
        enc_move(slot, 5).start()
        product(slot, x, put_mine)

    def enc_near(slot):
        send, sum_of = give[slot], sums[slot]

        def add_right(a, core):
            total = sum_of[8 * right + 2 * a + core, low] + wide(e1[slot, 0, a, core])
            send[2, a, core, low] = total.astype(jnp.bfloat16)

        def add_left(a, core):
            total = sum_of[8 * left + 2 * a + core, high] + wide(e1[slot, 1, a, core])
            send[3, a, core, high] = total.astype(jnp.bfloat16)

        enc_move(slot, 0).wait_recv()
        by_columns(add_right)
        enc_move(slot, 2).start()
        enc_move(slot, 1).wait_recv()
        by_columns(add_left)
        enc_move(slot, 3).start()

    def enc_done(slot):
        for kind in (4, 5, 2, 3):
            enc_move(slot, kind).wait_recv()

        for a in range(RING):
            for core in (0, 1):
                total = sums[slot][8 * x + 2 * a + core] + wide(e2[slot, 0, a, core]) + wide(e2[slot, 1, a, core])
                n = 2 * a + core
                enc_out[slot * NBR_LEN : (slot + 1) * NBR_LEN, n * HD : (n + 1) * HD] = total.astype(
                    jnp.bfloat16
                )
        for kind in range(6):
            enc_move(slot, kind).wait_send()

    there = (
        (0, own_out),
        (1, block_on),
        (2, band_out),
        (3, band_on),
        (4, band_last),
        (4, table_in),
    )
    back_small = ((9, sum_block), (8, sum_block_half))
    back_large = ((7, sum_band), (6, sum_band_half))
    turn = ((5, sibling_in), (4, attend), (5, sum_sibling))
    leave = ((5, halves_out),)
    between = {
        12: (lambda: enc_far(0),),
        13: (lambda: enc_near(0),),
        14: (lambda: enc_far(1),),
        15: (lambda: enc_near(1),),
    }
    after = {
        0: (rows_start,),
        2: (reads_in,),
        3: (rows_in,),
        7: (tail_out,),
        8: (rows_out, lambda: pair_start(0, 1)),
        9: (lambda: gather_pair(0), lambda: pair_start(2)),
        10: (lambda: gather_pair(1), lambda: pair_start(3)),
        15: (lambda: enc_done(0),),
        16: (lambda: enc_done(1),),
    }

    def at_times(i, table):
        for when, acts in table.items():

            @pl.when(i == when)
            def _(acts=acts):
                for act in acts:
                    act()

    def run(i, stages, parts):
        for lag, stage in stages:
            for start, stop, skip, slots in parts:

                @pl.when((i >= start + lag) & (i < stop + lag))
                def _(lag=lag, stage=stage, skip=skip, slots=slots):
                    for parity in (0, 1):
                        stage(Head(2 * (i - lag - skip) + parity, parity, slots))

    both = ((0, pairs, 0, (0, 1)),)
    apart = (
        (0, pairs - 2, 0, (0, 1)),
        (pairs - 2, pairs, 0, (0,)),
        (pairs, pairs + 2, 2, (1,)),
    )

    def step(i, carry):
        run(i, there, both)
        run(i, back_small, apart)
        at_times(i, between)
        run(i, back_large, apart)
        run(i, turn, both)
        run(i, leave, apart)
        at_times(i, after)
        return carry

    lax.fori_loop(0, max(after) + 1, step, 0)
    for copy in result_copies():
        copy.wait()


def core(owner, slot_of, enc, w_key, w_value, queries, cotangents):
    rows, width = queries.shape
    depth = enc.shape[1]
    heads, reads = width // HD, 2 * owner.shape[1]
    rest = (2, 2, NBR_LEN, HD)
    tail = (2, 2 * NBR_LEN, HD)
    bf16, f32 = jnp.bfloat16, jnp.float32
    in_vmem = pl.BlockSpec(memory_space=pltpu.VMEM)
    in_smem = pl.BlockSpec(memory_space=pltpu.SMEM)
    anywhere = pl.BlockSpec(memory_space=pl.ANY)
    band = (RING, RING) + tail
    dma = pltpu.SemaphoreType.DMA
    folded = (RING, RING, depth // (RING * RING), width)
    return pl.pallas_call(
        core_kernel,
        in_specs=[in_smem] * 2 + [anywhere] * 5,
        out_specs=[anywhere, anywhere, in_vmem, anywhere, anywhere],
        out_shape=[
            jax.ShapeDtypeStruct((rows, width), bf16),
            jax.ShapeDtypeStruct((rows, width), bf16),
            jax.ShapeDtypeStruct((tail[1], depth // RING), bf16),
            jax.ShapeDtypeStruct((heads, RING, RING, 2) + rest, bf16),
            jax.ShapeDtypeStruct((heads,) + band, bf16),
        ],
        scratch_shapes=[
            pltpu.VMEM((RING, RING, 2) + rest, bf16),
            pltpu.VMEM((RING, RING, 2) + rest, bf16),
            pltpu.VMEM((max(reads + 1, depth // HD), NBR_LEN, HD), f32),
            pltpu.VMEM((max(reads + 1, depth // HD), NBR_LEN, HD), f32),
            pltpu.VMEM((heads,) + band, bf16),
            pltpu.VMEM(band, bf16),
            pltpu.VMEM(band, bf16),
            pltpu.VMEM(band, bf16),
            pltpu.VMEM(band, bf16),
            pltpu.VMEM((heads,) + rest, bf16),
            pltpu.VMEM((rows + SPAN, width), bf16),
            pltpu.VMEM((rows + SPAN, width), bf16),
            pltpu.VMEM((rows + SPAN, width), bf16),
            pltpu.VMEM((rows + SPAN, width), bf16),
            pltpu.VMEM((heads, 2, RING) + tail[1:], bf16),
            pltpu.VMEM((heads, 2, RING) + tail, bf16),
            pltpu.VMEM((heads, 2) + tail[1:], bf16),
            pltpu.VMEM((heads, 2) + tail, bf16),
            pltpu.VMEM((2, 2, RING, 2, NBR_LEN // 2, HD), bf16),
            pltpu.VMEM((2, 2, RING, 2, NBR_LEN, HD), bf16),
            dma((heads, 12)),
            dma((heads, 12)),
            dma((heads, 17)),
            dma((heads, 17)),
            dma((heads,)),
            dma((heads, 2)),
            dma((depth // HD,)),
            dma((heads, 2)),
            dma((4,)),
            dma((4,)),
            dma((4,)),
            dma((heads // 2, 8)),
            dma((2, 6)),
            dma((2, 6)),
            pltpu.SMEM((reads,), jnp.int32),
            pltpu.SMEM((4 * RING * RING,), jnp.int32),
            pltpu.SMEM((4 * RING * RING,), jnp.int32),
        ],
        compiler_params=pltpu.CompilerParams(
            collective_id=0, has_side_effects=True, vmem_limit_bytes=64 * MIB
        ),
        name="core",
    )(owner, slot_of, enc, w_key.reshape(folded), w_value.reshape(folded), queries, cotangents)


def hand_out_kernel(*refs):
    count = len(refs) // 2
    for source, target in zip(refs[:count], refs[count:]):
        target[...] = source[...]


def hand_out(*values):
    parts = 4
    specs = [pl.BlockSpec((v.shape[0] // parts, v.shape[1]), lambda i: (i, 0)) for v in values]
    return pl.pallas_call(
        hand_out_kernel,
        grid=(parts,),
        in_specs=specs,
        out_specs=specs,
        out_shape=[jax.ShapeDtypeStruct(v.shape, v.dtype) for v in values],
        compiler_params=pltpu.CompilerParams(vmem_limit_bytes=62 * MIB),
        name="hand_out",
    )(*values)


def per_device(queries, d_attended, encodings, w_key, w_value, neighbour_owner, neighbour_slot):
    feat_width = queries.shape[1]
    owned = encodings.shape[0]
    enc_flat = encodings.reshape(owned * NBR_LEN, encodings.shape[2])
    attended, d_queries, d_encodings, _, _ = core(
        neighbour_owner.T, neighbour_slot.T, enc_flat, w_key, w_value, queries, d_attended
    )
    attended, d_queries, d_encodings = hand_out(attended, d_queries, d_encodings)
    return (attended, d_queries, d_encodings.reshape(owned, NBR_LEN, feat_width))


def solution(mesh):
    return jax.shard_map(
        per_device,
        mesh=mesh,
        in_specs=(
            P("seq", "enc"),
            P("seq", "enc"),
            P("seq", None, None),
            P(None, "enc"),
            P(None, "enc"),
            P("seq", None),
            P("seq", None),
        ),
        out_specs=(P("seq", "enc"), P("seq", "enc"), P("seq", None, "enc")),
        check_vma=False,
    )
```
